256 devices in a mesh: tilt: 64 (over x, z, core), slab: 4 (over y).
Axes of the slice: x: 4, y: 4, z: 8, core: 2. Of those that a mesh axis runs over, the one named last changes fastest.
Arguments:
- tilt_images: bfloat16 [64, 256, 256], P('tilt'), may hold values from -68 to 68
- corners: int32 [2, 64, 128], P(None, 'tilt'), may hold values from 0 to 128
- visible: int32 [64, 128], P('tilt'), may hold values 0 or 1
- defocus: float32 [128, 64], P('tilt'), may hold values from 5 to 40
- labels: int32 [128], P('tilt'), may hold values from 0 to 3
- row_owner: int32 [128, 64, 128, 1], P('tilt'), may hold values from 0 to 255; in each aligned block of 16384 rows (0 to 16383, 16384 to 32767, ..., all dimensions but the last counted through in order) at most 128 rows name the same one
- row_offset: int32 [128, 64, 128], P('tilt'), may hold values from 0 to 63
Outputs:
- class_maps: float32 [2, 4, 16384, 128], P(None, None, ('tilt', 'slab'))
The draws below stay inside these ranges and needn't reach their ends.
Inputs may be any that keep to these rules, and one draw needn't show every extreme that they name: `row_owner`: among the slice rows of the particles of one index of tilt, at most 128 fall in one block, and some block receives exactly 128.
All inputs are finite; a program needn't handle non-finite values. No bound on the sum of `visible` on one device may be relied on, other than what follows from the above.
Results may differ from the reference program's by a relative error of at most 0.007.
Values may be sent and summed in bfloat16 or wider, within the bound.
A program may use at most 128 MiB of HBM per device.

```python
import math
import jax
import jax.numpy as jnp
import numpy as np
from jax import lax

BOX = 128
HALFMAPS = 4
IMG = 256
PART_DEV = 2
TILTS = 64
PARTICLES = 128
OWNERS = 256
ROWS_OWN = 64
CAP = 128


def draw_tilt_images(key, part):
    first_key, second_key, third_key = jax.random.split(key, 3)
    tile_count = IMG // 32
    scales = jnp.exp(jax.random.uniform(first_key, (TILTS, tile_count, tile_count), jnp.float32, 0.0, math.log(10.0)))
    offsets = jnp.clip(3.0 * jax.random.normal(second_key, (TILTS, tile_count, tile_count), jnp.float32), -8.0, 8.0)
    noise = jnp.clip(jax.random.normal(third_key, (TILTS, IMG, IMG), jnp.float32), -6.0, 6.0)
    scales_full = jnp.repeat(jnp.repeat(scales, 32, axis=1), 32, axis=2)
    offsets_full = jnp.repeat(jnp.repeat(offsets, 32, axis=1), 32, axis=2)
    return (offsets_full + scales_full * noise).astype(jnp.bfloat16)


def set_ends(drawn, own_key, low, top_value):
    longest = drawn.shape.index(max(drawn.shape))
    spots = []
    for shift in (0, 1):
        where = [jax.random.randint(jax.random.fold_in(own_key, axis), (), 0, length) for axis, length in enumerate(drawn.shape)]
        where[longest] = (where[longest] + shift) % drawn.shape[longest]
        spots.append(tuple(where))
    return drawn.at[spots[0]].set(low).at[spots[1]].set(top_value)


def steps_of(own_key, extent, cuts, smallest, high):
    level, own = 1.0, jax.random.fold_in(own_key, 6)
    for axis_at, blocks in cuts:
        steps = jnp.exp(jax.random.uniform(jax.random.fold_in(own, axis_at), (blocks,), jnp.float32, smallest / len(cuts), high / len(cuts)))
        level = level * jnp.repeat(steps, extent[axis_at] // blocks).reshape([-1 if axis == axis_at else 1 for axis in range(len(extent))])
    return level


def deal_out(own_key, own, number, rows, count, top, limit, slope):
    order = jax.random.permutation(own_key, count)
    crowded, common = portions_of(count, rows * top, limit, slope, True), portions_of(count, rows * top, limit, slope, False)
    places = jnp.arange(count)

    def named(lengths, turn):
        used = int((lengths > 0).sum())
        fixed = max(1, used // 4)
        passed = fixed + (places - fixed + turn * (used - fixed)) % max(1, count - fixed)
        return jnp.zeros((count,), jnp.int32).at[order[jnp.where(places < fixed, places, passed)]].set(jnp.asarray(lengths, jnp.int32))

    lengths = jnp.where(number % 4 == 0, named(crowded, number // 4), named(common, number - number // 4 - 1))
    mixed = jax.random.permutation(jax.random.fold_in(own, 3), count)
    source_of, receiver = mixed[0:count // 2 * 2:2], mixed[1:count // 2 * 2:2]
    margin = jnp.minimum(lengths[source_of] - 1, limit - lengths[receiver]) // 2
    margin = jnp.where((source_of == order[0]) | (receiver == order[0]) | (lengths[receiver] == 0), 0, jnp.maximum(margin, 0))
    passed = jax.random.randint(jax.random.fold_in(own, 4), (count // 2,), 0, 1 << 20) % (margin + 1)
    lengths = lengths.at[source_of].add(-passed).at[receiver].add(passed)
    items = jnp.searchsorted(jnp.cumsum(lengths), jnp.arange(rows * top), side="right").astype(jnp.int32)
    listing = items.reshape(top, rows).T
    listing = listing[jax.random.permutation(jax.random.fold_in(own, 1), rows)]
    turn = jax.random.randint(jax.random.fold_in(own, 2), (rows, 1), 0, top)
    return jnp.take_along_axis(listing, (jnp.arange(top)[None, :] + turn) % top, axis=1)


def portions_of(amount, total, limit, skew, full):
    loads = [(1 << 20) // math.isqrt(grade ** skew) + 1 for grade in range(1, amount + 1)]
    largest = limit if full else min(limit, max(-(-total // amount), total * loads[0] // sum(loads)))
    least = 1 if total - largest >= amount - 1 else 0
    holding, spare = [largest] + [least] * (amount - 1), total - largest - least * (amount - 1)
    while spare > 0:
        candidates = [i for i in range(1, amount) if holding[i] < largest] or [i for i in range(1, amount) if holding[i] < limit]
        pool, remaining = sum([loads[i] for i in candidates]), spare
        for i in candidates:
            more = min(limit - holding[i], max(1, remaining * loads[i] // pool), spare)
            holding[i] = holding[i] + more
            spare = spare - more
    return np.array(holding)


def setup_inputs(seed: int = 0) -> dict:
    streams_of = jax.random.split(jax.random.key(seed), 8)
    tilt_images = draw_tilt_images(jax.random.fold_in(streams_of[7], 71), 0)
    corners = set_ends(jax.random.randint(streams_of[1], (2, TILTS, PARTICLES), 0, IMG - BOX + 1), jax.random.fold_in(streams_of[1], 1), 0, IMG - BOX).astype(jnp.int32)
    visible = set_ends((jax.random.randint(streams_of[2], (TILTS, PARTICLES), 0, 4) < 3).astype(jnp.int32), jax.random.fold_in(streams_of[2], 1), 0, 1)
    defocus = jnp.clip(jnp.exp(math.log(40.0) - 2.0794415 * jax.random.uniform(streams_of[3], (PARTICLES, TILTS), jnp.float32) ** steps_of(streams_of[3], (PARTICLES, TILTS), ((0, 64),), -0.2, 0.2)), 5.0, 40.0)
    labels = set_ends(jax.random.randint(streams_of[4], (PARTICLES,), 0, HALFMAPS), jax.random.fold_in(streams_of[4], 1), 0, HALFMAPS - 1).astype(jnp.int32)
    row_owner_keys = jax.random.split(jax.random.fold_in(streams_of[5], 1), PARTICLES * TILTS * BOX // (PART_DEV * TILTS * BOX))
    row_owner_turns = jax.random.permutation(jax.random.fold_in(streams_of[5], 3), PARTICLES * TILTS * BOX // (PART_DEV * TILTS * BOX))
    row_owner = jax.vmap(lambda own, number: deal_out(jax.random.fold_in(streams_of[5], 2), own, number, PART_DEV * TILTS * BOX, OWNERS, 1, CAP, 2))(row_owner_keys, row_owner_turns).reshape((PARTICLES, TILTS, BOX, 1))
    row_offset = set_ends(jax.random.randint(streams_of[6], (PARTICLES, TILTS, BOX), 0, ROWS_OWN), jax.random.fold_in(streams_of[6], 1), 0, ROWS_OWN - 1).astype(jnp.int32)
    return {"tilt_images": tilt_images, "corners": corners, "visible": visible, "defocus": defocus, "labels": labels, "row_owner": row_owner, "row_offset": row_offset}


AMPLITUDE = 0.1

def fourier_tables(width):
    positions = jnp.arange(width, dtype=jnp.int32)
    frequency = positions - width // 2
    phase_index = frequency[:, None] * positions[None, :] % width
    angles = phase_index.astype(jnp.float32) * (2.0 * jnp.pi / width)
    return (jnp.cos(angles).astype(jnp.bfloat16), (-jnp.sin(angles)).astype(jnp.bfloat16))

def contrast_transfer(defocus_values, width):
    frequency = (jnp.arange(width, dtype=jnp.int32) - width // 2).astype(jnp.float32) / width
    radius_sq = frequency[:, None] ** 2 + frequency[None, :] ** 2
    aberration = jnp.pi * defocus_values[..., None, None] * radius_sq
    return -(jnp.sqrt(1.0 - AMPLITUDE * AMPLITUDE) * jnp.sin(aberration) + AMPLITUDE * jnp.cos(aberration))

def normalize(patches, seen_mask):
    values = patches.astype(jnp.float32)
    average = lax.optimization_barrier(jnp.mean(values, axis=(-2, -1), keepdims=True))
    centered = values - average
    variance = lax.optimization_barrier(jnp.mean(centered * centered, axis=(-2, -1), keepdims=True))
    scaled = centered * lax.rsqrt(variance + 1e-05) * seen_mask.astype(jnp.float32)[..., None, None]
    return scaled.astype(jnp.bfloat16)

def cut_window(micrograph, corner_y, corner_x):
    return lax.dynamic_slice(micrograph, (corner_y, corner_x), (BOX, BOX))

def reference(tilt_images, corners, visible, defocus, labels, row_owner, row_offset):
    cos_table, sin_table = fourier_tables(BOX)
    stacked = jnp.concatenate([cos_table, sin_table], 0).astype(jnp.float32)
    map_rows_total = BOX * BOX

    def step(running, particle):
        patches = jax.vmap(cut_window)(tilt_images, corners[0, :, particle], corners[1, :, particle])
        patches = normalize(patches, visible[:, particle])
        first_section = jnp.einsum('kn,tnm->tkm', stacked, patches.astype(jnp.float32)).astype(jnp.bfloat16)
        second = jnp.einsum('tkm,lm->tkl', first_section.astype(jnp.float32), stacked)
        real_part = second[:, :BOX, :BOX] - second[:, BOX:, BOX:]
        imag_part = second[:, :BOX, BOX:] + second[:, BOX:, :BOX]
        transfer = contrast_transfer(defocus[particle], BOX)
        slice_real = (transfer * real_part / BOX).astype(jnp.bfloat16)
        slice_imag = (transfer * imag_part / BOX).astype(jnp.bfloat16)
        slices = jnp.stack([slice_real, slice_imag]).astype(jnp.float32).reshape(2, TILTS * BOX, BOX)
        target = (row_owner[particle, :, :, 0] * ROWS_OWN + row_offset[particle]).reshape(-1)
        segment_ids = labels[particle] * map_rows_total + target
        running = running.at[:, segment_ids].add(slices)
        return (running, None)
    initial = jnp.zeros((2, HALFMAPS * map_rows_total, BOX), jnp.float32)
    total, _ = lax.scan(step, initial, jnp.arange(PARTICLES, dtype=jnp.int32))
    return total.reshape(2, HALFMAPS, BOX * BOX, BOX)
```

```python
import jax
import jax.numpy as jnp
import numpy as np
from jax import lax
from jax.experimental import pallas as pl
from jax.experimental.pallas import tpu as pltpu
from jax.sharding import PartitionSpec as P

BOX = 128
HALFMAPS = 4
AMPLITUDE = 0.1
TILTS = 64
PARTICLES = 128
CELLS = TILTS * HALFMAPS * 64
GROUP = 16
WINDOW = 2 * GROUP


def fourier_tables(width):
    positions = jnp.arange(width, dtype=jnp.int32)
    frequency = positions - width // 2
    phase_index = frequency[:, None] * positions[None, :] % width
    angles = phase_index.astype(jnp.float32) * (2.0 * jnp.pi / width)
    return (jnp.cos(angles).astype(jnp.bfloat16), (-jnp.sin(angles)).astype(jnp.bfloat16))


def transfer_factors(defocus_values):
    frequency = (jnp.arange(BOX, dtype=jnp.int32) - BOX // 2).astype(jnp.float32) / BOX
    angle = jnp.pi * defocus_values[:, None] * (frequency * frequency)[None, :]
    cos_part, sin_part = jnp.cos(angle), jnp.sin(angle)
    main = jnp.sqrt(1.0 - AMPLITUDE * AMPLITUDE)
    first = -(main * sin_part + AMPLITUDE * cos_part) / BOX
    second = -(main * cos_part - AMPLITUDE * sin_part) / BOX
    return first.T, second.T, cos_part, sin_part


def insert_kernel(corner_ref, seen_ref, image_ref, places_ref, stacked_ref, mixed_ref, first_ref, second_ref,
                  cos_ref, sin_ref, out_ref, left, right, main_list, late_list, late_any, main_s, late_s, any_s,
                  slices_a, slices_b, table, sems):
    lane = lax.broadcasted_iota(jnp.int32, (BOX, BOX), 1)
    dump = 2 * CELLS + 2 * (lane % GROUP)
    places = places_ref[...]
    kept = places >= 0
    later = jnp.zeros((BOX, BOX), jnp.bool_)
    for d in range(1, WINDOW):
        other = pltpu.roll(places, BOX - d, axis=1)
        later = later | ((other == places) & (lane < BOX - d))
    late = later & kept
    main_list[...] = jnp.where(kept & ~late, places, dump)
    late_list[...] = jnp.where(late, places, dump)
    late_any[...] = jnp.broadcast_to(
        jnp.max(jnp.where(late, 1, 0), axis=1, keepdims=True), (BOX, BOX))
    copies = [
        pltpu.make_async_copy(main_list, main_s, sems.at[0]),
        pltpu.make_async_copy(late_list, late_s, sems.at[1]),
        pltpu.make_async_copy(late_any, any_s, sems.at[2]),
    ]
    for copy in copies:
        copy.start()
    left[...] = image_ref[:, :BOX].astype(jnp.float32)
    right[...] = image_ref[:, BOX:].astype(jnp.float32)

    def clear(i, carry):
        table[pl.ds(pl.multiple_of(i * 512, 512), 512), :] = jnp.zeros((512, BOX), jnp.float32)
        return carry

    lax.fori_loop(0, 2 * CELLS // 512, clear, 0)
    for copy in copies:
        copy.wait()

    def window(p):
        row, col = corner_ref[0, p], corner_ref[1, p]
        a = left[pl.ds(row, BOX), :]
        b = right[pl.ds(row, BOX), :]
        cut = pltpu.roll(jnp.where(lane >= col, a, b), (BOX - col) % BOX, axis=1)
        average = jnp.sum(jnp.sum(cut, axis=0, keepdims=True), axis=1, keepdims=True) * (1.0 / (BOX * BOX))
        centered = cut - average
        variance = jnp.sum(
            jnp.sum(centered * centered, axis=0, keepdims=True), axis=1, keepdims=True) * (1.0 / (BOX * BOX))
        scale = lax.rsqrt(variance + 1e-05) * seen_ref[0, p].astype(jnp.float32)
        return (centered * scale).astype(jnp.bfloat16)

    def slices_of(pair):
        p = 2 * pair
        patches = jnp.concatenate([window(p), window(p + 1)], axis=1)
        section = jnp.dot(stacked_ref[...], patches, preferred_element_type=jnp.float32).astype(jnp.bfloat16)
        for j, target in ((0, slices_a), (1, slices_b)):
            side = jnp.concatenate(
                [section[:BOX, j * BOX:(j + 1) * BOX], section[BOX:, j * BOX:(j + 1) * BOX]], axis=1)
            spectrum = jnp.dot(side, mixed_ref[...], preferred_element_type=jnp.float32)
            pick = jnp.full((BOX, BOX), p + j, jnp.int32)
            first = jnp.take_along_axis(first_ref[...], pick, axis=1)
            second = jnp.take_along_axis(second_ref[...], pick, axis=1)
            transfer = first * cos_ref[pl.ds(p + j, 1), :] + second * sin_ref[pl.ds(p + j, 1), :]
            target[pl.ds(0, BOX, stride=2), :] = transfer * spectrum[:, :BOX]
            target[pl.ds(1, BOX, stride=2), :] = transfer * spectrum[:, BOX:]

    def insert(p, source):
        waiting = None
        for g in range(BOX // GROUP + 1):
            if g < BOX // GROUP:
                spots = [main_s[p, g * GROUP + i] for i in range(GROUP)]
                sums = [table[pl.ds(spots[i], 2), :] + source[pl.ds(2 * (g * GROUP + i), 2), :]
                        for i in range(GROUP)]
            if waiting is not None:
                for spot, total in zip(*waiting):
                    table[pl.ds(spot, 2), :] = total
            waiting = (spots, sums)

        @pl.when(any_s[p, 0] > 0)
        def _():
            def one(i, carry):
                spot = late_s[p, i]
                table[pl.ds(spot, 2), :] += source[pl.ds(2 * i, 2), :]
                return carry

            lax.fori_loop(0, BOX, one, 0)

    def step(pair, carry):
        slices_of(pair)
        insert(2 * pair, slices_a)
        insert(2 * pair + 1, slices_b)
        return carry

    lax.fori_loop(0, PARTICLES // 2, step, 0)

    def finish(i, carry):
        rows = pl.ds(pl.multiple_of(i * 512, 512), 512)
        out_ref[rows, :] = table[rows, :].astype(jnp.bfloat16)
        return carry

    lax.fori_loop(0, 2 * CELLS // 512, finish, 0)


def insert(corners, seen, image, places, stacked, mixed, factors):
    whole = pl.BlockSpec(memory_space=pltpu.VMEM)
    scalars = pl.BlockSpec(memory_space=pltpu.SMEM)
    return pl.pallas_call(
        insert_kernel,
        out_shape=jax.ShapeDtypeStruct((2 * CELLS, BOX), jnp.bfloat16),
        in_specs=[scalars, scalars] + [whole] * 8,
        out_specs=whole,
        scratch_shapes=[
            pltpu.VMEM((256, BOX), jnp.float32),
            pltpu.VMEM((256, BOX), jnp.float32),
            pltpu.VMEM((BOX, BOX), jnp.int32),
            pltpu.VMEM((BOX, BOX), jnp.int32),
            pltpu.VMEM((BOX, BOX), jnp.int32),
            pltpu.SMEM((BOX, BOX), jnp.int32),
            pltpu.SMEM((BOX, BOX), jnp.int32),
            pltpu.SMEM((BOX, BOX), jnp.int32),
            pltpu.VMEM((2 * BOX, BOX), jnp.float32),
            pltpu.VMEM((2 * BOX, BOX), jnp.float32),
            pltpu.VMEM((2 * CELLS + 2 * GROUP, BOX), jnp.float32),
            pltpu.SemaphoreType.DMA((3,)),
        ],
        compiler_params=pltpu.CompilerParams(vmem_limit_bytes=48 * 2**20),
        name="insert_slices",
    )(corners, seen, image, places, stacked, mixed, *factors)


def tables():
    cos_table, sin_table = fourier_tables(BOX)
    stacked = jnp.concatenate([cos_table, sin_table], 0)
    mixed = jnp.concatenate([
        jnp.concatenate([cos_table.T, sin_table.T], 1),
        jnp.concatenate([-sin_table.T, cos_table.T], 1)], 0)
    return stacked, mixed


def places_of(rows, labels, slab_index, slab_count):
    owner, offset = rows // 64, rows % 64
    owner_tilt = owner // slab_count
    block = (owner_tilt % 2) * (TILTS // 2) + owner_tilt // 2
    place = 2 * ((block * HALFMAPS + labels[:, None]) * 64 + offset)
    return jnp.where(owner % slab_count == slab_index, place, -1 - lax.broadcasted_iota(jnp.int32, rows.shape, 1))


def body(tilt_images, corners, visible, defocus, labels, row_owner, row_offset):
    slab_count = lax.axis_size("slab")
    slab_index = lax.axis_index("slab")
    rows = (row_owner[..., 0] * 64 + row_offset).astype(jnp.float32)
    packed = jnp.concatenate([
        rows.transpose(1, 0, 2),
        jnp.pad(jnp.stack([defocus.T, jnp.broadcast_to(labels.astype(jnp.float32), (TILTS, 2))], 1),
                ((0, 0), (0, 0), (0, BOX - 2)))], 1)
    packed = lax.all_to_all(packed, "tilt", split_axis=0, concat_axis=0, tiled=True)
    rows = packed[:, :2].reshape(PARTICLES, BOX).astype(jnp.int32)
    defocus_all = packed[:, 2, :2].reshape(PARTICLES)
    labels_all = packed[:, 3, :2].reshape(PARTICLES).astype(jnp.int32)
    places = places_of(rows, labels_all, slab_index, slab_count)
    stacked, mixed = tables()
    table = insert(corners[:, 0], visible, tilt_images[0], places, stacked, mixed, transfer_factors(defocus_all))
    table = table.reshape(2, 4, 8, HALFMAPS, 64, 2, BOX).transpose(1, 2, 0, 3, 4, 5, 6).reshape(TILTS, -1, BOX)
    own = lax.psum_scatter(table, "tilt", scatter_dimension=0, tiled=True)
    own = own.reshape(HALFMAPS, 64, 2, BOX)
    return own.transpose(2, 0, 1, 3).astype(jnp.float32)


def solution(mesh):
    return jax.shard_map(
        body,
        mesh=mesh,
        in_specs=(
            P("tilt", None, None),
            P(None, "tilt", None),
            P("tilt", None),
            P("tilt", None),
            P("tilt"),
            P("tilt", None, None, None),
            P("tilt", None, None),
        ),
        out_specs=P(None, None, ("tilt", "slab"), None),
        check_vma=False,
    )
```

```python
import jax
import jax.numpy as jnp
import numpy as np
from jax import lax
from jax.experimental import pallas as pl
from jax.experimental.pallas import tpu as pltpu
from jax.sharding import PartitionSpec as P

BOX = 128
HALFMAPS = 4
AMPLITUDE = 0.1
TILTS = 64
PARTICLES = 128
CELLS = TILTS * HALFMAPS * 64
GROUP = 16
WINDOW = 2 * GROUP


def fourier_tables(width):
    positions = jnp.arange(width, dtype=jnp.int32)
    frequency = positions - width // 2
    phase_index = frequency[:, None] * positions[None, :] % width
    angles = phase_index.astype(jnp.float32) * (2.0 * jnp.pi / width)
    return (jnp.cos(angles).astype(jnp.bfloat16), (-jnp.sin(angles)).astype(jnp.bfloat16))


def transfer_factors(defocus_values):
    frequency = (jnp.arange(BOX, dtype=jnp.int32) - BOX // 2).astype(jnp.float32) / BOX
    angle = jnp.pi * defocus_values[:, None] * (frequency * frequency)[None, :]
    cos_part, sin_part = jnp.cos(angle), jnp.sin(angle)
    main = jnp.sqrt(1.0 - AMPLITUDE * AMPLITUDE)
    first = -(main * sin_part + AMPLITUDE * cos_part) / BOX
    second = -(main * cos_part - AMPLITUDE * sin_part) / BOX
    return first.T, second.T, cos_part, sin_part


def insert_kernel(corner_ref, seen_ref, image_ref, places_ref, stacked_ref, mixed_ref, first_ref, second_ref,
                  cos_ref, sin_ref, out_ref, left, right, main_list, late_list, late_any, main_s, late_s, any_s,
                  slices_a, slices_b, table, sems):
    lane = lax.broadcasted_iota(jnp.int32, (BOX, BOX), 1)
    dump = 2 * CELLS + 2 * (lane % GROUP)
    places = places_ref[...]
    kept = places >= 0
    later = jnp.zeros((BOX, BOX), jnp.bool_)
    for d in range(1, WINDOW):
        other = pltpu.roll(places, BOX - d, axis=1)
        later = later | ((other == places) & (lane < BOX - d))
    late = later & kept
    main_list[...] = jnp.where(kept & ~late, places, dump)
    late_list[...] = jnp.where(late, places, dump)
    late_any[...] = jnp.broadcast_to(
        jnp.max(jnp.where(late, 1, 0), axis=1, keepdims=True), (BOX, BOX))
    copies = [
        pltpu.make_async_copy(main_list, main_s, sems.at[0]),
        pltpu.make_async_copy(late_list, late_s, sems.at[1]),
        pltpu.make_async_copy(late_any, any_s, sems.at[2]),
    ]
    for copy in copies:
        copy.start()
    left[...] = image_ref[:, :BOX].astype(jnp.float32)
    right[...] = image_ref[:, BOX:].astype(jnp.float32)

    def clear(i, carry):
        table[pl.ds(pl.multiple_of(i * 512, 512), 512), :] = jnp.zeros((512, BOX), jnp.float32)
        return carry

    lax.fori_loop(0, 2 * CELLS // 512, clear, 0)
    for copy in copies:
        copy.wait()

    def window(p):
        row, col = corner_ref[0, p], corner_ref[1, p]
        a = left[pl.ds(row, BOX), :]
        b = right[pl.ds(row, BOX), :]
        cut = pltpu.roll(jnp.where(lane >= col, a, b), (BOX - col) % BOX, axis=1)
        average = jnp.sum(jnp.sum(cut, axis=0, keepdims=True), axis=1, keepdims=True) * (1.0 / (BOX * BOX))
        centered = cut - average
        variance = jnp.sum(
            jnp.sum(centered * centered, axis=0, keepdims=True), axis=1, keepdims=True) * (1.0 / (BOX * BOX))
        scale = lax.rsqrt(variance + 1e-05) * seen_ref[0, p].astype(jnp.float32)
        return (centered * scale).astype(jnp.bfloat16)

    def slices_of(pair):
        p = 2 * pair
        patches = jnp.concatenate([window(p), window(p + 1)], axis=1)
        section = jnp.dot(stacked_ref[...], patches, preferred_element_type=jnp.float32).astype(jnp.bfloat16)
        for j, target in ((0, slices_a), (1, slices_b)):
            side = jnp.concatenate(
                [section[:BOX, j * BOX:(j + 1) * BOX], section[BOX:, j * BOX:(j + 1) * BOX]], axis=1)
            spectrum = jnp.dot(side, mixed_ref[...], preferred_element_type=jnp.float32)
            pick = jnp.full((BOX, BOX), p + j, jnp.int32)
            first = jnp.take_along_axis(first_ref[...], pick, axis=1)
            second = jnp.take_along_axis(second_ref[...], pick, axis=1)
            transfer = first * cos_ref[pl.ds(p + j, 1), :] + second * sin_ref[pl.ds(p + j, 1), :]
            target[pl.ds(0, BOX, stride=2), :] = transfer * spectrum[:, :BOX]
            target[pl.ds(1, BOX, stride=2), :] = transfer * spectrum[:, BOX:]

    def insert(p, source):
        waiting = None
        for g in range(BOX // GROUP + 1):
            if g < BOX // GROUP:
                spots = [main_s[p, g * GROUP + i] for i in range(GROUP)]
                sums = [table[pl.ds(spots[i], 2), :] + source[pl.ds(2 * (g * GROUP + i), 2), :]
                        for i in range(GROUP)]
            if waiting is not None:
                for spot, total in zip(*waiting):
                    table[pl.ds(spot, 2), :] = total
            waiting = (spots, sums)

        @pl.when(any_s[p, 0] > 0)
        def _():
            def one(i, carry):
                spot = late_s[p, i]
                table[pl.ds(spot, 2), :] += source[pl.ds(2 * i, 2), :]
                return carry

            lax.fori_loop(0, BOX, one, 0)

    def step(pair, carry):
        slices_of(pair)
        insert(2 * pair, slices_a)
        insert(2 * pair + 1, slices_b)
        return carry

    lax.fori_loop(0, PARTICLES // 2, step, 0)

    def finish(i, carry):
        rows = pl.ds(pl.multiple_of(i * 512, 512), 512)
        out_ref[rows, :] = table[rows, :].astype(jnp.bfloat16)
        return carry

    lax.fori_loop(0, 2 * CELLS // 512, finish, 0)


def insert(corners, seen, image, places, stacked, mixed, factors):
    whole = pl.BlockSpec(memory_space=pltpu.VMEM)
    scalars = pl.BlockSpec(memory_space=pltpu.SMEM)
    return pl.pallas_call(
        insert_kernel,
        out_shape=jax.ShapeDtypeStruct((2 * CELLS, BOX), jnp.bfloat16),
        in_specs=[scalars, scalars] + [whole] * 8,
        out_specs=whole,
        scratch_shapes=[
            pltpu.VMEM((256, BOX), jnp.float32),
            pltpu.VMEM((256, BOX), jnp.float32),
            pltpu.VMEM((BOX, BOX), jnp.int32),
            pltpu.VMEM((BOX, BOX), jnp.int32),
            pltpu.VMEM((BOX, BOX), jnp.int32),
            pltpu.SMEM((BOX, BOX), jnp.int32),
            pltpu.SMEM((BOX, BOX), jnp.int32),
            pltpu.SMEM((BOX, BOX), jnp.int32),
            pltpu.VMEM((2 * BOX, BOX), jnp.float32),
            pltpu.VMEM((2 * BOX, BOX), jnp.float32),
            pltpu.VMEM((2 * CELLS + 2 * GROUP, BOX), jnp.float32),
            pltpu.SemaphoreType.DMA((3,)),
        ],
        compiler_params=pltpu.CompilerParams(vmem_limit_bytes=48 * 2**20),
        name="insert_slices",
    )(corners, seen, image, places, stacked, mixed, *factors)


ZS, XS = 8, 4
PART_ROWS = TILTS // 2 * BOX
SPOTS = 2 * CELLS


def reduce_kernel(table_ref, out_ref, own, sib, send_a, recv_a, send_b, recv_b, mid_a, mid_b, send_c, recv_c, send_d,
                  recv_d, last, own_sem, sib_send, sib_recv, a_send, a_recv, b_send, b_recv, c_send, c_recv, d_send,
                  d_recv):
    tilt, slab = lax.axis_index("tilt"), lax.axis_index("slab")
    core, z, x = tilt % 2, tilt // 2 % ZS, tilt // (2 * ZS)

    def at_z(step):
        return (x * (2 * ZS) + (z + step + ZS) % ZS * 2 + core, slab)

    def at_x(step):
        return ((x + step + XS) % XS * (2 * ZS) + z * 2 + core, slab)

    twin = (tilt + 1 - 2 * core, slab)
    barrier = pltpu.get_barrier_semaphore()
    for device in (twin, at_z(1), at_z(-1), at_x(1), at_x(-1)):
        pl.semaphore_signal(barrier, inc=1, device_id=device, device_id_type=pl.DeviceIdType.MESH)

    own_copies = []
    for q in (0, 1, 2, 3):
        copy = pltpu.make_async_copy(
            table_ref.at[pl.ds(pl.multiple_of((core * 4 + q) * PART_ROWS, PART_ROWS), PART_ROWS)],
            own.at[pl.ds(q * PART_ROWS, PART_ROWS)], own_sem.at[q])
        copy.start()
        own_copies.append(copy)
    pl.semaphore_wait(barrier, 5)

    def ring(q, n, size, here, at, sign, plain, send, recv, send_sem, recv_sem):
        half = n // 2

        def slot_of(kind, j):
            return j - 1 if kind == "major" else half + j - 1

        def copy_of(kind, j):
            slot = slot_of(kind, j)
            return pltpu.make_async_remote_copy(
                src_ref=send.at[q % 2, slot], dst_ref=recv.at[q % 2, slot],
                send_sem=send_sem.at[q % 2, slot], recv_sem=recv_sem.at[q % 2, slot],
                device_id=at(sign if kind == "major" else -sign), device_id_type=pl.DeviceIdType.MESH)

        def owner_of(kind, j):
            shift = sign * (half + 1 - j) if kind == "major" else -sign * (half - j)
            return (here + shift + n) % n

        def step(kind, j):
            o = owner_of(kind, j)
            slot = slot_of(kind, j)
            if j > 1:
                copy_of(kind, j - 1).wait_recv()

            def tile(i, carry):
                rows = pl.ds(pl.multiple_of(i * BOX, BOX), BOX)
                total = plain(o, i)
                if j > 1:
                    total = total + recv[q % 2, slot - 1, rows, :].astype(jnp.float32)
                send[q % 2, slot, rows, :] = total.astype(jnp.bfloat16)
                return carry

            lax.fori_loop(0, size // BOX, tile, 0)
            copy_of(kind, j).start()

        def final(store):
            copy_of("major", half).wait_recv()
            copy_of("minor", half - 1).wait_recv()

            def tile(i, carry):
                rows = pl.ds(pl.multiple_of(i * BOX, BOX), BOX)
                store(i, plain(here, i) + recv[q % 2, half - 1, rows, :].astype(jnp.float32)
                      + recv[q % 2, n - 2, rows, :].astype(jnp.float32))
                return carry

            lax.fori_loop(0, size // BOX, tile, 0)

        def drain():
            for kind, steps in (("major", half), ("minor", half - 1)):
                for j in range(1, steps + 1):
                    copy_of(kind, j).wait_send()

        return step, final, drain, owner_of

    A, B = XS * BOX, ZS * BOX
    twin_copies = {}

    def twin_copy(q, kind, j, o, size):
        index = len(twin_copies)
        rows = pl.multiple_of(q * PART_ROWS + o * size, size)
        copy = pltpu.make_async_remote_copy(
            src_ref=table_ref.at[pl.ds(pl.multiple_of((1 - core) * 4 * PART_ROWS + rows, size), size)],
            dst_ref=sib.at[pl.ds(rows, size)], send_sem=sib_send.at[index], recv_sem=sib_recv.at[index],
            device_id=twin, device_id_type=pl.DeviceIdType.MESH)
        copy.start()
        twin_copies[q, kind, j] = copy

    def plain_first(q, size):
        def plain(o, i):
            rows = pl.ds(pl.multiple_of(q * PART_ROWS + o * size + i * BOX, BOX), BOX)
            return own[rows, :].astype(jnp.float32) + sib[rows, :].astype(jnp.float32)
        return plain

    first, second = [], []
    for q in range(4):
        sign = 1 if q % 2 == 0 else -1
        if q < 2:
            first.append(ring(q, ZS, A, z, at_z, sign, plain_first(q, A), send_a, recv_a, a_send, a_recv))
            second.append(ring(q, XS, BOX, x, at_x, sign,
                               lambda o, i, q=q: mid_a[q % 2, pl.ds(pl.multiple_of(o * BOX, BOX), BOX), :],
                               send_c, recv_c, c_send, c_recv))
        else:
            first.append(ring(q, XS, B, x, at_x, sign, plain_first(q, B), send_b, recv_b, b_send, b_recv))
            second.append(ring(q, ZS, BOX, z, at_z, sign,
                               lambda o, i, q=q: mid_b[q % 2, pl.ds(pl.multiple_of(o * BOX, BOX), BOX), :],
                               send_d, recv_d, d_send, d_recv))

    order = []
    for kind in ("major", "minor"):
        order += [(0, kind, 1), (1, kind, 1)]
    order += [(2, "major", 1), (3, "major", 1), (2, "minor", 1), (3, "minor", 1)]
    order += [(0, "major", 2), (1, "major", 2), (0, "minor", 2), (1, "minor", 2)]
    order += [(2, "major", 2), (3, "major", 2)]
    for j in (3,):
        order += [(0, "major", j), (1, "major", j), (0, "minor", j), (1, "minor", j)]
    order += [(0, "major", 4), (1, "major", 4)]
    order += [(2, "own", 0), (3, "own", 0), (0, "own", 0), (1, "own", 0)]

    for q, kind, j in order:
        o = (z if q < 2 else x) if kind == "own" else first[q][3](kind, j)
        twin_copy(q, kind, j, o, A if q < 2 else B)

    waited = set()
    for q, kind, j in order:
        if q not in waited:
            own_copies[q].wait()
            waited.add(q)
        twin_copies[q, kind, j].wait_recv()
        if kind != "own":
            first[q][0](kind, j)
        else:
            def store(i, value, q=q):
                mid = mid_a if q < 2 else mid_b
                mid[q % 2, pl.ds(pl.multiple_of(i * BOX, BOX), BOX), :] = value
            first[q][1](store)
            second[q][0]("major", 1)
            second[q][0]("minor", 1)
    for j in (2, 3, 4):
        for q in (2, 3):
            second[q][0]("major", j)
            if j < 4:
                second[q][0]("minor", j)
        if j == 2:
            for q in (0, 1):
                second[q][0]("major", j)

    def store_last(i, value):
        last[...] = value

    for q in (0, 1, 2, 3):
        second[q][1](store_last)
        out_ref[0, q] = last[pl.ds(0, 64, stride=2), :]
        out_ref[1, q] = last[pl.ds(1, 64, stride=2), :]
    for q in range(4):
        first[q][2]()
        second[q][2]()
    for copy in twin_copies.values():
        copy.wait_send()


def reduce_table(table):
    dma = pltpu.SemaphoreType.DMA
    A, B = XS * BOX, ZS * BOX
    return pl.pallas_call(
        reduce_kernel,
        out_shape=jax.ShapeDtypeStruct((2, HALFMAPS, 64, BOX), jnp.float32),
        in_specs=[pl.BlockSpec(memory_space=pl.ANY)],
        out_specs=pl.BlockSpec(memory_space=pltpu.VMEM),
        scratch_shapes=[
            pltpu.VMEM((SPOTS // 2, BOX), jnp.bfloat16),
            pltpu.VMEM((SPOTS // 2, BOX), jnp.bfloat16),
            pltpu.VMEM((2, ZS - 1, A, BOX), jnp.bfloat16),
            pltpu.VMEM((2, ZS - 1, A, BOX), jnp.bfloat16),
            pltpu.VMEM((2, XS - 1, B, BOX), jnp.bfloat16),
            pltpu.VMEM((2, XS - 1, B, BOX), jnp.bfloat16),
            pltpu.VMEM((2, A, BOX), jnp.float32),
            pltpu.VMEM((2, B, BOX), jnp.float32),
            pltpu.VMEM((2, XS - 1, BOX, BOX), jnp.bfloat16),
            pltpu.VMEM((2, XS - 1, BOX, BOX), jnp.bfloat16),
            pltpu.VMEM((2, ZS - 1, BOX, BOX), jnp.bfloat16),
            pltpu.VMEM((2, ZS - 1, BOX, BOX), jnp.bfloat16),
            pltpu.VMEM((BOX, BOX), jnp.float32),
            dma((4,)), dma((24,)), dma((24,)),
            dma((2, ZS - 1)), dma((2, ZS - 1)), dma((2, XS - 1)), dma((2, XS - 1)),
            dma((2, XS - 1)), dma((2, XS - 1)), dma((2, ZS - 1)), dma((2, ZS - 1)),
        ],
        compiler_params=pltpu.CompilerParams(
            collective_id=0, has_side_effects=True, vmem_limit_bytes=40 * 2**20),
        name="reduce_table",
    )(table)


def tables():
    cos_table, sin_table = fourier_tables(BOX)
    stacked = jnp.concatenate([cos_table, sin_table], 0)
    mixed = jnp.concatenate([
        jnp.concatenate([cos_table.T, sin_table.T], 1),
        jnp.concatenate([-sin_table.T, cos_table.T], 1)], 0)
    return stacked, mixed


def places_of(rows, labels, slab_index, slab_count):
    owner, offset = rows // 64, rows % 64
    tilt = owner // slab_count
    core, z, x = tilt % 2, tilt // 2 % ZS, tilt // (2 * ZS)
    label = labels[:, None]
    chip = jnp.where(label < 2, z * XS + x, x * ZS + z)
    place = 2 * (((core * HALFMAPS + label) * (TILTS // 2) + chip) * 64 + offset)
    return jnp.where(owner % slab_count == slab_index, place, -1 - lax.broadcasted_iota(jnp.int32, rows.shape, 1))


def body(tilt_images, corners, visible, defocus, labels, row_owner, row_offset):
    slab_count = lax.axis_size("slab")
    slab_index = lax.axis_index("slab")
    rows = (row_owner[..., 0] * 64 + row_offset).astype(jnp.float32)
    packed = jnp.concatenate([
        rows.transpose(1, 0, 2),
        jnp.pad(jnp.stack([defocus.T, jnp.broadcast_to(labels.astype(jnp.float32), (TILTS, 2))], 1),
                ((0, 0), (0, 0), (0, BOX - 2)))], 1)
    packed = lax.all_to_all(packed, "tilt", split_axis=0, concat_axis=0, tiled=True)
    rows = packed[:, :2].reshape(PARTICLES, BOX).astype(jnp.int32)
    defocus_all = packed[:, 2, :2].reshape(PARTICLES)
    labels_all = packed[:, 3, :2].reshape(PARTICLES).astype(jnp.int32)
    places = places_of(rows, labels_all, slab_index, slab_count)
    stacked, mixed = tables()
    table = insert(corners[:, 0], visible, tilt_images[0], places, stacked, mixed, transfer_factors(defocus_all))
    return reduce_table(table)


def solution(mesh):
    return jax.shard_map(
        body,
        mesh=mesh,
        in_specs=(
            P("tilt", None, None),
            P(None, "tilt", None),
            P("tilt", None),
            P("tilt", None),
            P("tilt"),
            P("tilt", None, None, None),
            P("tilt", None, None),
        ),
        out_specs=P(None, None, ("tilt", "slab"), None),
        check_vma=False,
    )
```

```python
import jax
import jax.numpy as jnp
import numpy as np
from jax import lax
from jax.experimental import pallas as pl
from jax.experimental.pallas import tpu as pltpu
from jax.sharding import PartitionSpec as P

BOX = 128
HALFMAPS = 4
AMPLITUDE = 0.1
TILTS = 64
PARTICLES = 128
CELLS = TILTS * HALFMAPS * 64
GROUP = 8
PAIRS = PARTICLES // 2
WINDOW = 2 * GROUP
SLOTS = 64


def fourier_tables(width):
    positions = jnp.arange(width, dtype=jnp.int32)
    frequency = positions - width // 2
    phase_index = frequency[:, None] * positions[None, :] % width
    angles = phase_index.astype(jnp.float32) * (2.0 * jnp.pi / width)
    return (jnp.cos(angles).astype(jnp.bfloat16), (-jnp.sin(angles)).astype(jnp.bfloat16))


def transfer_factors(defocus_values):
    frequency = (jnp.arange(BOX, dtype=jnp.int32) - BOX // 2).astype(jnp.float32) / BOX
    angle = jnp.pi * defocus_values[:, None] * (frequency * frequency)[None, :]
    cos_part, sin_part = jnp.cos(angle), jnp.sin(angle)
    main = jnp.sqrt(1.0 - AMPLITUDE * AMPLITUDE)
    first = -(main * sin_part + AMPLITUDE * cos_part) / BOX
    second = -(main * cos_part - AMPLITUDE * sin_part) / BOX
    return first.T, second.T, cos_part, sin_part


def insert_kernel(corner_ref, seen_ref, image_ref, places_ref, stacked_ref, mixed_ref, first_ref, second_ref,
                  cos_ref, sin_ref, out_ref, left, right, lists, spans, late_rows, spot_s, row_s, late_s, span_s,
                  late_rows_s, patches, sides, slices_a, slices_b, kept_slices, table, sems):
    lane = lax.broadcasted_iota(jnp.int32, (BOX, BOX), 1)
    entry = lax.broadcasted_iota(jnp.int32, (8, BOX), 0)
    rank = jnp.zeros((8, BOX), jnp.int32)
    spots = [2 * CELLS + 2 * ((8 * s + entry) % (2 * GROUP)) for s in range(SLOTS // 8)]
    spare = jnp.concatenate(spots, axis=0)
    sources = [jnp.zeros((8, BOX), jnp.int32) for _ in range(SLOTS // 8)]
    first_row, last_row = jnp.full((8, BOX), BOX, jnp.int32), jnp.zeros((8, BOX), jnp.int32)
    for j in range(BOX // 8):
        place = places_ref[8 * j:8 * j + 8, :]
        kept = place >= 0
        for s in range(SLOTS // 8):
            hit = kept & (rank == s)
            spots[s] = jnp.where(hit, place, spots[s])
            sources[s] = jnp.where(hit, 2 * (8 * j + entry), sources[s])
        over = kept & (rank >= SLOTS // 8)
        late_rows[8 * j:8 * j + 8, :] = jnp.where(over, place, 2 * CELLS)
        first_row = jnp.minimum(first_row, jnp.where(over, 8 * j + entry, BOX))
        last_row = jnp.maximum(last_row, jnp.where(over, 8 * j + entry + 1, 0))
        rank = rank + jnp.where(kept, 1, 0)
    spot = jnp.concatenate(spots, axis=0)
    slot = lax.broadcasted_iota(jnp.int32, (SLOTS, BOX), 0)
    late = jnp.zeros((SLOTS, BOX), jnp.bool_)
    for d in range(1, WINDOW):
        late = late | ((pltpu.roll(spot, SLOTS - d, axis=0) == spot) & (slot < SLOTS - d))
    lists[0, :, :BOX] = jnp.where(late, spare, spot)
    lists[0, :, BOX:] = spare
    lists[1, :, :BOX] = jnp.concatenate(sources, axis=0)
    lists[1, :, BOX:] = jnp.zeros((SLOTS, BOX), jnp.int32)
    lists[2, :, :BOX] = jnp.where(late, spot, spare)
    lists[2, :, BOX:] = spare
    row = lax.broadcasted_iota(jnp.int32, (8, BOX), 0)
    bounds = [
        jnp.min(jnp.where(late, slot, SLOTS), axis=0, keepdims=True),
        jnp.max(jnp.where(late, slot + 1, 0), axis=0, keepdims=True),
        jnp.min(first_row, axis=0, keepdims=True),
        jnp.max(last_row, axis=0, keepdims=True),
    ]
    spans[...] = jnp.where(row == 0, bounds[0], jnp.where(row == 1, bounds[1], jnp.where(row == 2, bounds[2], bounds[3])))
    copies = [
        pltpu.make_async_copy(lists.at[0], spot_s, sems.at[0]),
        pltpu.make_async_copy(lists.at[1], row_s, sems.at[1]),
        pltpu.make_async_copy(lists.at[2], late_s, sems.at[2]),
        pltpu.make_async_copy(spans, span_s, sems.at[3]),
        pltpu.make_async_copy(late_rows, late_rows_s, sems.at[4]),
    ]
    for copy in copies:
        copy.start()
    left[...] = image_ref[:, :BOX].astype(jnp.float32)
    right[...] = image_ref[:, BOX:].astype(jnp.float32)

    def clear(i, carry):
        table[pl.ds(pl.multiple_of(i * 512, 512), 512), :] = jnp.zeros((512, BOX), jnp.float32)
        return carry

    lax.fori_loop(0, 2 * CELLS // 512, clear, 0)
    for copy in copies:
        copy.wait()

    def window(p):
        row, col = corner_ref[0, p], corner_ref[1, p]
        a = left[pl.ds(row, BOX), :]
        b = right[pl.ds(row, BOX), :]
        cut = pltpu.roll(jnp.where(lane >= col, a, b), (BOX - col) % BOX, axis=1)
        average = jnp.sum(jnp.sum(cut, axis=0, keepdims=True), axis=1, keepdims=True) * (1.0 / (BOX * BOX))
        centered = cut - average
        variance = jnp.sum(
            jnp.sum(centered * centered, axis=0, keepdims=True), axis=1, keepdims=True) * (1.0 / (BOX * BOX))
        scale = lax.rsqrt(variance + 1e-05) * seen_ref[0, p].astype(jnp.float32)
        return (centered * scale).astype(jnp.bfloat16)

    def cut_pair(pair, target):
        p = 2 * jnp.minimum(pair, PAIRS - 1)
        target[:, :BOX] = window(p)
        target[:, BOX:] = window(p + 1)

    def first_pair(source, target):
        section = jnp.dot(stacked_ref[...], source[...], preferred_element_type=jnp.float32).astype(jnp.bfloat16)
        for j in range(2):
            target[j * BOX:(j + 1) * BOX, :BOX] = section[:BOX, j * BOX:(j + 1) * BOX]
            target[j * BOX:(j + 1) * BOX, BOX:] = section[BOX:, j * BOX:(j + 1) * BOX]

    def second_pair(pair, source, targets):
        p = 2 * jnp.clip(pair, 0, PAIRS - 1)
        spectrum = jnp.dot(source[...], mixed_ref[...], preferred_element_type=jnp.float32)
        for j, target in enumerate(targets):
            pick = jnp.full((BOX, BOX), p + j, jnp.int32)
            first = jnp.take_along_axis(first_ref[...], pick, axis=1)
            second = jnp.take_along_axis(second_ref[...], pick, axis=1)
            transfer = first * cos_ref[pl.ds(p + j, 1), :] + second * sin_ref[pl.ds(p + j, 1), :]
            real = transfer * spectrum[j * BOX:(j + 1) * BOX, :BOX]
            imag = transfer * spectrum[j * BOX:(j + 1) * BOX, BOX:]
            target[pl.ds(0, BOX, stride=2), :] = real
            target[pl.ds(1, BOX, stride=2), :] = imag
            kept_slices[p + j, pl.ds(0, BOX, stride=2), :] = real
            kept_slices[p + j, pl.ds(1, BOX, stride=2), :] = imag

    def insert(p, source):
        waiting = None
        for g in range(SLOTS // GROUP + 1):
            if g < SLOTS // GROUP:
                spots = [spot_s[g * GROUP + i, p] for i in range(GROUP)]
                sums = [table[pl.ds(spots[i], 2), :] + source[pl.ds(row_s[g * GROUP + i, p], 2), :]
                        for i in range(GROUP)]
            if waiting is not None:
                for spot, total in zip(*waiting):
                    table[pl.ds(spot, 2), :] = total
            waiting = (spots, sums)

    def insert_late(p, carry):
        @pl.when(span_s[1, p] + span_s[3, p] > 0)
        def _():
            def from_slot(i, carry):
                table[pl.ds(late_s[i, p], 2), :] += kept_slices[p, pl.ds(row_s[i, p], 2), :]
                return carry

            def from_row(i, carry):
                table[pl.ds(late_rows_s[i, p], 2), :] += kept_slices[p, pl.ds(2 * i, 2), :]
                return carry

            lax.fori_loop(span_s[0, p], span_s[1, p], from_slot, 0)
            lax.fori_loop(span_s[2, p], span_s[3, p], from_row, 0)

        return carry

    def step(i, carry):
        for h in range(2):
            tick = 2 * i + h
            done = tick - 3
            p = 2 * jnp.where(done < 0, PAIRS, done)
            insert(p, slices_a[1 - h])
            insert(p + 1, slices_b[1 - h])
            second_pair(tick - 2, sides[h], (slices_a[h], slices_b[h]))
            first_pair(patches[1 - h], sides[1 - h])
            cut_pair(tick, patches[h])
        return carry

    lax.fori_loop(0, (PAIRS + 4) // 2, step, 0)
    lax.fori_loop(0, PARTICLES, insert_late, 0)

    def finish(i, carry):
        rows = pl.ds(pl.multiple_of(i * 512, 512), 512)
        out_ref[rows, :] = table[rows, :].astype(jnp.bfloat16)
        return carry

    lax.fori_loop(0, 2 * CELLS // 512, finish, 0)


def insert(corners, seen, image, places, stacked, mixed, factors):
    whole = pl.BlockSpec(memory_space=pltpu.VMEM)
    scalars = pl.BlockSpec(memory_space=pltpu.SMEM)
    return pl.pallas_call(
        insert_kernel,
        out_shape=jax.ShapeDtypeStruct((2 * CELLS, BOX), jnp.bfloat16),
        in_specs=[scalars, scalars] + [whole] * 8,
        out_specs=whole,
        scratch_shapes=[
            pltpu.VMEM((256, BOX), jnp.float32),
            pltpu.VMEM((256, BOX), jnp.float32),
            pltpu.VMEM((3, SLOTS, 2 * BOX), jnp.int32),
            pltpu.VMEM((8, BOX), jnp.int32),
            pltpu.VMEM((BOX, BOX), jnp.int32),
            pltpu.SMEM((SLOTS, 2 * BOX), jnp.int32),
            pltpu.SMEM((SLOTS, 2 * BOX), jnp.int32),
            pltpu.SMEM((SLOTS, 2 * BOX), jnp.int32),
            pltpu.SMEM((8, BOX), jnp.int32),
            pltpu.SMEM((BOX, BOX), jnp.int32),
            [pltpu.VMEM((BOX, 2 * BOX), jnp.bfloat16)] * 2,
            [pltpu.VMEM((2 * BOX, 2 * BOX), jnp.bfloat16)] * 2,
            [pltpu.VMEM((2 * BOX, BOX), jnp.float32)] * 2,
            [pltpu.VMEM((2 * BOX, BOX), jnp.float32)] * 2,
            pltpu.VMEM((PARTICLES, 2 * BOX, BOX), jnp.float32),
            pltpu.VMEM((2 * CELLS + 4 * GROUP, BOX), jnp.float32),
            pltpu.SemaphoreType.DMA((5,)),
        ],
        compiler_params=pltpu.CompilerParams(vmem_limit_bytes=56 * 2**20),
        name="insert_slices",
    )(corners, seen, image, places, stacked, mixed, *factors)


ZS, XS = 8, 4
PART_ROWS = TILTS // 2 * BOX
SPOTS = 2 * CELLS


def reduce_kernel(table_ref, out_ref, own, sib, send_a, recv_a, send_b, recv_b, mid_a, mid_b, send_c, recv_c, send_d,
                  recv_d, last, own_sem, sib_send, sib_recv, a_send, a_recv, b_send, b_recv, c_send, c_recv, d_send,
                  d_recv):
    tilt, slab = lax.axis_index("tilt"), lax.axis_index("slab")
    core, z, x = tilt % 2, tilt // 2 % ZS, tilt // (2 * ZS)

    def at_z(step):
        return (x * (2 * ZS) + (z + step + ZS) % ZS * 2 + core, slab)

    def at_x(step):
        return ((x + step + XS) % XS * (2 * ZS) + z * 2 + core, slab)

    twin = (tilt + 1 - 2 * core, slab)
    barrier = pltpu.get_barrier_semaphore()
    for device in (twin, at_z(1), at_z(-1), at_x(1), at_x(-1)):
        pl.semaphore_signal(barrier, inc=1, device_id=device, device_id_type=pl.DeviceIdType.MESH)

    own_copies = []
    for q in (0, 1, 2, 3):
        copy = pltpu.make_async_copy(
            table_ref.at[pl.ds(pl.multiple_of((core * 4 + q) * PART_ROWS, PART_ROWS), PART_ROWS)],
            own.at[pl.ds(q * PART_ROWS, PART_ROWS)], own_sem.at[q])
        copy.start()
        own_copies.append(copy)
    pl.semaphore_wait(barrier, 5)

    def ring(q, n, size, here, at, sign, plain, send, recv, send_sem, recv_sem):
        half = n // 2

        def slot_of(kind, j):
            return j - 1 if kind == "major" else half + j - 1

        def copy_of(kind, j):
            slot = slot_of(kind, j)
            return pltpu.make_async_remote_copy(
                src_ref=send.at[q % 2, slot], dst_ref=recv.at[q % 2, slot],
                send_sem=send_sem.at[q % 2, slot], recv_sem=recv_sem.at[q % 2, slot],
                device_id=at(sign if kind == "major" else -sign), device_id_type=pl.DeviceIdType.MESH)

        def owner_of(kind, j):
            shift = sign * (half + 1 - j) if kind == "major" else -sign * (half - j)
            return (here + shift + n) % n

        def step(kind, j):
            o = owner_of(kind, j)
            slot = slot_of(kind, j)
            if j > 1:
                copy_of(kind, j - 1).wait_recv()

            def tile(i, carry):
                rows = pl.ds(pl.multiple_of(i * BOX, BOX), BOX)
                total = plain(o, i)
                if j > 1:
                    total = total + recv[q % 2, slot - 1, rows, :].astype(jnp.float32)
                send[q % 2, slot, rows, :] = total.astype(jnp.bfloat16)
                return carry

            lax.fori_loop(0, size // BOX, tile, 0)
            copy_of(kind, j).start()

        def final(store):
            copy_of("major", half).wait_recv()
            copy_of("minor", half - 1).wait_recv()

            def tile(i, carry):
                rows = pl.ds(pl.multiple_of(i * BOX, BOX), BOX)
                store(i, plain(here, i) + recv[q % 2, half - 1, rows, :].astype(jnp.float32)
                      + recv[q % 2, n - 2, rows, :].astype(jnp.float32))
                return carry

            lax.fori_loop(0, size // BOX, tile, 0)

        def drain():
            for kind, steps in (("major", half), ("minor", half - 1)):
                for j in range(1, steps + 1):
                    copy_of(kind, j).wait_send()

        return step, final, drain, owner_of

    A, B = XS * BOX, ZS * BOX
    twin_copies = {}

    def twin_copy(q, kind, j, o, size):
        index = len(twin_copies)
        rows = pl.multiple_of(q * PART_ROWS + o * size, size)
        copy = pltpu.make_async_remote_copy(
            src_ref=table_ref.at[pl.ds(pl.multiple_of((1 - core) * 4 * PART_ROWS + rows, size), size)],
            dst_ref=sib.at[pl.ds(rows, size)], send_sem=sib_send.at[index], recv_sem=sib_recv.at[index],
            device_id=twin, device_id_type=pl.DeviceIdType.MESH)
        copy.start()
        twin_copies[q, kind, j] = copy

    def plain_first(q, size):
        def plain(o, i):
            rows = pl.ds(pl.multiple_of(q * PART_ROWS + o * size + i * BOX, BOX), BOX)
            return own[rows, :].astype(jnp.float32) + sib[rows, :].astype(jnp.float32)
        return plain

    first, second = [], []
    for q in range(4):
        sign = 1 if q % 2 == 0 else -1
        if q < 2:
            first.append(ring(q, ZS, A, z, at_z, sign, plain_first(q, A), send_a, recv_a, a_send, a_recv))
            second.append(ring(q, XS, BOX, x, at_x, sign,
                               lambda o, i, q=q: mid_a[q % 2, pl.ds(pl.multiple_of(o * BOX, BOX), BOX), :],
                               send_c, recv_c, c_send, c_recv))
        else:
            first.append(ring(q, XS, B, x, at_x, sign, plain_first(q, B), send_b, recv_b, b_send, b_recv))
            second.append(ring(q, ZS, BOX, z, at_z, sign,
                               lambda o, i, q=q: mid_b[q % 2, pl.ds(pl.multiple_of(o * BOX, BOX), BOX), :],
                               send_d, recv_d, d_send, d_recv))

    order = []
    for kind in ("major", "minor"):
        order += [(0, kind, 1), (1, kind, 1)]
    order += [(2, "major", 1), (3, "major", 1), (2, "minor", 1), (3, "minor", 1)]
    order += [(0, "major", 2), (1, "major", 2), (0, "minor", 2), (1, "minor", 2)]
    order += [(2, "major", 2), (3, "major", 2)]
    for j in (3,):
        order += [(0, "major", j), (1, "major", j), (0, "minor", j), (1, "minor", j)]
    order += [(0, "major", 4), (1, "major", 4)]
    order += [(2, "own", 0), (3, "own", 0), (0, "own", 0), (1, "own", 0)]

    for q, kind, j in order:
        o = (z if q < 2 else x) if kind == "own" else first[q][3](kind, j)
        twin_copy(q, kind, j, o, A if q < 2 else B)

    waited = set()
    for q, kind, j in order:
        if q not in waited:
            own_copies[q].wait()
            waited.add(q)
        twin_copies[q, kind, j].wait_recv()
        if kind != "own":
            first[q][0](kind, j)
        else:
            def store(i, value, q=q):
                mid = mid_a if q < 2 else mid_b
                mid[q % 2, pl.ds(pl.multiple_of(i * BOX, BOX), BOX), :] = value
            first[q][1](store)
            second[q][0]("major", 1)
            second[q][0]("minor", 1)
    for j in (2, 3, 4):
        for q in (2, 3):
            second[q][0]("major", j)
            if j < 4:
                second[q][0]("minor", j)
        if j == 2:
            for q in (0, 1):
                second[q][0]("major", j)

    def store_last(i, value):
        last[...] = value

    for q in (0, 1, 2, 3):
        second[q][1](store_last)
        out_ref[0, q] = last[pl.ds(0, 64, stride=2), :]
        out_ref[1, q] = last[pl.ds(1, 64, stride=2), :]
    for q in range(4):
        first[q][2]()
        second[q][2]()
    for copy in twin_copies.values():
        copy.wait_send()


def reduce_table(table):
    dma = pltpu.SemaphoreType.DMA
    A, B = XS * BOX, ZS * BOX
    return pl.pallas_call(
        reduce_kernel,
        out_shape=jax.ShapeDtypeStruct((2, HALFMAPS, 64, BOX), jnp.float32),
        in_specs=[pl.BlockSpec(memory_space=pl.ANY)],
        out_specs=pl.BlockSpec(memory_space=pltpu.VMEM),
        scratch_shapes=[
            pltpu.VMEM((SPOTS // 2, BOX), jnp.bfloat16),
            pltpu.VMEM((SPOTS // 2, BOX), jnp.bfloat16),
            pltpu.VMEM((2, ZS - 1, A, BOX), jnp.bfloat16),
            pltpu.VMEM((2, ZS - 1, A, BOX), jnp.bfloat16),
            pltpu.VMEM((2, XS - 1, B, BOX), jnp.bfloat16),
            pltpu.VMEM((2, XS - 1, B, BOX), jnp.bfloat16),
            pltpu.VMEM((2, A, BOX), jnp.float32),
            pltpu.VMEM((2, B, BOX), jnp.float32),
            pltpu.VMEM((2, XS - 1, BOX, BOX), jnp.bfloat16),
            pltpu.VMEM((2, XS - 1, BOX, BOX), jnp.bfloat16),
            pltpu.VMEM((2, ZS - 1, BOX, BOX), jnp.bfloat16),
            pltpu.VMEM((2, ZS - 1, BOX, BOX), jnp.bfloat16),
            pltpu.VMEM((BOX, BOX), jnp.float32),
            dma((4,)), dma((24,)), dma((24,)),
            dma((2, ZS - 1)), dma((2, ZS - 1)), dma((2, XS - 1)), dma((2, XS - 1)),
            dma((2, XS - 1)), dma((2, XS - 1)), dma((2, ZS - 1)), dma((2, ZS - 1)),
        ],
        compiler_params=pltpu.CompilerParams(
            collective_id=0, has_side_effects=True, vmem_limit_bytes=60 * 2**20),
        name="reduce_table",
    )(table)


def tables():
    cos_table, sin_table = fourier_tables(BOX)
    stacked = jnp.concatenate([cos_table, sin_table], 0)
    mixed = jnp.concatenate([
        jnp.concatenate([cos_table.T, sin_table.T], 1),
        jnp.concatenate([-sin_table.T, cos_table.T], 1)], 0)
    return stacked, mixed


def places_of(rows, labels, slab_index, slab_count):
    owner, offset = rows // 64, rows % 64
    tilt = owner // slab_count
    core, z, x = tilt % 2, tilt // 2 % ZS, tilt // (2 * ZS)
    label = labels[:, None]
    chip = jnp.where(label < 2, z * XS + x, x * ZS + z)
    place = 2 * (((core * HALFMAPS + label) * (TILTS // 2) + chip) * 64 + offset)
    return jnp.where(owner % slab_count == slab_index, place, -1).T


def body(tilt_images, corners, visible, defocus, labels, row_owner, row_offset):
    slab_count = lax.axis_size("slab")
    slab_index = lax.axis_index("slab")
    rows = (row_owner[..., 0] * 64 + row_offset).astype(jnp.float32)
    packed = jnp.concatenate([
        rows.transpose(1, 0, 2),
        jnp.pad(jnp.stack([defocus.T, jnp.broadcast_to(labels.astype(jnp.float32), (TILTS, 2))], 1),
                ((0, 0), (0, 0), (0, BOX - 2)))], 1)
    packed = lax.all_to_all(packed, "tilt", split_axis=0, concat_axis=0, tiled=True)
    rows = packed[:, :2].reshape(PARTICLES, BOX).astype(jnp.int32)
    defocus_all = packed[:, 2, :2].reshape(PARTICLES)
    labels_all = packed[:, 3, :2].reshape(PARTICLES).astype(jnp.int32)
    places = places_of(rows, labels_all, slab_index, slab_count)
    stacked, mixed = tables()
    table = insert(corners[:, 0], visible, tilt_images[0], places, stacked, mixed, transfer_factors(defocus_all))
    return reduce_table(table)


def solution(mesh):
    return jax.shard_map(
        body,
        mesh=mesh,
        in_specs=(
            P("tilt", None, None),
            P(None, "tilt", None),
            P("tilt", None),
            P("tilt", None),
            P("tilt"),
            P("tilt", None, None, None),
            P("tilt", None, None),
        ),
        out_specs=P(None, None, ("tilt", "slab"), None),
        check_vma=False,
    )
```

```python
import math

import jax
import jax.numpy as jnp
import numpy as np
from jax import lax
from jax.experimental import pallas as pl
from jax.experimental.pallas import tpu as pltpu
from jax.sharding import PartitionSpec as P

BOX = 128
HALFMAPS = 4
AMPLITUDE = 0.1
TILTS = 64
PARTICLES = 128
CELLS = TILTS * HALFMAPS * 64
GROUP = 8
PAIRS = PARTICLES // 2
WINDOW = 2 * GROUP
SLOTS = 64
CUTS = 4


def fourier_tables(width):
    positions = jnp.arange(width, dtype=jnp.int32)
    frequency = positions - width // 2
    phase_index = frequency[:, None] * positions[None, :] % width
    angles = phase_index.astype(jnp.float32) * (2.0 * jnp.pi / width)
    return (jnp.cos(angles).astype(jnp.bfloat16), (-jnp.sin(angles)).astype(jnp.bfloat16))


def transfer_factors(defocus, column):
    frequency = (column - BOX // 2).astype(jnp.float32) / BOX
    angle = jnp.pi * defocus * (frequency * frequency)
    cos_part, sin_part = jnp.cos(angle), jnp.sin(angle)
    main = math.sqrt(1.0 - AMPLITUDE * AMPLITUDE)
    first = -(main * sin_part + AMPLITUDE * cos_part) / BOX
    second = -(main * cos_part - AMPLITUDE * sin_part) / BOX
    return first, second, cos_part, sin_part


def swap_kernel(corner_ref, seen_ref, image_ref, owner_ref, offset_ref, misc_ref, patches_ref, places_ref, first_ref,
                second_ref, cos_ref, sin_ref, left, right, outbox, inbox, send_sem, recv_sem):
    tilt, slab = lax.axis_index("tilt"), lax.axis_index("slab")
    barrier = pltpu.get_barrier_semaphore()

    def peer(d):
        return (tilt + d) % TILTS

    def greet(d, carry):
        pl.semaphore_signal(barrier, inc=1, device_id=(peer(d), slab), device_id_type=pl.DeviceIdType.MESH)
        return carry

    lax.fori_loop(1, TILTS, greet, 0)
    for j in range(2):
        outbox[:, j, :] = (owner_ref[j] * 64 + offset_ref[j]).astype(jnp.float32)
        outbox[:, 2 + j, :] = jnp.broadcast_to(misc_ref[j:j + 1, :], (TILTS, BOX))
    pl.semaphore_wait(barrier, TILTS - 1)

    def message(to, origin):
        return pltpu.make_async_remote_copy(
            src_ref=outbox.at[to], dst_ref=inbox.at[origin], send_sem=send_sem.at[to], recv_sem=recv_sem.at[origin],
            device_id=(to, slab), device_id_type=pl.DeviceIdType.MESH)

    def send(d, carry):
        message(peer(d), tilt).start()
        return carry

    lax.fori_loop(1, TILTS, send, 0)
    inbox[tilt] = outbox[tilt]
    left[...] = image_ref[:, :BOX].astype(jnp.float32)
    right[...] = image_ref[:, BOX:].astype(jnp.float32)
    lane = lax.broadcasted_iota(jnp.int32, (BOX, BOX), 1)

    def window(p):
        row, col = corner_ref[0, p], corner_ref[1, p]
        a = left[pl.ds(row, BOX), :]
        b = right[pl.ds(row, BOX), :]
        cut = pltpu.roll(jnp.where(lane >= col, a, b), (BOX - col) % BOX, axis=1)
        average = jnp.sum(jnp.sum(cut, axis=0, keepdims=True), axis=1, keepdims=True) * (1.0 / (BOX * BOX))
        centered = cut - average
        variance = jnp.sum(
            jnp.sum(centered * centered, axis=0, keepdims=True), axis=1, keepdims=True) * (1.0 / (BOX * BOX))
        scale = lax.rsqrt(variance + 1e-05) * seen_ref[0, p].astype(jnp.float32)
        return (centered * scale).astype(jnp.bfloat16)

    def cut_pairs(i, carry):
        windows = [window(CUTS * i + j) for j in range(CUTS)]
        for j, patch in enumerate(windows):
            patches_ref[CUTS // 2 * i + j // 2, :, j % 2 * BOX:(j % 2 + 1) * BOX] = patch
        return carry

    lax.fori_loop(0, PARTICLES // CUTS, cut_pairs, 0)

    def receive(d, carry):
        message(tilt, peer(d)).wait_recv()
        return carry

    lax.fori_loop(1, TILTS, receive, 0)

    rows = jnp.concatenate([inbox[:, 0, :], inbox[:, 1, :]], axis=0).astype(jnp.int32)
    misc = jnp.concatenate([inbox[:, 2, :]] * 2, axis=0)
    line = lax.broadcasted_iota(jnp.int32, (BOX, BOX), 0)
    mine = jnp.where(lane == jnp.where(line < TILTS, tilt, TILTS + tilt), misc, 0.0)
    defocus = jnp.sum(mine, axis=1, keepdims=True)
    labels = jnp.concatenate([inbox[:, 3, :]] * 2, axis=0)
    label = jnp.sum(jnp.where(lane == jnp.where(line < TILTS, 0, TILTS), labels, 0.0), axis=1, keepdims=True)
    places_ref[...] = places_of(rows, label.astype(jnp.int32), slab, lax.axis_size("slab")).T
    first, second, cos_part, sin_part = transfer_factors(defocus, lane)
    first_ref[...] = first.T
    second_ref[...] = second.T
    cos_ref[...] = cos_part
    sin_ref[...] = sin_part

    def sent(d, carry):
        message(peer(d), tilt).wait_send()
        return carry

    lax.fori_loop(1, TILTS, sent, 0)


def swap(corners, seen, image, owners, offsets, misc):
    whole = pl.BlockSpec(memory_space=pltpu.VMEM)
    scalars = pl.BlockSpec(memory_space=pltpu.SMEM)
    square = jax.ShapeDtypeStruct((BOX, BOX), jnp.float32)
    return pl.pallas_call(
        swap_kernel,
        out_shape=[jax.ShapeDtypeStruct((PAIRS, BOX, 2 * BOX), jnp.bfloat16),
                   jax.ShapeDtypeStruct((BOX, BOX), jnp.int32)] + [square] * 4,
        in_specs=[scalars, scalars] + [whole] * 4,
        out_specs=[whole] * 6,
        scratch_shapes=[
            pltpu.VMEM((256, BOX), jnp.float32),
            pltpu.VMEM((256, BOX), jnp.float32),
            pltpu.VMEM((TILTS, 4, BOX), jnp.float32),
            pltpu.VMEM((TILTS, 4, BOX), jnp.float32),
            pltpu.SemaphoreType.DMA((TILTS,)),
            pltpu.SemaphoreType.DMA((TILTS,)),
        ],
        compiler_params=pltpu.CompilerParams(
            collective_id=1, has_side_effects=True, vmem_limit_bytes=24 * 2**20),
        name="swap_rows",
    )(corners, seen, image, owners, offsets, misc)


def insert_kernel(patches_ref, places_ref, stacked_ref, mixed_ref, first_ref, second_ref, cos_ref, sin_ref, out_ref,
                  lists, spans, late_rows, spot_s, row_s, late_s, span_s, late_rows_s, sides, slices_a, slices_b, kept_slices, table, sems):
    entry = lax.broadcasted_iota(jnp.int32, (8, BOX), 0)
    rank = jnp.zeros((8, BOX), jnp.int32)
    spots = [2 * CELLS + 2 * ((8 * s + entry) % (2 * GROUP)) for s in range(SLOTS // 8)]
    spare = jnp.concatenate(spots, axis=0)
    sources = [jnp.zeros((8, BOX), jnp.int32) for _ in range(SLOTS // 8)]
    first_row, last_row = jnp.full((8, BOX), BOX, jnp.int32), jnp.zeros((8, BOX), jnp.int32)
    for j in range(BOX // 8):
        place = places_ref[8 * j:8 * j + 8, :]
        kept = place >= 0
        for s in range(SLOTS // 8):
            hit = kept & (rank == s)
            spots[s] = jnp.where(hit, place, spots[s])
            sources[s] = jnp.where(hit, 2 * (8 * j + entry), sources[s])
        over = kept & (rank >= SLOTS // 8)
        late_rows[8 * j:8 * j + 8, :] = jnp.where(over, place, 2 * CELLS)
        first_row = jnp.minimum(first_row, jnp.where(over, 8 * j + entry, BOX))
        last_row = jnp.maximum(last_row, jnp.where(over, 8 * j + entry + 1, 0))
        rank = rank + jnp.where(kept, 1, 0)
    spot = jnp.concatenate(spots, axis=0)
    slot = lax.broadcasted_iota(jnp.int32, (SLOTS, BOX), 0)
    late = jnp.zeros((SLOTS, BOX), jnp.bool_)
    for d in range(1, WINDOW):
        late = late | ((pltpu.roll(spot, SLOTS - d, axis=0) == spot) & (slot < SLOTS - d))
    lists[0, :, :BOX] = jnp.where(late, spare, spot)
    lists[0, :, BOX:] = spare
    lists[1, :, :BOX] = jnp.concatenate(sources, axis=0)
    lists[1, :, BOX:] = jnp.zeros((SLOTS, BOX), jnp.int32)
    lists[2, :, :BOX] = jnp.where(late, spot, spare)
    lists[2, :, BOX:] = spare
    row = lax.broadcasted_iota(jnp.int32, (8, BOX), 0)
    bounds = [
        jnp.min(jnp.where(late, slot, SLOTS), axis=0, keepdims=True),
        jnp.max(jnp.where(late, slot + 1, 0), axis=0, keepdims=True),
        jnp.min(first_row, axis=0, keepdims=True),
        jnp.max(last_row, axis=0, keepdims=True),
    ]
    spans[...] = jnp.where(row == 0, bounds[0], jnp.where(row == 1, bounds[1], jnp.where(row == 2, bounds[2], bounds[3])))
    copies = [
        pltpu.make_async_copy(lists.at[0], spot_s, sems.at[0]),
        pltpu.make_async_copy(lists.at[1], row_s, sems.at[1]),
        pltpu.make_async_copy(lists.at[2], late_s, sems.at[2]),
        pltpu.make_async_copy(spans, span_s, sems.at[3]),
        pltpu.make_async_copy(late_rows, late_rows_s, sems.at[4]),
    ]
    for copy in copies:
        copy.start()

    def clear(i, carry):
        table[pl.ds(pl.multiple_of(i * 512, 512), 512), :] = jnp.zeros((512, BOX), jnp.float32)
        return carry

    lax.fori_loop(0, 2 * CELLS // 512, clear, 0)
    for copy in copies:
        copy.wait()

    def line(pair, j):
        return j * PAIRS + pair

    def first_pair(patch, target):
        section = jnp.dot(stacked_ref[...], patch, preferred_element_type=jnp.float32).astype(jnp.bfloat16)
        for j in range(2):
            target[j * BOX:(j + 1) * BOX, :BOX] = section[:BOX, j * BOX:(j + 1) * BOX]
            target[j * BOX:(j + 1) * BOX, BOX:] = section[BOX:, j * BOX:(j + 1) * BOX]

    def second_pair(pair, rows, source, targets):
        spectrum = jnp.dot(source[...], mixed_ref[...], preferred_element_type=jnp.float32)
        for j, target in enumerate(targets):
            pick = jnp.full((BOX, BOX), line(pair, j), jnp.int32)
            first = jnp.take_along_axis(first_ref[...], pick, axis=1)
            second = jnp.take_along_axis(second_ref[...], pick, axis=1)
            transfer = first * rows[j][0] + second * rows[j][1]
            real = transfer * spectrum[j * BOX:(j + 1) * BOX, :BOX]
            imag = transfer * spectrum[j * BOX:(j + 1) * BOX, BOX:]
            target[pl.ds(0, BOX, stride=2), :] = real
            target[pl.ds(1, BOX, stride=2), :] = imag
            kept_slices[line(pair, j), pl.ds(0, BOX, stride=2), :] = real
            kept_slices[line(pair, j), pl.ds(1, BOX, stride=2), :] = imag

    def insert(p, source):
        waiting = None
        for g in range(SLOTS // GROUP + 1):
            if g < SLOTS // GROUP:
                spots = [spot_s[g * GROUP + i, p] for i in range(GROUP)]
                sums = [table[pl.ds(spots[i], 2), :] + source[pl.ds(row_s[g * GROUP + i, p], 2), :]
                        for i in range(GROUP)]
            if waiting is not None:
                for spot, total in zip(*waiting):
                    table[pl.ds(spot, 2), :] = total
            waiting = (spots, sums)

    def insert_late(p, carry):
        @pl.when(span_s[1, p] + span_s[3, p] > 0)
        def _():
            def from_slot(i, carry):
                table[pl.ds(late_s[i, p], 2), :] += kept_slices[p, pl.ds(row_s[i, p], 2), :]
                return carry

            def from_row(i, carry):
                table[pl.ds(late_rows_s[i, p], 2), :] += kept_slices[p, pl.ds(2 * i, 2), :]
                return carry

            lax.fori_loop(span_s[0, p], span_s[1, p], from_slot, 0)
            lax.fori_loop(span_s[2, p], span_s[3, p], from_row, 0)

        return carry

    def step(i, carry):
        for h in range(2):
            tick = 2 * i + h
            patch = patches_ref[jnp.minimum(tick, PAIRS - 1)]
            pair = jnp.clip(tick - 1, 0, PAIRS - 1)
            rows = [(cos_ref[pl.ds(line(pair, j), 1), :], sin_ref[pl.ds(line(pair, j), 1), :]) for j in range(2)]
            idle = (tick < 2) | (tick >= PAIRS + 2)
            insert(jnp.where(idle, PARTICLES, tick - 2), slices_a[h])
            insert(jnp.where(idle, PARTICLES, line(tick - 2, 1)), slices_b[h])
            first_pair(patch, sides[h])
            second_pair(pair, rows, sides[1 - h], (slices_a[1 - h], slices_b[1 - h]))
        return carry

    lax.fori_loop(0, (PAIRS + 2) // 2, step, 0)
    lax.fori_loop(0, PARTICLES, insert_late, 0)

    def finish(i, carry):
        rows = pl.ds(pl.multiple_of(i * 512, 512), 512)
        out_ref[rows, :] = table[rows, :].astype(jnp.bfloat16)
        return carry

    lax.fori_loop(0, 2 * CELLS // 512, finish, 0)


def insert(patches, places, stacked, mixed, factors):
    whole = pl.BlockSpec(memory_space=pltpu.VMEM)
    return pl.pallas_call(
        insert_kernel,
        out_shape=jax.ShapeDtypeStruct((2 * CELLS, BOX), jnp.bfloat16),
        in_specs=[whole] * 8,
        out_specs=whole,
        scratch_shapes=[
            pltpu.VMEM((3, SLOTS, 2 * BOX), jnp.int32),
            pltpu.VMEM((8, BOX), jnp.int32),
            pltpu.VMEM((BOX, BOX), jnp.int32),
            pltpu.SMEM((SLOTS, 2 * BOX), jnp.int32),
            pltpu.SMEM((SLOTS, 2 * BOX), jnp.int32),
            pltpu.SMEM((SLOTS, 2 * BOX), jnp.int32),
            pltpu.SMEM((8, BOX), jnp.int32),
            pltpu.SMEM((BOX, BOX), jnp.int32),
            [pltpu.VMEM((2 * BOX, 2 * BOX), jnp.bfloat16)] * 2,
            [pltpu.VMEM((2 * BOX, BOX), jnp.float32)] * 2,
            [pltpu.VMEM((2 * BOX, BOX), jnp.float32)] * 2,
            pltpu.VMEM((PARTICLES, 2 * BOX, BOX), jnp.float32),
            pltpu.VMEM((2 * CELLS + 4 * GROUP, BOX), jnp.float32),
            pltpu.SemaphoreType.DMA((5,)),
        ],
        compiler_params=pltpu.CompilerParams(vmem_limit_bytes=46 * 2**20),
        name="insert_slices",
    )(patches, places, stacked, mixed, *factors)


ZS, XS = 8, 4
PART_ROWS = TILTS // 2 * BOX
SPOTS = 2 * CELLS


def reduce_kernel(table_ref, out_ref, own, sib, send_a, recv_a, send_b, recv_b, mid_a, mid_b, send_c, recv_c, send_d,
                  recv_d, last, own_sem, sib_send, sib_recv, a_send, a_recv, b_send, b_recv, c_send, c_recv, d_send,
                  d_recv):
    tilt, slab = lax.axis_index("tilt"), lax.axis_index("slab")
    core, z, x = tilt % 2, tilt // 2 % ZS, tilt // (2 * ZS)

    def at_z(step):
        return (x * (2 * ZS) + (z + step + ZS) % ZS * 2 + core, slab)

    def at_x(step):
        return ((x + step + XS) % XS * (2 * ZS) + z * 2 + core, slab)

    twin = (tilt + 1 - 2 * core, slab)
    barrier = pltpu.get_barrier_semaphore()
    for device in (twin, at_z(1), at_z(-1), at_x(1), at_x(-1)):
        pl.semaphore_signal(barrier, inc=1, device_id=device, device_id_type=pl.DeviceIdType.MESH)

    own_copies = []
    for q in (0, 1, 2, 3):
        copy = pltpu.make_async_copy(
            table_ref.at[pl.ds(pl.multiple_of((core * 4 + q) * PART_ROWS, PART_ROWS), PART_ROWS)],
            own.at[pl.ds(q * PART_ROWS, PART_ROWS)], own_sem.at[q])
        copy.start()
        own_copies.append(copy)
    pl.semaphore_wait(barrier, 5)

    def ring(q, n, size, here, at, sign, plain, send, recv, send_sem, recv_sem):
        half = n // 2

        def slot_of(kind, j):
            return j - 1 if kind == "major" else half + j - 1

        def copy_of(kind, j):
            slot = slot_of(kind, j)
            return pltpu.make_async_remote_copy(
                src_ref=send.at[q % 2, slot], dst_ref=recv.at[q % 2, slot],
                send_sem=send_sem.at[q % 2, slot], recv_sem=recv_sem.at[q % 2, slot],
                device_id=at(sign if kind == "major" else -sign), device_id_type=pl.DeviceIdType.MESH)

        def owner_of(kind, j):
            shift = sign * (half + 1 - j) if kind == "major" else -sign * (half - j)
            return (here + shift + n) % n

        def step(kind, j):
            o = owner_of(kind, j)
            slot = slot_of(kind, j)
            if j > 1:
                copy_of(kind, j - 1).wait_recv()

            def tile(i, carry):
                rows = pl.ds(pl.multiple_of(i * BOX, BOX), BOX)
                total = plain(o, i)
                if j > 1:
                    total = total + recv[q % 2, slot - 1, rows, :].astype(jnp.float32)
                send[q % 2, slot, rows, :] = total.astype(jnp.bfloat16)
                return carry

            lax.fori_loop(0, size // BOX, tile, 0)
            copy_of(kind, j).start()

        def final(store):
            copy_of("major", half).wait_recv()
            copy_of("minor", half - 1).wait_recv()

            def tile(i, carry):
                rows = pl.ds(pl.multiple_of(i * BOX, BOX), BOX)
                store(i, plain(here, i) + recv[q % 2, half - 1, rows, :].astype(jnp.float32)
                      + recv[q % 2, n - 2, rows, :].astype(jnp.float32))
                return carry

            lax.fori_loop(0, size // BOX, tile, 0)

        def drain():
            for kind, steps in (("major", half), ("minor", half - 1)):
                for j in range(1, steps + 1):
                    copy_of(kind, j).wait_send()

        return step, final, drain, owner_of

    A, B = XS * BOX, ZS * BOX
    twin_copies = {}

    def twin_copy(q, kind, j, o, size):
        index = len(twin_copies)
        rows = pl.multiple_of(q * PART_ROWS + o * size, size)
        copy = pltpu.make_async_remote_copy(
            src_ref=table_ref.at[pl.ds(pl.multiple_of((1 - core) * 4 * PART_ROWS + rows, size), size)],
            dst_ref=sib.at[pl.ds(rows, size)], send_sem=sib_send.at[index], recv_sem=sib_recv.at[index],
            device_id=twin, device_id_type=pl.DeviceIdType.MESH)
        copy.start()
        twin_copies[q, kind, j] = copy

    def plain_first(q, size):
        def plain(o, i):
            rows = pl.ds(pl.multiple_of(q * PART_ROWS + o * size + i * BOX, BOX), BOX)
            return own[rows, :].astype(jnp.float32) + sib[rows, :].astype(jnp.float32)
        return plain

    first, second = [], []
    for q in range(4):
        sign = 1 if q % 2 == 0 else -1
        if q < 2:
            first.append(ring(q, ZS, A, z, at_z, sign, plain_first(q, A), send_a, recv_a, a_send, a_recv))
            second.append(ring(q, XS, BOX, x, at_x, sign,
                               lambda o, i, q=q: mid_a[q % 2, pl.ds(pl.multiple_of(o * BOX, BOX), BOX), :],
                               send_c, recv_c, c_send, c_recv))
        else:
            first.append(ring(q, XS, B, x, at_x, sign, plain_first(q, B), send_b, recv_b, b_send, b_recv))
            second.append(ring(q, ZS, BOX, z, at_z, sign,
                               lambda o, i, q=q: mid_b[q % 2, pl.ds(pl.multiple_of(o * BOX, BOX), BOX), :],
                               send_d, recv_d, d_send, d_recv))

    order = []
    for kind in ("major", "minor"):
        order += [(0, kind, 1), (1, kind, 1)]
    order += [(2, "major", 1), (3, "major", 1), (2, "minor", 1), (3, "minor", 1)]
    order += [(0, "major", 2), (1, "major", 2), (0, "minor", 2), (1, "minor", 2)]
    order += [(2, "major", 2), (3, "major", 2)]
    for j in (3,):
        order += [(0, "major", j), (1, "major", j), (0, "minor", j), (1, "minor", j)]
    order += [(0, "major", 4), (1, "major", 4)]
    order += [(2, "own", 0), (3, "own", 0), (0, "own", 0), (1, "own", 0)]

    for q, kind, j in order:
        o = (z if q < 2 else x) if kind == "own" else first[q][3](kind, j)
        twin_copy(q, kind, j, o, A if q < 2 else B)

    waited = set()
    for q, kind, j in order:
        if q not in waited:
            own_copies[q].wait()
            waited.add(q)
        twin_copies[q, kind, j].wait_recv()
        if kind != "own":
            first[q][0](kind, j)
        else:
            def store(i, value, q=q):
                mid = mid_a if q < 2 else mid_b
                mid[q % 2, pl.ds(pl.multiple_of(i * BOX, BOX), BOX), :] = value
            first[q][1](store)
            second[q][0]("major", 1)
            second[q][0]("minor", 1)
    for j in (2, 3, 4):
        for q in (2, 3):
            second[q][0]("major", j)
            if j < 4:
                second[q][0]("minor", j)
        if j == 2:
            for q in (0, 1):
                second[q][0]("major", j)

    def store_last(i, value):
        last[...] = value

    for q in (0, 1, 2, 3):
        second[q][1](store_last)
        out_ref[0, q] = last[pl.ds(0, 64, stride=2), :]
        out_ref[1, q] = last[pl.ds(1, 64, stride=2), :]
    for q in range(4):
        first[q][2]()
        second[q][2]()
    for copy in twin_copies.values():
        copy.wait_send()


def reduce_table(table):
    dma = pltpu.SemaphoreType.DMA
    A, B = XS * BOX, ZS * BOX
    return pl.pallas_call(
        reduce_kernel,
        out_shape=jax.ShapeDtypeStruct((2, HALFMAPS, 64, BOX), jnp.float32),
        in_specs=[pl.BlockSpec(memory_space=pl.ANY)],
        out_specs=pl.BlockSpec(memory_space=pltpu.VMEM),
        scratch_shapes=[
            pltpu.VMEM((SPOTS // 2, BOX), jnp.bfloat16),
            pltpu.VMEM((SPOTS // 2, BOX), jnp.bfloat16),
            pltpu.VMEM((2, ZS - 1, A, BOX), jnp.bfloat16),
            pltpu.VMEM((2, ZS - 1, A, BOX), jnp.bfloat16),
            pltpu.VMEM((2, XS - 1, B, BOX), jnp.bfloat16),
            pltpu.VMEM((2, XS - 1, B, BOX), jnp.bfloat16),
            pltpu.VMEM((2, A, BOX), jnp.float32),
            pltpu.VMEM((2, B, BOX), jnp.float32),
            pltpu.VMEM((2, XS - 1, BOX, BOX), jnp.bfloat16),
            pltpu.VMEM((2, XS - 1, BOX, BOX), jnp.bfloat16),
            pltpu.VMEM((2, ZS - 1, BOX, BOX), jnp.bfloat16),
            pltpu.VMEM((2, ZS - 1, BOX, BOX), jnp.bfloat16),
            pltpu.VMEM((BOX, BOX), jnp.float32),
            dma((4,)), dma((24,)), dma((24,)),
            dma((2, ZS - 1)), dma((2, ZS - 1)), dma((2, XS - 1)), dma((2, XS - 1)),
            dma((2, XS - 1)), dma((2, XS - 1)), dma((2, ZS - 1)), dma((2, ZS - 1)),
        ],
        compiler_params=pltpu.CompilerParams(
            collective_id=0, has_side_effects=True, vmem_limit_bytes=60 * 2**20),
        name="reduce_table",
    )(table)


def tables():
    cos_table, sin_table = fourier_tables(BOX)
    stacked = jnp.concatenate([cos_table, sin_table], 0)
    mixed = jnp.concatenate([
        jnp.concatenate([cos_table.T, sin_table.T], 1),
        jnp.concatenate([-sin_table.T, cos_table.T], 1)], 0)
    return stacked, mixed


def places_of(rows, labels, slab_index, slab_count):
    owner, offset = rows // 64, rows % 64
    tilt = owner // slab_count
    core, z, x = tilt % 2, tilt // 2 % ZS, tilt // (2 * ZS)
    label = labels
    chip = jnp.where(label < 2, z * XS + x, x * ZS + z)
    place = 2 * (((core * HALFMAPS + label) * (TILTS // 2) + chip) * 64 + offset)
    return jnp.where(owner % slab_count == slab_index, place, -1)


def body(tilt_images, corners, visible, defocus, labels, row_owner, row_offset):
    misc = jnp.stack([defocus.reshape(BOX), jnp.repeat(labels.astype(jnp.float32), TILTS)])
    patches, places, *factors = swap(
        corners[:, 0], visible, tilt_images[0], row_owner[..., 0], row_offset, misc)
    stacked, mixed = tables()
    return reduce_table(insert(patches, places, stacked, mixed, factors))


def solution(mesh):
    return jax.shard_map(
        body,
        mesh=mesh,
        in_specs=(
            P("tilt", None, None),
            P(None, "tilt", None),
            P("tilt", None),
            P("tilt", None),
            P("tilt"),
            P("tilt", None, None, None),
            P("tilt", None, None),
        ),
        out_specs=P(None, None, ("tilt", "slab"), None),
        check_vma=False,
    )
```

```python
import math

import jax
import jax.numpy as jnp
import numpy as np
from jax import lax
from jax.experimental import pallas as pl
from jax.experimental.pallas import tpu as pltpu
from jax.sharding import PartitionSpec as P

BOX = 128
HALFMAPS = 4
AMPLITUDE = 0.1
TILTS = 64
PARTICLES = 128
CELLS = TILTS * HALFMAPS * 64
GROUP = 8
PAIRS = PARTICLES // 2
WINDOW = 2 * GROUP
SLOTS = 64
CUTS = 8
CHUNK = 4096


def fourier_tables(width):
    positions = jnp.arange(width, dtype=jnp.int32)
    frequency = positions - width // 2
    phase_index = frequency[:, None] * positions[None, :] % width
    angles = phase_index.astype(jnp.float32) * (2.0 * jnp.pi / width)
    return (jnp.cos(angles).astype(jnp.bfloat16), (-jnp.sin(angles)).astype(jnp.bfloat16))


def transfer_factors(defocus, column):
    frequency = (column - BOX // 2).astype(jnp.float32) / BOX
    angle = jnp.pi * defocus * (frequency * frequency)
    cos_part, sin_part = jnp.cos(angle), jnp.sin(angle)
    main = math.sqrt(1.0 - AMPLITUDE * AMPLITUDE)
    first = -(main * sin_part + AMPLITUDE * cos_part) / BOX
    second = -(main * cos_part - AMPLITUDE * sin_part) / BOX
    return first, second, cos_part, sin_part


def swap_kernel(corner_hbm, seen_hbm, image_hbm, owner_hbm, offset_hbm, defocus_hbm, label_hbm, patches_hbm, places_ref,
                first_ref, second_ref, cos_ref, sin_ref, corner_ref, seen_ref, image_ref, owner_ref, offset_ref,
                defocus_ref, label_ref, left, right, outbox, inbox, patches_ref, send_sem, recv_sem, load_sem, store_sem):
    loads = [
        pltpu.make_async_copy(source, target, load_sem.at[i]) for i, (source, target) in enumerate((
            (owner_hbm, owner_ref), (offset_hbm, offset_ref), (defocus_hbm, defocus_ref), (label_hbm, label_ref),
            (image_hbm, image_ref), (corner_hbm, corner_ref), (seen_hbm, seen_ref)))]
    for load in loads:
        load.start()
    tilt, slab = lax.axis_index("tilt"), lax.axis_index("slab")
    barrier = pltpu.get_barrier_semaphore()

    def peer(d):
        return (tilt + d) % TILTS

    def greet(d, carry):
        pl.semaphore_signal(barrier, inc=1, device_id=(peer(d), slab), device_id_type=pl.DeviceIdType.MESH)
        return carry

    lax.fori_loop(1, TILTS, greet, 0)
    for load in loads[:4]:
        load.wait()
    column = lax.broadcasted_iota(jnp.int32, (TILTS, BOX), 1)
    for j in range(2):
        outbox[:, j, :] = (owner_ref[j] * 64 + offset_ref[j]).astype(jnp.float32)
        outbox[:, 2, j * TILTS:(j + 1) * TILTS] = jnp.broadcast_to(defocus_ref[j:j + 1, :], (TILTS, TILTS))
    outbox[:, 3, :] = jnp.where(column < TILTS, label_ref[0, 0], label_ref[0, 1]).astype(jnp.float32)
    pl.semaphore_wait(barrier, TILTS - 1)

    def message(to, origin):
        return pltpu.make_async_remote_copy(
            src_ref=outbox.at[to], dst_ref=inbox.at[origin], send_sem=send_sem.at[to], recv_sem=recv_sem.at[origin],
            device_id=(to, slab), device_id_type=pl.DeviceIdType.MESH)

    def send(d, carry):
        message(peer(d), tilt).start()
        return carry

    lax.fori_loop(1, TILTS, send, 0)
    inbox[tilt] = outbox[tilt]
    for load in loads[4:]:
        load.wait()
    left[...] = image_ref[:, :BOX].astype(jnp.float32)
    right[...] = image_ref[:, BOX:].astype(jnp.float32)
    lane = lax.broadcasted_iota(jnp.int32, (BOX, BOX), 1)

    def window(p):
        row, col = corner_ref[0, p], corner_ref[1, p]
        a = left[pl.ds(row, BOX), :]
        b = right[pl.ds(row, BOX), :]
        cut = pltpu.roll(jnp.where(lane >= col, a, b), (BOX - col) % BOX, axis=1)
        average = jnp.sum(jnp.sum(cut, axis=0, keepdims=True), axis=1, keepdims=True) * (1.0 / (BOX * BOX))
        centered = cut - average
        variance = jnp.sum(
            jnp.sum(centered * centered, axis=0, keepdims=True), axis=1, keepdims=True) * (1.0 / (BOX * BOX))
        scale = lax.rsqrt(variance + 1e-05) * seen_ref[0, p].astype(jnp.float32)
        return (centered * scale).astype(jnp.bfloat16)

    def leave(i):
        pairs = pl.ds(CUTS // 2 * i, CUTS // 2)
        return pltpu.make_async_copy(patches_ref.at[pairs], patches_hbm.at[pairs], store_sem.at[i])

    def cut_pairs(i, carry):
        windows = [window(CUTS * i + j) for j in range(CUTS)]
        for j, patch in enumerate(windows):
            patches_ref[CUTS // 2 * i + j // 2, :, j % 2 * BOX:(j % 2 + 1) * BOX] = patch
        leave(i).start()
        return carry

    lax.fori_loop(0, PARTICLES // CUTS, cut_pairs, 0)

    def receive(d, carry):
        message(tilt, peer(d)).wait_recv()
        return carry

    lax.fori_loop(1, TILTS, receive, 0)

    rows = jnp.concatenate([inbox[:, 0, :], inbox[:, 1, :]], axis=0).astype(jnp.int32)
    misc = jnp.concatenate([inbox[:, 2, :]] * 2, axis=0)
    line = lax.broadcasted_iota(jnp.int32, (BOX, BOX), 0)
    mine = jnp.where(lane == jnp.where(line < TILTS, tilt, TILTS + tilt), misc, 0.0)
    defocus = jnp.sum(mine, axis=1, keepdims=True)
    labels = jnp.concatenate([inbox[:, 3, :]] * 2, axis=0)
    label = jnp.sum(jnp.where(lane == jnp.where(line < TILTS, 0, TILTS), labels, 0.0), axis=1, keepdims=True)
    places_ref[...] = places_of(rows, label.astype(jnp.int32), slab, lax.axis_size("slab")).T
    first, second, cos_part, sin_part = transfer_factors(defocus, lane)
    first_ref[...] = first.T
    second_ref[...] = second.T
    cos_ref[...] = cos_part
    sin_ref[...] = sin_part

    def sent(d, carry):
        message(peer(d), tilt).wait_send()
        return carry

    lax.fori_loop(1, TILTS, sent, 0)

    def left_all(i, carry):
        leave(i).wait()
        return carry

    lax.fori_loop(0, PARTICLES // CUTS, left_all, 0)


def swap(*operands):
    whole = pl.BlockSpec(memory_space=pltpu.VMEM)
    square = jax.ShapeDtypeStruct((BOX, BOX), jnp.float32)
    return pl.pallas_call(
        swap_kernel,
        out_shape=[jax.ShapeDtypeStruct((PAIRS, BOX, 2 * BOX), jnp.bfloat16),
                   jax.ShapeDtypeStruct((BOX, BOX), jnp.int32)] + [square] * 4,
        in_specs=[pl.BlockSpec(memory_space=pltpu.HBM)] * 7,
        out_specs=[pl.BlockSpec(memory_space=pltpu.HBM)] + [whole] * 5,
        scratch_shapes=[
            pltpu.SMEM((2, BOX), jnp.int32),
            pltpu.SMEM((1, BOX), jnp.int32),
            pltpu.VMEM((256, 256), jnp.bfloat16),
            pltpu.VMEM((2, TILTS, BOX), jnp.int32),
            pltpu.VMEM((2, TILTS, BOX), jnp.int32),
            pltpu.VMEM((2, TILTS), jnp.float32),
            pltpu.SMEM((1, 2), jnp.int32),
            pltpu.VMEM((256, BOX), jnp.float32),
            pltpu.VMEM((256, BOX), jnp.float32),
            pltpu.VMEM((TILTS, 4, BOX), jnp.float32),
            pltpu.VMEM((TILTS, 4, BOX), jnp.float32),
            pltpu.VMEM((PAIRS, BOX, 2 * BOX), jnp.bfloat16),
            pltpu.SemaphoreType.DMA((TILTS,)),
            pltpu.SemaphoreType.DMA((TILTS,)),
            pltpu.SemaphoreType.DMA((7,)),
            pltpu.SemaphoreType.DMA((PARTICLES // CUTS,)),
        ],
        compiler_params=pltpu.CompilerParams(
            collective_id=1, has_side_effects=True, vmem_limit_bytes=62 * 2**20),
        name="swap_rows",
    )(*operands)


def insert_kernel(patches_hbm, places_ref, stacked_ref, mixed_ref, first_ref, second_ref, cos_ref, sin_ref, out_ref,
                  lists, spans, late_rows, spot_s, row_s, late_s, span_s, late_rows_s, sides, slices_a, slices_b, staged, kept_slices, table, patches_ref, sems):
    fetch = pltpu.make_async_copy(patches_hbm, patches_ref, sems.at[5])
    fetch.start()
    entry = lax.broadcasted_iota(jnp.int32, (8, BOX), 0)
    rank = jnp.zeros((8, BOX), jnp.int32)
    spots = [2 * CELLS + 2 * ((8 * s + entry) % (2 * GROUP)) for s in range(SLOTS // 8)]
    spare = jnp.concatenate(spots, axis=0)
    sources = [jnp.zeros((8, BOX), jnp.int32) for _ in range(SLOTS // 8)]
    first_row, last_row = jnp.full((8, BOX), BOX, jnp.int32), jnp.zeros((8, BOX), jnp.int32)
    for j in range(BOX // 8):
        place = places_ref[8 * j:8 * j + 8, :]
        kept = place >= 0
        for s in range(SLOTS // 8):
            hit = kept & (rank == s)
            spots[s] = jnp.where(hit, place, spots[s])
            sources[s] = jnp.where(hit, 2 * (8 * j + entry), sources[s])
        over = kept & (rank >= SLOTS // 8)
        late_rows[8 * j:8 * j + 8, :] = jnp.where(over, place, 2 * CELLS)
        first_row = jnp.minimum(first_row, jnp.where(over, 8 * j + entry, BOX))
        last_row = jnp.maximum(last_row, jnp.where(over, 8 * j + entry + 1, 0))
        rank = rank + jnp.where(kept, 1, 0)
    spot = jnp.concatenate(spots, axis=0)
    slot = lax.broadcasted_iota(jnp.int32, (SLOTS, BOX), 0)
    late = jnp.zeros((SLOTS, BOX), jnp.bool_)
    for d in range(1, WINDOW):
        late = late | ((pltpu.roll(spot, SLOTS - d, axis=0) == spot) & (slot < SLOTS - d))
    lists[0, :, :BOX] = jnp.where(late, spare, spot)
    lists[0, :, BOX:] = spare
    lists[1, :, :BOX] = jnp.concatenate(sources, axis=0)
    lists[1, :, BOX:] = jnp.zeros((SLOTS, BOX), jnp.int32)
    lists[2, :, :BOX] = jnp.where(late, spot, spare)
    lists[2, :, BOX:] = spare
    row = lax.broadcasted_iota(jnp.int32, (8, BOX), 0)
    bounds = [
        jnp.min(jnp.where(late, slot, SLOTS), axis=0, keepdims=True),
        jnp.max(jnp.where(late, slot + 1, 0), axis=0, keepdims=True),
        jnp.min(first_row, axis=0, keepdims=True),
        jnp.max(last_row, axis=0, keepdims=True),
    ]
    spans[...] = jnp.where(row == 0, bounds[0], jnp.where(row == 1, bounds[1], jnp.where(row == 2, bounds[2], bounds[3])))
    amount = bounds[1] + bounds[3]
    for shift in (1, 2, 4, 8):
        amount = amount + pltpu.roll(amount, BOX - shift, axis=1)
    spans[4:5, :] = amount
    copies = [
        pltpu.make_async_copy(lists.at[0], spot_s, sems.at[0]),
        pltpu.make_async_copy(lists.at[1], row_s, sems.at[1]),
        pltpu.make_async_copy(lists.at[2], late_s, sems.at[2]),
        pltpu.make_async_copy(spans, span_s, sems.at[3]),
        pltpu.make_async_copy(late_rows, late_rows_s, sems.at[4]),
    ]
    for copy in copies:
        copy.start()

    def clear(i, carry):
        table[pl.ds(pl.multiple_of(i * 512, 512), 512), :] = jnp.zeros((512, BOX), jnp.float32)
        return carry

    lax.fori_loop(0, 2 * CELLS // 512, clear, 0)
    for copy in copies:
        copy.wait()

    def line(pair, j):
        return j * PAIRS + pair

    def first_pair(patch, target):
        section = jnp.dot(stacked_ref[...], patch, preferred_element_type=jnp.float32).astype(jnp.bfloat16)
        for j in range(2):
            target[j * BOX:(j + 1) * BOX, :BOX] = section[:BOX, j * BOX:(j + 1) * BOX]
            target[j * BOX:(j + 1) * BOX, BOX:] = section[BOX:, j * BOX:(j + 1) * BOX]

    def second_pair(pair, rows, source, targets):
        spectrum = jnp.dot(source[...], mixed_ref[...], preferred_element_type=jnp.float32)
        for j, target in enumerate(targets):
            pick = jnp.full((BOX, BOX), line(pair, j), jnp.int32)
            first = jnp.take_along_axis(first_ref[...], pick, axis=1)
            second = jnp.take_along_axis(second_ref[...], pick, axis=1)
            transfer = first * rows[j][0] + second * rows[j][1]
            real = transfer * spectrum[j * BOX:(j + 1) * BOX, :BOX]
            imag = transfer * spectrum[j * BOX:(j + 1) * BOX, BOX:]
            target[pl.ds(0, BOX, stride=2), :] = real
            target[pl.ds(1, BOX, stride=2), :] = imag
            kept_slices[line(pair, j), pl.ds(0, BOX, stride=2), :] = real
            kept_slices[line(pair, j), pl.ds(1, BOX, stride=2), :] = imag

    def insert(p, source):
        waiting = None
        for g in range(SLOTS // GROUP + 1):
            if g < SLOTS // GROUP:
                spots = [spot_s[g * GROUP + i, p] for i in range(GROUP)]
                sums = [table[pl.ds(spots[i], 2), :] + source[pl.ds(row_s[g * GROUP + i, p], 2), :]
                        for i in range(GROUP)]
            if waiting is not None:
                for spot, total in zip(*waiting):
                    table[pl.ds(spot, 2), :] = total
            waiting = (spots, sums)

    def insert_late(p, carry):
        @pl.when(span_s[1, p] + span_s[3, p] > 0)
        def _():
            def from_slot(i, carry):
                table[pl.ds(late_s[i, p], 2), :] += kept_slices[p, pl.ds(row_s[i, p], 2), :]
                return carry

            def from_row(i, carry):
                table[pl.ds(late_rows_s[i, p], 2), :] += kept_slices[p, pl.ds(2 * i, 2), :]
                return carry

            lax.fori_loop(span_s[0, p], span_s[1, p], from_slot, 0)
            lax.fori_loop(span_s[2, p], span_s[3, p], from_row, 0)

        return carry

    def step(i, carry):
        for h in range(2):
            tick = 2 * i + h
            patch = patches_ref[jnp.minimum(tick, PAIRS - 1)]
            pair = jnp.clip(tick - 1, 0, PAIRS - 1)
            rows = [(cos_ref[pl.ds(line(pair, j), 1), :], sin_ref[pl.ds(line(pair, j), 1), :]) for j in range(2)]
            idle = (tick < 2) | (tick >= PAIRS + 2)
            insert(jnp.where(idle, PARTICLES, tick - 2), slices_a[h])
            insert(jnp.where(idle, PARTICLES, line(tick - 2, 1)), slices_b[h])
            first_pair(patch, sides[h])
            second_pair(pair, rows, sides[1 - h], (slices_a[1 - h], slices_b[1 - h]))
        return carry

    fetch.wait()
    lax.fori_loop(0, (PAIRS + 2) // 2, step, 0)
    for block in range(PARTICLES // 16):
        @pl.when(span_s[4, 16 * block] > 0)
        def _():
            lax.fori_loop(16 * block, 16 * block + 16, insert_late, 0)


    def leave(c):
        return pltpu.make_async_copy(
            staged.at[c % 2], out_ref.at[pl.ds(c * CHUNK, CHUNK)], sems.at[c % 2])

    for c in range(2 * CELLS // CHUNK):
        if c >= 2:
            leave(c - 2).wait()

        def convert(i, carry):
            rows = pl.ds(pl.multiple_of(i * 512, 512), 512)
            staged[c % 2, rows, :] = table[pl.ds(pl.multiple_of(c * CHUNK + i * 512, 512), 512), :].astype(jnp.bfloat16)
            return carry

        lax.fori_loop(0, CHUNK // 512, convert, 0)
        leave(c).start()
    for c in range(2 * CELLS // CHUNK - 2, 2 * CELLS // CHUNK):
        leave(c).wait()


def insert(patches, places, stacked, mixed, factors):
    whole = pl.BlockSpec(memory_space=pltpu.VMEM)
    return pl.pallas_call(
        insert_kernel,
        out_shape=jax.ShapeDtypeStruct((2 * CELLS, BOX), jnp.bfloat16),
        in_specs=[pl.BlockSpec(memory_space=pltpu.HBM)] + [whole] * 7,
        out_specs=pl.BlockSpec(memory_space=pltpu.HBM),
        scratch_shapes=[
            pltpu.VMEM((3, SLOTS, 2 * BOX), jnp.int32),
            pltpu.VMEM((8, BOX), jnp.int32),
            pltpu.VMEM((BOX, BOX), jnp.int32),
            pltpu.SMEM((SLOTS, 2 * BOX), jnp.int32),
            pltpu.SMEM((SLOTS, 2 * BOX), jnp.int32),
            pltpu.SMEM((SLOTS, 2 * BOX), jnp.int32),
            pltpu.SMEM((8, BOX), jnp.int32),
            pltpu.SMEM((BOX, BOX), jnp.int32),
            [pltpu.VMEM((2 * BOX, 2 * BOX), jnp.bfloat16)] * 2,
            [pltpu.VMEM((2 * BOX, BOX), jnp.float32)] * 2,
            [pltpu.VMEM((2 * BOX, BOX), jnp.float32)] * 2,
            pltpu.VMEM((2, CHUNK, BOX), jnp.bfloat16),
            pltpu.VMEM((PARTICLES, 2 * BOX, BOX), jnp.float32),
            pltpu.VMEM((2 * CELLS + 4 * GROUP, BOX), jnp.float32),
            pltpu.VMEM((PAIRS, BOX, 2 * BOX), jnp.bfloat16),
            pltpu.SemaphoreType.DMA((6,)),
        ],
        compiler_params=pltpu.CompilerParams(vmem_limit_bytes=62 * 2**20),
        name="insert_slices",
    )(patches, places, stacked, mixed, *factors)


ZS, XS = 8, 4
PART_ROWS = TILTS // 2 * BOX
SPOTS = 2 * CELLS


def reduce_kernel(table_ref, out_ref, own, sib, send_a, recv_a, send_b, recv_b, mid_a, mid_b, send_c, recv_c, send_d,
                  recv_d, last, own_sem, sib_send, sib_recv, a_send, a_recv, b_send, b_recv, c_send, c_recv, d_send,
                  d_recv):
    tilt, slab = lax.axis_index("tilt"), lax.axis_index("slab")
    core, z, x = tilt % 2, tilt // 2 % ZS, tilt // (2 * ZS)

    def at_z(step):
        return (x * (2 * ZS) + (z + step + ZS) % ZS * 2 + core, slab)

    def at_x(step):
        return ((x + step + XS) % XS * (2 * ZS) + z * 2 + core, slab)

    twin = (tilt + 1 - 2 * core, slab)
    barrier = pltpu.get_barrier_semaphore()
    for device in (twin, at_z(1), at_z(-1), at_x(1), at_x(-1)):
        pl.semaphore_signal(barrier, inc=1, device_id=device, device_id_type=pl.DeviceIdType.MESH)

    own_copies = []
    for q in (0, 1, 2, 3):
        copy = pltpu.make_async_copy(
            table_ref.at[pl.ds(pl.multiple_of((core * 4 + q) * PART_ROWS, PART_ROWS), PART_ROWS)],
            own.at[pl.ds(q * PART_ROWS, PART_ROWS)], own_sem.at[q])
        copy.start()
        own_copies.append(copy)
    pl.semaphore_wait(barrier, 5)

    def ring(q, n, size, here, at, sign, plain, send, recv, send_sem, recv_sem):
        half = n // 2

        def slot_of(kind, j):
            return j - 1 if kind == "major" else half + j - 1

        def copy_of(kind, j):
            slot = slot_of(kind, j)
            return pltpu.make_async_remote_copy(
                src_ref=send.at[q % 2, slot], dst_ref=recv.at[q % 2, slot],
                send_sem=send_sem.at[q % 2, slot], recv_sem=recv_sem.at[q % 2, slot],
                device_id=at(sign if kind == "major" else -sign), device_id_type=pl.DeviceIdType.MESH)

        def owner_of(kind, j):
            shift = sign * (half + 1 - j) if kind == "major" else -sign * (half - j)
            return (here + shift + n) % n

        def step(kind, j):
            o = owner_of(kind, j)
            slot = slot_of(kind, j)
            if j > 1:
                copy_of(kind, j - 1).wait_recv()

            def tile(i, carry):
                rows = pl.ds(pl.multiple_of(i * BOX, BOX), BOX)
                total = plain(o, i)
                if j > 1:
                    total = total + recv[q % 2, slot - 1, rows, :].astype(jnp.float32)
                send[q % 2, slot, rows, :] = total.astype(jnp.bfloat16)
                return carry

            lax.fori_loop(0, size // BOX, tile, 0)
            copy_of(kind, j).start()

        def final(store):
            copy_of("major", half).wait_recv()
            copy_of("minor", half - 1).wait_recv()

            def tile(i, carry):
                rows = pl.ds(pl.multiple_of(i * BOX, BOX), BOX)
                store(i, plain(here, i) + recv[q % 2, half - 1, rows, :].astype(jnp.float32)
                      + recv[q % 2, n - 2, rows, :].astype(jnp.float32))
                return carry

            lax.fori_loop(0, size // BOX, tile, 0)

        def drain():
            for kind, steps in (("major", half), ("minor", half - 1)):
                for j in range(1, steps + 1):
                    copy_of(kind, j).wait_send()

        return step, final, drain, owner_of

    A, B = XS * BOX, ZS * BOX
    twin_copies = {}

    def twin_copy(q, kind, j, o, size):
        index = len(twin_copies)
        rows = pl.multiple_of(q * PART_ROWS + o * size, size)
        copy = pltpu.make_async_remote_copy(
            src_ref=table_ref.at[pl.ds(pl.multiple_of((1 - core) * 4 * PART_ROWS + rows, size), size)],
            dst_ref=sib.at[pl.ds(rows, size)], send_sem=sib_send.at[index], recv_sem=sib_recv.at[index],
            device_id=twin, device_id_type=pl.DeviceIdType.MESH)
        copy.start()
        twin_copies[q, kind, j] = copy

    def plain_first(q, size):
        def plain(o, i):
            rows = pl.ds(pl.multiple_of(q * PART_ROWS + o * size + i * BOX, BOX), BOX)
            return own[rows, :].astype(jnp.float32) + sib[rows, :].astype(jnp.float32)
        return plain

    first, second = [], []
    for q in range(4):
        sign = 1 if q % 2 == 0 else -1
        if q < 2:
            first.append(ring(q, ZS, A, z, at_z, sign, plain_first(q, A), send_a, recv_a, a_send, a_recv))
            second.append(ring(q, XS, BOX, x, at_x, sign,
                               lambda o, i, q=q: mid_a[q % 2, pl.ds(pl.multiple_of(o * BOX, BOX), BOX), :],
                               send_c, recv_c, c_send, c_recv))
        else:
            first.append(ring(q, XS, B, x, at_x, sign, plain_first(q, B), send_b, recv_b, b_send, b_recv))
            second.append(ring(q, ZS, BOX, z, at_z, sign,
                               lambda o, i, q=q: mid_b[q % 2, pl.ds(pl.multiple_of(o * BOX, BOX), BOX), :],
                               send_d, recv_d, d_send, d_recv))

    order = []
    for kind in ("major", "minor"):
        order += [(0, kind, 1), (1, kind, 1)]
    order += [(2, "major", 1), (3, "major", 1), (2, "minor", 1), (3, "minor", 1)]
    order += [(0, "major", 2), (1, "major", 2), (0, "minor", 2), (1, "minor", 2)]
    order += [(2, "major", 2), (3, "major", 2)]
    for j in (3,):
        order += [(0, "major", j), (1, "major", j), (0, "minor", j), (1, "minor", j)]
    order += [(0, "major", 4), (1, "major", 4)]
    order += [(2, "own", 0), (3, "own", 0), (0, "own", 0), (1, "own", 0)]

    for q, kind, j in order:
        o = (z if q < 2 else x) if kind == "own" else first[q][3](kind, j)
        twin_copy(q, kind, j, o, A if q < 2 else B)

    waited = set()
    for q, kind, j in order:
        if q not in waited:
            own_copies[q].wait()
            waited.add(q)
        twin_copies[q, kind, j].wait_recv()
        if kind != "own":
            first[q][0](kind, j)
        else:
            def store(i, value, q=q):
                mid = mid_a if q < 2 else mid_b
                mid[q % 2, pl.ds(pl.multiple_of(i * BOX, BOX), BOX), :] = value
            first[q][1](store)
            second[q][0]("major", 1)
            second[q][0]("minor", 1)
    for j in (2, 3, 4):
        for q in (2, 3):
            second[q][0]("major", j)
            if j < 4:
                second[q][0]("minor", j)
        if j == 2:
            for q in (0, 1):
                second[q][0]("major", j)

    def store_last(i, value):
        last[...] = value

    for q in (0, 1, 2, 3):
        second[q][1](store_last)
        out_ref[0, q] = last[pl.ds(0, 64, stride=2), :]
        out_ref[1, q] = last[pl.ds(1, 64, stride=2), :]
    for q in range(4):
        first[q][2]()
        second[q][2]()
    for copy in twin_copies.values():
        copy.wait_send()


def reduce_table(table):
    dma = pltpu.SemaphoreType.DMA
    A, B = XS * BOX, ZS * BOX
    return pl.pallas_call(
        reduce_kernel,
        out_shape=jax.ShapeDtypeStruct((2, HALFMAPS, 64, BOX), jnp.float32),
        in_specs=[pl.BlockSpec(memory_space=pl.ANY)],
        out_specs=pl.BlockSpec(memory_space=pltpu.VMEM),
        scratch_shapes=[
            pltpu.VMEM((SPOTS // 2, BOX), jnp.bfloat16),
            pltpu.VMEM((SPOTS // 2, BOX), jnp.bfloat16),
            pltpu.VMEM((2, ZS - 1, A, BOX), jnp.bfloat16),
            pltpu.VMEM((2, ZS - 1, A, BOX), jnp.bfloat16),
            pltpu.VMEM((2, XS - 1, B, BOX), jnp.bfloat16),
            pltpu.VMEM((2, XS - 1, B, BOX), jnp.bfloat16),
            pltpu.VMEM((2, A, BOX), jnp.float32),
            pltpu.VMEM((2, B, BOX), jnp.float32),
            pltpu.VMEM((2, XS - 1, BOX, BOX), jnp.bfloat16),
            pltpu.VMEM((2, XS - 1, BOX, BOX), jnp.bfloat16),
            pltpu.VMEM((2, ZS - 1, BOX, BOX), jnp.bfloat16),
            pltpu.VMEM((2, ZS - 1, BOX, BOX), jnp.bfloat16),
            pltpu.VMEM((BOX, BOX), jnp.float32),
            dma((4,)), dma((24,)), dma((24,)),
            dma((2, ZS - 1)), dma((2, ZS - 1)), dma((2, XS - 1)), dma((2, XS - 1)),
            dma((2, XS - 1)), dma((2, XS - 1)), dma((2, ZS - 1)), dma((2, ZS - 1)),
        ],
        compiler_params=pltpu.CompilerParams(
            collective_id=0, has_side_effects=True, vmem_limit_bytes=57 * 2**20),
        name="reduce_table",
    )(table)


def tables():
    cos_table, sin_table = fourier_tables(BOX)
    stacked = jnp.concatenate([cos_table, sin_table], 0)
    mixed = jnp.concatenate([
        jnp.concatenate([cos_table.T, sin_table.T], 1),
        jnp.concatenate([-sin_table.T, cos_table.T], 1)], 0)
    return stacked, mixed


def places_of(rows, labels, slab_index, slab_count):
    owner, offset = rows // 64, rows % 64
    tilt = owner // slab_count
    core, z, x = tilt % 2, tilt // 2 % ZS, tilt // (2 * ZS)
    label = labels
    chip = jnp.where(label < 2, z * XS + x, x * ZS + z)
    place = 2 * (((core * HALFMAPS + label) * (TILTS // 2) + chip) * 64 + offset)
    return jnp.where(owner % slab_count == slab_index, place, -1)


def body(tilt_images, corners, visible, defocus, labels, row_owner, row_offset):
    patches, places, *factors = swap(
        corners[:, 0], visible, tilt_images[0], row_owner[..., 0], row_offset, defocus, labels[None])
    stacked, mixed = tables()
    return reduce_table(insert(patches, places, stacked, mixed, factors))


def solution(mesh):
    return jax.shard_map(
        body,
        mesh=mesh,
        in_specs=(
            P("tilt", None, None),
            P(None, "tilt", None),
            P("tilt", None),
            P("tilt", None),
            P("tilt"),
            P("tilt", None, None, None),
            P("tilt", None, None),
        ),
        out_specs=P(None, None, ("tilt", "slab"), None),
        check_vma=False,
    )
```

```python
import math

import jax
import jax.numpy as jnp
import numpy as np
from jax import lax
from jax.experimental import pallas as pl
from jax.experimental.pallas import tpu as pltpu
from jax.sharding import PartitionSpec as P

BOX = 128
HALFMAPS = 4
AMPLITUDE = 0.1
TILTS = 64
PARTICLES = 128
CELLS = TILTS * HALFMAPS * 64
GROUP = 4
PAIRS = PARTICLES // 2
WINDOW = 2 * GROUP
SLOTS = 104
CUTS = 8
CHUNK = 4096


def fourier_tables(width):
    positions = jnp.arange(width, dtype=jnp.int32)
    frequency = positions - width // 2
    phase_index = frequency[:, None] * positions[None, :] % width
    angles = phase_index.astype(jnp.float32) * (2.0 * jnp.pi / width)
    return (jnp.cos(angles).astype(jnp.bfloat16), (-jnp.sin(angles)).astype(jnp.bfloat16))


def transfer_factors(defocus, column):
    frequency = (column - BOX // 2).astype(jnp.float32) / BOX
    angle = jnp.pi * defocus * (frequency * frequency)
    cos_part, sin_part = jnp.cos(angle), jnp.sin(angle)
    main = math.sqrt(1.0 - AMPLITUDE * AMPLITUDE)
    first = -(main * sin_part + AMPLITUDE * cos_part) / BOX
    second = -(main * cos_part - AMPLITUDE * sin_part) / BOX
    return first, second, cos_part, sin_part


def swap_kernel(corner_hbm, seen_hbm, image_hbm, owner_hbm, offset_hbm, defocus_hbm, label_hbm, patches_hbm, places_ref,
                first_ref, second_ref, cos_ref, sin_ref, corner_ref, seen_ref, image_ref, owner_ref, offset_ref,
                defocus_ref, label_ref, left, right, outbox, inbox, patches_ref, send_sem, recv_sem, load_sem, store_sem):
    loads = [
        pltpu.make_async_copy(source, target, load_sem.at[i]) for i, (source, target) in enumerate((
            (owner_hbm, owner_ref), (offset_hbm, offset_ref), (defocus_hbm, defocus_ref), (label_hbm, label_ref),
            (image_hbm, image_ref), (corner_hbm, corner_ref), (seen_hbm, seen_ref)))]
    for load in loads:
        load.start()
    tilt, slab = lax.axis_index("tilt"), lax.axis_index("slab")
    barrier = pltpu.get_barrier_semaphore()

    def peer(d):
        return (tilt + d) % TILTS

    def greet(d, carry):
        pl.semaphore_signal(barrier, inc=1, device_id=(peer(d), slab), device_id_type=pl.DeviceIdType.MESH)
        return carry

    lax.fori_loop(1, TILTS, greet, 0)
    for load in loads[:4]:
        load.wait()
    column = lax.broadcasted_iota(jnp.int32, (TILTS, BOX), 1)
    for j in range(2):
        outbox[:, j, :] = (owner_ref[j] * 64 + offset_ref[j]).astype(jnp.float32)
        outbox[:, 2, j * TILTS:(j + 1) * TILTS] = jnp.broadcast_to(defocus_ref[j:j + 1, :], (TILTS, TILTS))
    outbox[:, 3, :] = jnp.where(column < TILTS, label_ref[0, 0], label_ref[0, 1]).astype(jnp.float32)
    pl.semaphore_wait(barrier, TILTS - 1)

    def message(to, origin):
        return pltpu.make_async_remote_copy(
            src_ref=outbox.at[to], dst_ref=inbox.at[origin], send_sem=send_sem.at[to], recv_sem=recv_sem.at[origin],
            device_id=(to, slab), device_id_type=pl.DeviceIdType.MESH)

    def send(d, carry):
        message(peer(d), tilt).start()
        return carry

    lax.fori_loop(1, TILTS, send, 0)
    inbox[tilt] = outbox[tilt]
    for load in loads[4:]:
        load.wait()
    left[...] = image_ref[:, :BOX].astype(jnp.float32)
    right[...] = image_ref[:, BOX:].astype(jnp.float32)
    lane = lax.broadcasted_iota(jnp.int32, (BOX, BOX), 1)

    def window(p):
        row, col = corner_ref[0, p], corner_ref[1, p]
        a = left[pl.ds(row, BOX), :]
        b = right[pl.ds(row, BOX), :]
        cut = pltpu.roll(jnp.where(lane >= col, a, b), (BOX - col) % BOX, axis=1)
        average = jnp.sum(jnp.sum(cut, axis=0, keepdims=True), axis=1, keepdims=True) * (1.0 / (BOX * BOX))
        centered = cut - average
        variance = jnp.sum(
            jnp.sum(centered * centered, axis=0, keepdims=True), axis=1, keepdims=True) * (1.0 / (BOX * BOX))
        scale = lax.rsqrt(variance + 1e-05) * seen_ref[0, p].astype(jnp.float32)
        return (centered * scale).astype(jnp.bfloat16)

    def leave(i):
        pairs = pl.ds(CUTS // 2 * i, CUTS // 2)
        return pltpu.make_async_copy(patches_ref.at[pairs], patches_hbm.at[pairs], store_sem.at[i])

    def cut_pairs(i, carry):
        windows = [window(CUTS * i + j) for j in range(CUTS)]
        for j, patch in enumerate(windows):
            patches_ref[CUTS // 2 * i + j // 2, :, j % 2 * BOX:(j % 2 + 1) * BOX] = patch
        leave(i).start()
        return carry

    lax.fori_loop(0, PARTICLES // CUTS, cut_pairs, 0)

    def receive(d, carry):
        message(tilt, peer(d)).wait_recv()
        return carry

    lax.fori_loop(1, TILTS, receive, 0)

    rows = jnp.concatenate([inbox[:, 0, :], inbox[:, 1, :]], axis=0).astype(jnp.int32)
    misc = jnp.concatenate([inbox[:, 2, :]] * 2, axis=0)
    line = lax.broadcasted_iota(jnp.int32, (BOX, BOX), 0)
    mine = jnp.where(lane == jnp.where(line < TILTS, tilt, TILTS + tilt), misc, 0.0)
    defocus = jnp.sum(mine, axis=1, keepdims=True)
    labels = jnp.concatenate([inbox[:, 3, :]] * 2, axis=0)
    label = jnp.sum(jnp.where(lane == jnp.where(line < TILTS, 0, TILTS), labels, 0.0), axis=1, keepdims=True)
    places_ref[...] = places_of(rows, label.astype(jnp.int32), slab, lax.axis_size("slab")).T
    first, second, cos_part, sin_part = transfer_factors(defocus, lane)
    first_ref[...] = first.T
    second_ref[...] = second.T
    cos_ref[...] = cos_part
    sin_ref[...] = sin_part

    def sent(d, carry):
        message(peer(d), tilt).wait_send()
        return carry

    lax.fori_loop(1, TILTS, sent, 0)

    def left_all(i, carry):
        leave(i).wait()
        return carry

    lax.fori_loop(0, PARTICLES // CUTS, left_all, 0)


def swap(*operands):
    whole = pl.BlockSpec(memory_space=pltpu.VMEM)
    square = jax.ShapeDtypeStruct((BOX, BOX), jnp.float32)
    return pl.pallas_call(
        swap_kernel,
        out_shape=[jax.ShapeDtypeStruct((PAIRS, BOX, 2 * BOX), jnp.bfloat16),
                   jax.ShapeDtypeStruct((BOX, BOX), jnp.int32)] + [square] * 4,
        in_specs=[pl.BlockSpec(memory_space=pltpu.HBM)] * 7,
        out_specs=[pl.BlockSpec(memory_space=pltpu.HBM)] + [whole] * 5,
        scratch_shapes=[
            pltpu.SMEM((2, BOX), jnp.int32),
            pltpu.SMEM((1, BOX), jnp.int32),
            pltpu.VMEM((256, 256), jnp.bfloat16),
            pltpu.VMEM((2, TILTS, BOX), jnp.int32),
            pltpu.VMEM((2, TILTS, BOX), jnp.int32),
            pltpu.VMEM((2, TILTS), jnp.float32),
            pltpu.SMEM((1, 2), jnp.int32),
            pltpu.VMEM((256, BOX), jnp.float32),
            pltpu.VMEM((256, BOX), jnp.float32),
            pltpu.VMEM((TILTS, 4, BOX), jnp.float32),
            pltpu.VMEM((TILTS, 4, BOX), jnp.float32),
            pltpu.VMEM((PAIRS, BOX, 2 * BOX), jnp.bfloat16),
            pltpu.SemaphoreType.DMA((TILTS,)),
            pltpu.SemaphoreType.DMA((TILTS,)),
            pltpu.SemaphoreType.DMA((7,)),
            pltpu.SemaphoreType.DMA((PARTICLES // CUTS,)),
        ],
        compiler_params=pltpu.CompilerParams(
            collective_id=1, has_side_effects=True, vmem_limit_bytes=62 * 2**20),
        name="swap_rows",
    )(*operands)


def insert_kernel(patches_hbm, places_ref, stacked_ref, mixed_ref, first_ref, second_ref, cos_ref, sin_ref, out_ref,
                  lists, spans, late_rows, spot_s, row_s, late_s, span_s, late_rows_s, sides, slices, staged, kept_slices, table, patches_ref, sems):
    fetch = pltpu.make_async_copy(patches_hbm, patches_ref, sems.at[5])
    fetch.start()
    entry = lax.broadcasted_iota(jnp.int32, (8, BOX), 0)
    lane = lax.broadcasted_iota(jnp.int32, (8, BOX), 1)
    rank = jnp.zeros((8, BOX), jnp.int32)
    spots = [2 * CELLS + 2 * ((8 * s + entry) % (2 * GROUP)) for s in range(SLOTS // 8)]
    spare = jnp.concatenate(spots, axis=0)
    sources = [jnp.zeros((8, BOX), jnp.int32) for _ in range(SLOTS // 8)]
    bounds = []
    for j in range(2):
        first_row, last_row = jnp.full((8, BOX), BOX, jnp.int32), jnp.zeros((8, BOX), jnp.int32)
        for block in range(BOX // 8):
            place = places_ref[8 * block:8 * block + 8, :]
            if j == 1:
                place = pltpu.roll(place, PAIRS, axis=1)
            kept = (place >= 0) & (lane < PAIRS)
            for s in range(SLOTS // 8):
                hit = kept & (rank == s)
                spots[s] = jnp.where(hit, place, spots[s])
                sources[s] = jnp.where(hit, 2 * (BOX * j + 8 * block + entry), sources[s])
            over = kept & (rank >= SLOTS // 8)
            late_rows[j, 8 * block:8 * block + 8, :] = jnp.where(over, place, 2 * CELLS)
            first_row = jnp.minimum(first_row, jnp.where(over, 8 * block + entry, BOX))
            last_row = jnp.maximum(last_row, jnp.where(over, 8 * block + entry + 1, 0))
            rank = rank + jnp.where(kept, 1, 0)
        bounds += [jnp.min(first_row, axis=0, keepdims=True), jnp.max(last_row, axis=0, keepdims=True)]
    spot = jnp.concatenate(spots, axis=0)
    slot = lax.broadcasted_iota(jnp.int32, (SLOTS, BOX), 0)
    late = jnp.zeros((SLOTS, BOX), jnp.bool_)
    for d in range(1, WINDOW):
        late = late | ((pltpu.roll(spot, SLOTS - d, axis=0) == spot) & (slot < SLOTS - d))
    lists[0] = jnp.where(late, spare, spot)
    lists[1] = jnp.concatenate(sources, axis=0)
    lists[2] = jnp.where(late, spot, spare)
    bounds += [jnp.min(jnp.where(late, slot, SLOTS), axis=0, keepdims=True),
               jnp.max(jnp.where(late, slot + 1, 0), axis=0, keepdims=True)]
    for i, bound in enumerate(bounds):
        spans[i:i + 1, :] = bound
    spans[6:7, :] = bounds[1] + bounds[3] + bounds[5]
    copies = [
        pltpu.make_async_copy(lists.at[0], spot_s, sems.at[0]),
        pltpu.make_async_copy(lists.at[1], row_s, sems.at[1]),
        pltpu.make_async_copy(lists.at[2], late_s, sems.at[2]),
        pltpu.make_async_copy(spans, span_s, sems.at[3]),
        pltpu.make_async_copy(late_rows, late_rows_s, sems.at[4]),
    ]
    for copy in copies:
        copy.start()

    def clear(i, carry):
        table[pl.ds(pl.multiple_of(i * 512, 512), 512), :] = jnp.zeros((512, BOX), jnp.float32)
        return carry

    lax.fori_loop(0, 2 * CELLS // 512, clear, 0)
    for copy in copies[:2]:
        copy.wait()

    def line(pair, j):
        return j * PAIRS + pair

    def first_pair(patch, target):
        section = jnp.dot(stacked_ref[...], patch, preferred_element_type=jnp.float32).astype(jnp.bfloat16)
        for j in range(2):
            target[j * BOX:(j + 1) * BOX, :BOX] = section[:BOX, j * BOX:(j + 1) * BOX]
            target[j * BOX:(j + 1) * BOX, BOX:] = section[BOX:, j * BOX:(j + 1) * BOX]

    def second_pair(pair, rows, source, target):
        spectrum = jnp.dot(source[...], mixed_ref[...], preferred_element_type=jnp.float32)
        for j in range(2):
            pick = jnp.full((BOX, BOX), line(pair, j), jnp.int32)
            first = jnp.take_along_axis(first_ref[...], pick, axis=1)
            second = jnp.take_along_axis(second_ref[...], pick, axis=1)
            transfer = first * rows[j][0] + second * rows[j][1]
            real = transfer * spectrum[j * BOX:(j + 1) * BOX, :BOX]
            imag = transfer * spectrum[j * BOX:(j + 1) * BOX, BOX:]
            target[pl.ds(2 * BOX * j, BOX, stride=2), :] = real
            target[pl.ds(2 * BOX * j + 1, BOX, stride=2), :] = imag
            kept_slices[pair, pl.ds(2 * BOX * j, BOX, stride=2), :] = real
            kept_slices[pair, pl.ds(2 * BOX * j + 1, BOX, stride=2), :] = imag

    def insert(p, source):
        waiting = None
        for g in range(SLOTS // GROUP + 1):
            if g < SLOTS // GROUP:
                spots = [spot_s[g * GROUP + i, p] for i in range(GROUP)]
                sums = [table[pl.ds(spots[i], 2), :] + source[pl.ds(row_s[g * GROUP + i, p], 2), :]
                        for i in range(GROUP)]
            if waiting is not None:
                for spot, total in zip(*waiting):
                    table[pl.ds(spot, 2), :] = total
            waiting = (spots, sums)

    def insert_late(p, carry):
        @pl.when(span_s[6, p] > 0)
        def _():
            def from_slot(i, carry):
                table[pl.ds(late_s[i, p], 2), :] += kept_slices[p, pl.ds(row_s[i, p], 2), :]
                return carry

            lax.fori_loop(span_s[4, p], span_s[5, p], from_slot, 0)
            for j in range(2):
                def from_row(i, carry):
                    table[pl.ds(late_rows_s[j, i, p], 2), :] += kept_slices[p, pl.ds(2 * BOX * j + 2 * i, 2), :]
                    return carry

                lax.fori_loop(span_s[2 * j, p], span_s[2 * j + 1, p], from_row, 0)

        return carry

    def step(i, carry):
        for h in range(2):
            tick = 2 * i + h
            patch = patches_ref[jnp.minimum(tick, PAIRS - 1)]
            pair = jnp.clip(tick - 1, 0, PAIRS - 1)
            rows = [(cos_ref[pl.ds(line(pair, j), 1), :], sin_ref[pl.ds(line(pair, j), 1), :]) for j in range(2)]
            idle = (tick < 2) | (tick >= PAIRS + 2)
            insert(jnp.where(idle, PAIRS, tick - 2), slices[h])
            first_pair(patch, sides[h])
            second_pair(pair, rows, sides[1 - h], slices[1 - h])
        return carry

    fetch.wait()
    lax.fori_loop(0, (PAIRS + 2) // 2, step, 0)
    for copy in copies[2:]:
        copy.wait()
    lax.fori_loop(0, PAIRS, insert_late, 0)

    def leave(c):
        return pltpu.make_async_copy(
            staged.at[c % 2], out_ref.at[pl.ds(c * CHUNK, CHUNK)], sems.at[c % 2])

    for c in range(2 * CELLS // CHUNK):
        if c >= 2:
            leave(c - 2).wait()

        def convert(i, carry):
            rows = pl.ds(pl.multiple_of(i * 512, 512), 512)
            staged[c % 2, rows, :] = table[pl.ds(pl.multiple_of(c * CHUNK + i * 512, 512), 512), :].astype(jnp.bfloat16)
            return carry

        lax.fori_loop(0, CHUNK // 512, convert, 0)
        leave(c).start()
    for c in range(2 * CELLS // CHUNK - 2, 2 * CELLS // CHUNK):
        leave(c).wait()


def insert(patches, places, stacked, mixed, factors):
    whole = pl.BlockSpec(memory_space=pltpu.VMEM)
    return pl.pallas_call(
        insert_kernel,
        out_shape=jax.ShapeDtypeStruct((2 * CELLS, BOX), jnp.bfloat16),
        in_specs=[pl.BlockSpec(memory_space=pltpu.HBM)] + [whole] * 7,
        out_specs=pl.BlockSpec(memory_space=pltpu.HBM),
        scratch_shapes=[
            pltpu.VMEM((3, SLOTS, BOX), jnp.int32),
            pltpu.VMEM((8, BOX), jnp.int32),
            pltpu.VMEM((2, BOX, BOX), jnp.int32),
            pltpu.SMEM((SLOTS, BOX), jnp.int32),
            pltpu.SMEM((SLOTS, BOX), jnp.int32),
            pltpu.SMEM((SLOTS, BOX), jnp.int32),
            pltpu.SMEM((8, BOX), jnp.int32),
            pltpu.SMEM((2, BOX, BOX), jnp.int32),
            [pltpu.VMEM((2 * BOX, 2 * BOX), jnp.bfloat16)] * 2,
            [pltpu.VMEM((4 * BOX, BOX), jnp.float32)] * 2,
            pltpu.VMEM((2, CHUNK, BOX), jnp.bfloat16),
            pltpu.VMEM((PAIRS, 4 * BOX, BOX), jnp.float32),
            pltpu.VMEM((2 * CELLS + 4 * GROUP, BOX), jnp.float32),
            pltpu.VMEM((PAIRS, BOX, 2 * BOX), jnp.bfloat16),
            pltpu.SemaphoreType.DMA((6,)),
        ],
        compiler_params=pltpu.CompilerParams(vmem_limit_bytes=62 * 2**20),
        name="insert_slices",
    )(patches, places, stacked, mixed, *factors)


ZS, XS = 8, 4
PART_ROWS = TILTS // 2 * BOX
SPOTS = 2 * CELLS


def reduce_kernel(table_ref, out_ref, own, sib, send_a, recv_a, send_b, recv_b, mid_a, mid_b, send_c, recv_c, send_d,
                  recv_d, last, own_sem, sib_send, sib_recv, a_send, a_recv, b_send, b_recv, c_send, c_recv, d_send,
                  d_recv):
    tilt, slab = lax.axis_index("tilt"), lax.axis_index("slab")
    core, z, x = tilt % 2, tilt // 2 % ZS, tilt // (2 * ZS)

    def at_z(step):
        return (x * (2 * ZS) + (z + step + ZS) % ZS * 2 + core, slab)

    def at_x(step):
        return ((x + step + XS) % XS * (2 * ZS) + z * 2 + core, slab)

    twin = (tilt + 1 - 2 * core, slab)
    barrier = pltpu.get_barrier_semaphore()
    for device in (twin, at_z(1), at_z(-1), at_x(1), at_x(-1)):
        pl.semaphore_signal(barrier, inc=1, device_id=device, device_id_type=pl.DeviceIdType.MESH)

    own_copies = []
    for q in (0, 1, 2, 3):
        copy = pltpu.make_async_copy(
            table_ref.at[pl.ds(pl.multiple_of((core * 4 + q) * PART_ROWS, PART_ROWS), PART_ROWS)],
            own.at[pl.ds(q * PART_ROWS, PART_ROWS)], own_sem.at[q])
        copy.start()
        own_copies.append(copy)
    pl.semaphore_wait(barrier, 5)

    def ring(q, n, size, here, at, sign, plain, send, recv, send_sem, recv_sem):
        half = n // 2

        def slot_of(kind, j):
            return j - 1 if kind == "major" else half + j - 1

        def copy_of(kind, j):
            slot = slot_of(kind, j)
            return pltpu.make_async_remote_copy(
                src_ref=send.at[q % 2, slot], dst_ref=recv.at[q % 2, slot],
                send_sem=send_sem.at[q % 2, slot], recv_sem=recv_sem.at[q % 2, slot],
                device_id=at(sign if kind == "major" else -sign), device_id_type=pl.DeviceIdType.MESH)

        def owner_of(kind, j):
            shift = sign * (half + 1 - j) if kind == "major" else -sign * (half - j)
            return (here + shift + n) % n

        def step(kind, j):
            o = owner_of(kind, j)
            slot = slot_of(kind, j)
            if j > 1:
                copy_of(kind, j - 1).wait_recv()

            def tile(i, carry):
                rows = pl.ds(pl.multiple_of(i * BOX, BOX), BOX)
                total = plain(o, i)
                if j > 1:
                    total = total + recv[q % 2, slot - 1, rows, :].astype(jnp.float32)
                send[q % 2, slot, rows, :] = total.astype(jnp.bfloat16)
                return carry

            lax.fori_loop(0, size // BOX, tile, 0)
            copy_of(kind, j).start()

        def final(store):
            copy_of("major", half).wait_recv()
            copy_of("minor", half - 1).wait_recv()

            def tile(i, carry):
                rows = pl.ds(pl.multiple_of(i * BOX, BOX), BOX)
                store(i, plain(here, i) + recv[q % 2, half - 1, rows, :].astype(jnp.float32)
                      + recv[q % 2, n - 2, rows, :].astype(jnp.float32))
                return carry

            lax.fori_loop(0, size // BOX, tile, 0)

        def drain():
            for kind, steps in (("major", half), ("minor", half - 1)):
                for j in range(1, steps + 1):
                    copy_of(kind, j).wait_send()

        return step, final, drain, owner_of

    A, B = XS * BOX, ZS * BOX
    twin_copies = {}

    def twin_copy(q, kind, j, o, size):
        index = len(twin_copies)
        rows = pl.multiple_of(q * PART_ROWS + o * size, size)
        copy = pltpu.make_async_remote_copy(
            src_ref=table_ref.at[pl.ds(pl.multiple_of((1 - core) * 4 * PART_ROWS + rows, size), size)],
            dst_ref=sib.at[pl.ds(rows, size)], send_sem=sib_send.at[index], recv_sem=sib_recv.at[index],
            device_id=twin, device_id_type=pl.DeviceIdType.MESH)
        copy.start()
        twin_copies[q, kind, j] = copy

    def plain_first(q, size):
        def plain(o, i):
            rows = pl.ds(pl.multiple_of(q * PART_ROWS + o * size + i * BOX, BOX), BOX)
            return own[rows, :].astype(jnp.float32) + sib[rows, :].astype(jnp.float32)
        return plain

    first, second = [], []
    for q in range(4):
        sign = 1 if q % 2 == 0 else -1
        if q < 2:
            first.append(ring(q, ZS, A, z, at_z, sign, plain_first(q, A), send_a, recv_a, a_send, a_recv))
            second.append(ring(q, XS, BOX, x, at_x, sign,
                               lambda o, i, q=q: mid_a[q % 2, pl.ds(pl.multiple_of(o * BOX, BOX), BOX), :],
                               send_c, recv_c, c_send, c_recv))
        else:
            first.append(ring(q, XS, B, x, at_x, sign, plain_first(q, B), send_b, recv_b, b_send, b_recv))
            second.append(ring(q, ZS, BOX, z, at_z, sign,
                               lambda o, i, q=q: mid_b[q % 2, pl.ds(pl.multiple_of(o * BOX, BOX), BOX), :],
                               send_d, recv_d, d_send, d_recv))

    order = []
    for kind in ("major", "minor"):
        order += [(0, kind, 1), (1, kind, 1)]
    order += [(2, "major", 1), (3, "major", 1), (2, "minor", 1), (3, "minor", 1)]
    order += [(0, "major", 2), (1, "major", 2), (0, "minor", 2), (1, "minor", 2)]
    order += [(2, "major", 2), (3, "major", 2)]
    for j in (3,):
        order += [(0, "major", j), (1, "major", j), (0, "minor", j), (1, "minor", j)]
    order += [(0, "major", 4), (1, "major", 4)]
    order += [(2, "own", 0), (3, "own", 0), (0, "own", 0), (1, "own", 0)]

    for q, kind, j in order:
        o = (z if q < 2 else x) if kind == "own" else first[q][3](kind, j)
        twin_copy(q, kind, j, o, A if q < 2 else B)

    waited = set()
    for q, kind, j in order:
        if q not in waited:
            own_copies[q].wait()
            waited.add(q)
        twin_copies[q, kind, j].wait_recv()
        if kind != "own":
            first[q][0](kind, j)
        else:
            def store(i, value, q=q):
                mid = mid_a if q < 2 else mid_b
                mid[q % 2, pl.ds(pl.multiple_of(i * BOX, BOX), BOX), :] = value
            first[q][1](store)
            second[q][0]("major", 1)
            second[q][0]("minor", 1)
    for j in (2, 3, 4):
        for q in (2, 3):
            second[q][0]("major", j)
            if j < 4:
                second[q][0]("minor", j)
        if j == 2:
            for q in (0, 1):
                second[q][0]("major", j)

    def store_last(i, value):
        last[...] = value

    for q in (0, 1, 2, 3):
        second[q][1](store_last)
        out_ref[0, q] = last[pl.ds(0, 64, stride=2), :]
        out_ref[1, q] = last[pl.ds(1, 64, stride=2), :]
    for q in range(4):
        first[q][2]()
        second[q][2]()
    for copy in twin_copies.values():
        copy.wait_send()


def reduce_table(table):
    dma = pltpu.SemaphoreType.DMA
    A, B = XS * BOX, ZS * BOX
    return pl.pallas_call(
        reduce_kernel,
        out_shape=jax.ShapeDtypeStruct((2, HALFMAPS, 64, BOX), jnp.float32),
        in_specs=[pl.BlockSpec(memory_space=pl.ANY)],
        out_specs=pl.BlockSpec(memory_space=pltpu.VMEM),
        scratch_shapes=[
            pltpu.VMEM((SPOTS // 2, BOX), jnp.bfloat16),
            pltpu.VMEM((SPOTS // 2, BOX), jnp.bfloat16),
            pltpu.VMEM((2, ZS - 1, A, BOX), jnp.bfloat16),
            pltpu.VMEM((2, ZS - 1, A, BOX), jnp.bfloat16),
            pltpu.VMEM((2, XS - 1, B, BOX), jnp.bfloat16),
            pltpu.VMEM((2, XS - 1, B, BOX), jnp.bfloat16),
            pltpu.VMEM((2, A, BOX), jnp.float32),
            pltpu.VMEM((2, B, BOX), jnp.float32),
            pltpu.VMEM((2, XS - 1, BOX, BOX), jnp.bfloat16),
            pltpu.VMEM((2, XS - 1, BOX, BOX), jnp.bfloat16),
            pltpu.VMEM((2, ZS - 1, BOX, BOX), jnp.bfloat16),
            pltpu.VMEM((2, ZS - 1, BOX, BOX), jnp.bfloat16),
            pltpu.VMEM((BOX, BOX), jnp.float32),
            dma((4,)), dma((24,)), dma((24,)),
            dma((2, ZS - 1)), dma((2, ZS - 1)), dma((2, XS - 1)), dma((2, XS - 1)),
            dma((2, XS - 1)), dma((2, XS - 1)), dma((2, ZS - 1)), dma((2, ZS - 1)),
        ],
        compiler_params=pltpu.CompilerParams(
            collective_id=0, has_side_effects=True, vmem_limit_bytes=57 * 2**20),
        name="reduce_table",
    )(table)


def tables():
    cos_table, sin_table = fourier_tables(BOX)
    stacked = jnp.concatenate([cos_table, sin_table], 0)
    mixed = jnp.concatenate([
        jnp.concatenate([cos_table.T, sin_table.T], 1),
        jnp.concatenate([-sin_table.T, cos_table.T], 1)], 0)
    return stacked, mixed


def places_of(rows, labels, slab_index, slab_count):
    owner, offset = rows // 64, rows % 64
    tilt = owner // slab_count
    core, z, x = tilt % 2, tilt // 2 % ZS, tilt // (2 * ZS)
    label = labels
    chip = jnp.where(label < 2, z * XS + x, x * ZS + z)
    place = 2 * (((core * HALFMAPS + label) * (TILTS // 2) + chip) * 64 + offset)
    return jnp.where(owner % slab_count == slab_index, place, -1)


def body(tilt_images, corners, visible, defocus, labels, row_owner, row_offset):
    patches, places, *factors = swap(
        corners[:, 0], visible, tilt_images[0], row_owner[..., 0], row_offset, defocus, labels[None])
    stacked, mixed = tables()
    return reduce_table(insert(patches, places, stacked, mixed, factors))


def solution(mesh):
    return jax.shard_map(
        body,
        mesh=mesh,
        in_specs=(
            P("tilt", None, None),
            P(None, "tilt", None),
            P("tilt", None),
            P("tilt", None),
            P("tilt"),
            P("tilt", None, None, None),
            P("tilt", None, None),
        ),
        out_specs=P(None, None, ("tilt", "slab"), None),
        check_vma=False,
    )
```

```python
import math

import jax
import jax.numpy as jnp
import numpy as np
from jax import lax
from jax.experimental import pallas as pl
from jax.experimental.pallas import tpu as pltpu
from jax.sharding import PartitionSpec as P

BOX = 128
HALFMAPS = 4
AMPLITUDE = 0.1
TILTS = 64
PARTICLES = 128
CELLS = TILTS * HALFMAPS * 64
GROUP = 4
PAIRS = PARTICLES // 2
WINDOW = 2 * GROUP
SLOTS = 104
CUTS = 8
CHUNK = 4096


def fourier_tables(width):
    positions = jnp.arange(width, dtype=jnp.int32)
    frequency = positions - width // 2
    phase_index = frequency[:, None] * positions[None, :] % width
    angles = phase_index.astype(jnp.float32) * (2.0 * jnp.pi / width)
    return (jnp.cos(angles).astype(jnp.bfloat16), (-jnp.sin(angles)).astype(jnp.bfloat16))


def transfer_factors(defocus, column):
    frequency = (column - BOX // 2).astype(jnp.float32) / BOX
    angle = jnp.pi * defocus * (frequency * frequency)
    cos_part, sin_part = jnp.cos(angle), jnp.sin(angle)
    main = math.sqrt(1.0 - AMPLITUDE * AMPLITUDE)
    first = -(main * sin_part + AMPLITUDE * cos_part) / BOX
    second = -(main * cos_part - AMPLITUDE * sin_part) / BOX
    return first, second, cos_part, sin_part


def swap_kernel(corner_hbm, seen_hbm, image_hbm, owner_hbm, offset_hbm, defocus_hbm, label_hbm, patches_hbm, places_ref,
                first_ref, second_ref, cos_ref, sin_ref, corner_ref, seen_ref, image_ref, owner_ref, offset_ref,
                defocus_ref, label_ref, left, right, rows_ref, outbox, between, inbox, patches_ref, send_sem, recv_sem, load_sem, store_sem):
    loads = [
        pltpu.make_async_copy(source, target, load_sem.at[i]) for i, (source, target) in enumerate((
            (owner_hbm, owner_ref), (offset_hbm, offset_ref), (defocus_hbm, defocus_ref), (label_hbm, label_ref),
            (image_hbm, image_ref), (corner_hbm, corner_ref), (seen_hbm, seen_ref)))]
    for load in loads:
        load.start()
    tilt, slab = lax.axis_index("tilt"), lax.axis_index("slab")
    barrier = pltpu.get_barrier_semaphore()

    z, side = tilt // 2 % ZS, tilt // (2 * ZS) * 2 + tilt % 2

    def along_z(other):
        return (tilt - 2 * z + 2 * other, slab)

    def along_side(other):
        return (other // 2 * (2 * ZS) + 2 * z + other % 2, slab)

    for d in range(1, 8):
        for partner in (along_z((z + d) % 8), along_side((side + d) % 8)):
            pl.semaphore_signal(barrier, inc=1, device_id=partner, device_id_type=pl.DeviceIdType.MESH)
    for load in loads[:4]:
        load.wait()
    column = lax.broadcasted_iota(jnp.int32, (TILTS, BOX), 1)
    for j in range(2):
        rows_ref[j] = (owner_ref[j] * 64 + offset_ref[j]).astype(jnp.float32)
        outbox[:, :, 2, j * TILTS:(j + 1) * TILTS] = jnp.broadcast_to(
            defocus_ref[j:j + 1, :].reshape(1, 1, TILTS), (8, 8, TILTS))
        for to in range(8):
            outbox[:, to, j, :] = rows_ref[j, pl.ds(to // 2 * 16 + to % 2, 8, stride=2), :]
    column = lax.broadcasted_iota(jnp.int32, (8, 8, BOX), 2)
    outbox[:, :, 3, :] = jnp.where(column < TILTS, label_ref[0, 0], label_ref[0, 1]).astype(jnp.float32)
    pl.semaphore_wait(barrier, 14)

    def first_message(to, origin):
        return pltpu.make_async_remote_copy(
            src_ref=outbox.at[to], dst_ref=between.at[origin], send_sem=send_sem.at[0, to],
            recv_sem=recv_sem.at[0, origin], device_id=along_z(to), device_id_type=pl.DeviceIdType.MESH)

    def second_message(to, origin):
        return pltpu.make_async_remote_copy(
            src_ref=between.at[:, to], dst_ref=inbox.at[origin], send_sem=send_sem.at[1, to],
            recv_sem=recv_sem.at[1, origin], device_id=along_side(to), device_id_type=pl.DeviceIdType.MESH)

    for d in range(1, 8):
        first_message((z + d) % 8, z).start()
    between[z] = outbox[z]
    for load in loads[4:]:
        load.wait()
    left[...] = image_ref[:, :BOX].astype(jnp.float32)
    right[...] = image_ref[:, BOX:].astype(jnp.float32)
    lane = lax.broadcasted_iota(jnp.int32, (BOX, BOX), 1)

    def window(p):
        row, col = corner_ref[0, p], corner_ref[1, p]
        a = left[pl.ds(row, BOX), :]
        b = right[pl.ds(row, BOX), :]
        cut = pltpu.roll(jnp.where(lane >= col, a, b), (BOX - col) % BOX, axis=1)
        average = jnp.sum(jnp.sum(cut, axis=0, keepdims=True), axis=1, keepdims=True) * (1.0 / (BOX * BOX))
        centered = cut - average
        variance = jnp.sum(
            jnp.sum(centered * centered, axis=0, keepdims=True), axis=1, keepdims=True) * (1.0 / (BOX * BOX))
        scale = lax.rsqrt(variance + 1e-05) * seen_ref[0, p].astype(jnp.float32)
        return (centered * scale).astype(jnp.bfloat16)

    def leave(i):
        pairs = pl.ds(CUTS // 2 * i, CUTS // 2)
        return pltpu.make_async_copy(patches_ref.at[pairs], patches_hbm.at[pairs], store_sem.at[i])

    def cut_pairs(i, carry):
        windows = []
        for j in range(CUTS):
            pair = CUTS // 2 * i + j // 2
            source = pair // 16 * 16 + pair % 8 * 2 + pair // 8 % 2
            windows.append(window(2 * source + j % 2))
        for j, patch in enumerate(windows):
            patches_ref[CUTS // 2 * i + j // 2, :, j % 2 * BOX:(j % 2 + 1) * BOX] = patch
        leave(i).start()
        return carry

    lax.fori_loop(0, PARTICLES // CUTS // 2, cut_pairs, 0)
    for d in range(1, 8):
        first_message(z, (z + d) % 8).wait_recv()
    for d in range(1, 8):
        second_message((side + d) % 8, side).start()
    inbox[side] = between[:, side]
    lax.fori_loop(PARTICLES // CUTS // 2, PARTICLES // CUTS, cut_pairs, 0)
    for d in range(1, 8):
        second_message(side, (side + d) % 8).wait_recv()

    def received(r):
        return inbox[:, :, r, :].reshape(TILTS, BOX)

    rows = jnp.concatenate([received(0), received(1)], axis=0).astype(jnp.int32)
    misc = jnp.concatenate([received(2)] * 2, axis=0)
    line = lax.broadcasted_iota(jnp.int32, (BOX, BOX), 0)
    mine = jnp.where(lane == jnp.where(line < TILTS, tilt, TILTS + tilt), misc, 0.0)
    defocus = jnp.sum(mine, axis=1, keepdims=True)
    labels = jnp.concatenate([received(3)] * 2, axis=0)
    label = jnp.sum(jnp.where(lane == jnp.where(line < TILTS, 0, TILTS), labels, 0.0), axis=1, keepdims=True)
    places_ref[...] = places_of(rows, label.astype(jnp.int32), slab, lax.axis_size("slab")).T
    first, second, cos_part, sin_part = transfer_factors(defocus, lane)
    first_ref[...] = first.T
    second_ref[...] = second.T
    cos_ref[...] = cos_part
    sin_ref[...] = sin_part

    for d in range(1, 8):
        first_message((z + d) % 8, z).wait_send()
        second_message((side + d) % 8, side).wait_send()

    def left_all(i, carry):
        leave(i).wait()
        return carry

    lax.fori_loop(0, PARTICLES // CUTS, left_all, 0)


def swap(*operands):
    whole = pl.BlockSpec(memory_space=pltpu.VMEM)
    square = jax.ShapeDtypeStruct((BOX, BOX), jnp.float32)
    return pl.pallas_call(
        swap_kernel,
        out_shape=[jax.ShapeDtypeStruct((PAIRS, BOX, 2 * BOX), jnp.bfloat16),
                   jax.ShapeDtypeStruct((BOX, BOX), jnp.int32)] + [square] * 4,
        in_specs=[pl.BlockSpec(memory_space=pltpu.HBM)] * 7,
        out_specs=[pl.BlockSpec(memory_space=pltpu.HBM)] + [whole] * 5,
        scratch_shapes=[
            pltpu.SMEM((2, BOX), jnp.int32),
            pltpu.SMEM((1, BOX), jnp.int32),
            pltpu.VMEM((256, 256), jnp.bfloat16),
            pltpu.VMEM((2, TILTS, BOX), jnp.int32),
            pltpu.VMEM((2, TILTS, BOX), jnp.int32),
            pltpu.VMEM((2, TILTS), jnp.float32),
            pltpu.SMEM((1, 2), jnp.int32),
            pltpu.VMEM((256, BOX), jnp.float32),
            pltpu.VMEM((256, BOX), jnp.float32),
            pltpu.VMEM((2, TILTS, BOX), jnp.float32),
            pltpu.VMEM((8, 8, 4, BOX), jnp.float32),
            pltpu.VMEM((8, 8, 4, BOX), jnp.float32),
            pltpu.VMEM((8, 8, 4, BOX), jnp.float32),
            pltpu.VMEM((PAIRS, BOX, 2 * BOX), jnp.bfloat16),
            pltpu.SemaphoreType.DMA((2, 8)),
            pltpu.SemaphoreType.DMA((2, 8)),
            pltpu.SemaphoreType.DMA((7,)),
            pltpu.SemaphoreType.DMA((PARTICLES // CUTS,)),
        ],
        compiler_params=pltpu.CompilerParams(
            collective_id=1, has_side_effects=True, vmem_limit_bytes=62 * 2**20),
        name="swap_rows",
    )(*operands)


def insert_kernel(patches_hbm, places_ref, stacked_ref, mixed_ref, first_ref, second_ref, cos_ref, sin_ref, out_ref,
                  lists, spans, late_rows, spot_s, row_s, late_s, span_s, late_rows_s, sides, slices, staged, kept_slices, table, patches_ref, sems):
    fetch = pltpu.make_async_copy(patches_hbm, patches_ref, sems.at[5])
    fetch.start()
    entry = lax.broadcasted_iota(jnp.int32, (8, BOX), 0)
    lane = lax.broadcasted_iota(jnp.int32, (8, BOX), 1)
    rank = jnp.zeros((8, BOX), jnp.int32)
    spots = [2 * CELLS + 2 * ((8 * s + entry) % (2 * GROUP)) for s in range(SLOTS // 8)]
    spare = jnp.concatenate(spots, axis=0)
    sources = [jnp.zeros((8, BOX), jnp.int32) for _ in range(SLOTS // 8)]
    bounds = []
    for j in range(2):
        first_row, last_row = jnp.full((8, BOX), BOX, jnp.int32), jnp.zeros((8, BOX), jnp.int32)
        for block in range(BOX // 8):
            place = places_ref[8 * block:8 * block + 8, :]
            if j == 1:
                place = pltpu.roll(place, PAIRS, axis=1)
            kept = (place >= 0) & (lane < PAIRS)
            for s in range(SLOTS // 8):
                hit = kept & (rank == s)
                spots[s] = jnp.where(hit, place, spots[s])
                sources[s] = jnp.where(hit, 2 * (BOX * j + 8 * block + entry), sources[s])
            over = kept & (rank >= SLOTS // 8)
            late_rows[j, 8 * block:8 * block + 8, :] = jnp.where(over, place, 2 * CELLS)
            first_row = jnp.minimum(first_row, jnp.where(over, 8 * block + entry, BOX))
            last_row = jnp.maximum(last_row, jnp.where(over, 8 * block + entry + 1, 0))
            rank = rank + jnp.where(kept, 1, 0)
        bounds += [jnp.min(first_row, axis=0, keepdims=True), jnp.max(last_row, axis=0, keepdims=True)]
    spot = jnp.concatenate(spots, axis=0)
    slot = lax.broadcasted_iota(jnp.int32, (SLOTS, BOX), 0)
    late = jnp.zeros((SLOTS, BOX), jnp.bool_)
    for d in range(1, WINDOW):
        late = late | ((pltpu.roll(spot, SLOTS - d, axis=0) == spot) & (slot < SLOTS - d))
    lists[0] = jnp.where(late, spare, spot)
    lists[1] = jnp.concatenate(sources, axis=0)
    lists[2] = jnp.where(late, spot, spare)
    bounds += [jnp.min(jnp.where(late, slot, SLOTS), axis=0, keepdims=True),
               jnp.max(jnp.where(late, slot + 1, 0), axis=0, keepdims=True)]
    for i, bound in enumerate(bounds):
        spans[i:i + 1, :] = bound
    spans[6:7, :] = bounds[1] + bounds[3] + bounds[5]
    copies = [
        pltpu.make_async_copy(lists.at[0], spot_s, sems.at[0]),
        pltpu.make_async_copy(lists.at[1], row_s, sems.at[1]),
        pltpu.make_async_copy(lists.at[2], late_s, sems.at[2]),
        pltpu.make_async_copy(spans, span_s, sems.at[3]),
        pltpu.make_async_copy(late_rows, late_rows_s, sems.at[4]),
    ]
    for copy in copies:
        copy.start()

    def clear(i, carry):
        table[pl.ds(pl.multiple_of(i * 512, 512), 512), :] = jnp.zeros((512, BOX), jnp.float32)
        return carry

    lax.fori_loop(0, 2 * CELLS // 512, clear, 0)
    for copy in copies[:2]:
        copy.wait()

    def line(pair, j):
        return j * PAIRS + pair

    def first_pair(patch, target):
        section = jnp.dot(stacked_ref[...], patch, preferred_element_type=jnp.float32).astype(jnp.bfloat16)
        for j in range(2):
            target[j * BOX:(j + 1) * BOX, :BOX] = section[:BOX, j * BOX:(j + 1) * BOX]
            target[j * BOX:(j + 1) * BOX, BOX:] = section[BOX:, j * BOX:(j + 1) * BOX]

    def second_pair(pair, rows, source, target):
        spectrum = jnp.dot(source[...], mixed_ref[...], preferred_element_type=jnp.float32)
        for j in range(2):
            pick = jnp.full((BOX, BOX), line(pair, j), jnp.int32)
            first = jnp.take_along_axis(first_ref[...], pick, axis=1)
            second = jnp.take_along_axis(second_ref[...], pick, axis=1)
            transfer = first * rows[j][0] + second * rows[j][1]
            real = transfer * spectrum[j * BOX:(j + 1) * BOX, :BOX]
            imag = transfer * spectrum[j * BOX:(j + 1) * BOX, BOX:]
            target[pl.ds(2 * BOX * j, BOX, stride=2), :] = real
            target[pl.ds(2 * BOX * j + 1, BOX, stride=2), :] = imag
            kept_slices[pair, pl.ds(2 * BOX * j, BOX, stride=2), :] = real
            kept_slices[pair, pl.ds(2 * BOX * j + 1, BOX, stride=2), :] = imag

    def insert(p, source):
        waiting = None
        for g in range(SLOTS // GROUP + 1):
            if g < SLOTS // GROUP:
                spots = [spot_s[g * GROUP + i, p] for i in range(GROUP)]
                sums = [table[pl.ds(spots[i], 2), :] + source[pl.ds(row_s[g * GROUP + i, p], 2), :]
                        for i in range(GROUP)]
            if waiting is not None:
                for spot, total in zip(*waiting):
                    table[pl.ds(spot, 2), :] = total
            waiting = (spots, sums)

    def insert_late(p, carry):
        @pl.when(span_s[6, p] > 0)
        def _():
            def from_slot(i, carry):
                table[pl.ds(late_s[i, p], 2), :] += kept_slices[p, pl.ds(row_s[i, p], 2), :]
                return carry

            lax.fori_loop(span_s[4, p], span_s[5, p], from_slot, 0)
            for j in range(2):
                def from_row(i, carry):
                    table[pl.ds(late_rows_s[j, i, p], 2), :] += kept_slices[p, pl.ds(2 * BOX * j + 2 * i, 2), :]
                    return carry

                lax.fori_loop(span_s[2 * j, p], span_s[2 * j + 1, p], from_row, 0)

        return carry

    def step(i, carry):
        for h in range(2):
            tick = 2 * i + h
            patch = patches_ref[jnp.minimum(tick, PAIRS - 1)]
            pair = jnp.clip(tick - 1, 0, PAIRS - 1)
            rows = [(cos_ref[pl.ds(line(pair, j), 1), :], sin_ref[pl.ds(line(pair, j), 1), :]) for j in range(2)]
            idle = (tick < 2) | (tick >= PAIRS + 2)
            insert(jnp.where(idle, PAIRS, tick - 2), slices[h])
            first_pair(patch, sides[h])
            second_pair(pair, rows, sides[1 - h], slices[1 - h])
        return carry

    fetch.wait()
    lax.fori_loop(0, (PAIRS + 2) // 2, step, 0)
    for copy in copies[2:]:
        copy.wait()
    lax.fori_loop(0, PAIRS, insert_late, 0)

    def leave(c):
        return pltpu.make_async_copy(
            staged.at[c % 2], out_ref.at[pl.ds(c * CHUNK, CHUNK)], sems.at[c % 2])

    for c in range(2 * CELLS // CHUNK):
        if c >= 2:
            leave(c - 2).wait()

        def convert(i, carry):
            rows = pl.ds(pl.multiple_of(i * 512, 512), 512)
            staged[c % 2, rows, :] = table[pl.ds(pl.multiple_of(c * CHUNK + i * 512, 512), 512), :].astype(jnp.bfloat16)
            return carry

        lax.fori_loop(0, CHUNK // 512, convert, 0)
        leave(c).start()
    for c in range(2 * CELLS // CHUNK - 2, 2 * CELLS // CHUNK):
        leave(c).wait()


def insert(patches, places, stacked, mixed, factors):
    whole = pl.BlockSpec(memory_space=pltpu.VMEM)
    return pl.pallas_call(
        insert_kernel,
        out_shape=jax.ShapeDtypeStruct((2 * CELLS, BOX), jnp.bfloat16),
        in_specs=[pl.BlockSpec(memory_space=pltpu.HBM)] + [whole] * 7,
        out_specs=pl.BlockSpec(memory_space=pltpu.HBM),
        scratch_shapes=[
            pltpu.VMEM((3, SLOTS, BOX), jnp.int32),
            pltpu.VMEM((8, BOX), jnp.int32),
            pltpu.VMEM((2, BOX, BOX), jnp.int32),
            pltpu.SMEM((SLOTS, BOX), jnp.int32),
            pltpu.SMEM((SLOTS, BOX), jnp.int32),
            pltpu.SMEM((SLOTS, BOX), jnp.int32),
            pltpu.SMEM((8, BOX), jnp.int32),
            pltpu.SMEM((2, BOX, BOX), jnp.int32),
            [pltpu.VMEM((2 * BOX, 2 * BOX), jnp.bfloat16)] * 2,
            [pltpu.VMEM((4 * BOX, BOX), jnp.float32)] * 2,
            pltpu.VMEM((2, CHUNK, BOX), jnp.bfloat16),
            pltpu.VMEM((PAIRS, 4 * BOX, BOX), jnp.float32),
            pltpu.VMEM((2 * CELLS + 4 * GROUP, BOX), jnp.float32),
            pltpu.VMEM((PAIRS, BOX, 2 * BOX), jnp.bfloat16),
            pltpu.SemaphoreType.DMA((6,)),
        ],
        compiler_params=pltpu.CompilerParams(vmem_limit_bytes=62 * 2**20),
        name="insert_slices",
    )(patches, places, stacked, mixed, *factors)


ZS, XS = 8, 4
PART_ROWS = TILTS // 2 * BOX
SPOTS = 2 * CELLS


def reduce_kernel(table_ref, out_ref, own, sib, send_a, recv_a, send_b, recv_b, mid_a, mid_b, send_c, recv_c, send_d,
                  recv_d, last, own_sem, sib_send, sib_recv, a_send, a_recv, b_send, b_recv, c_send, c_recv, d_send,
                  d_recv):
    tilt, slab = lax.axis_index("tilt"), lax.axis_index("slab")
    core, z, x = tilt % 2, tilt // 2 % ZS, tilt // (2 * ZS)

    def at_z(step):
        return (x * (2 * ZS) + (z + step + ZS) % ZS * 2 + core, slab)

    def at_x(step):
        return ((x + step + XS) % XS * (2 * ZS) + z * 2 + core, slab)

    twin = (tilt + 1 - 2 * core, slab)
    barrier = pltpu.get_barrier_semaphore()
    for device in (twin, at_z(1), at_z(-1), at_x(1), at_x(-1)):
        pl.semaphore_signal(barrier, inc=1, device_id=device, device_id_type=pl.DeviceIdType.MESH)

    own_copies = []
    for q in (0, 1, 2, 3):
        copy = pltpu.make_async_copy(
            table_ref.at[pl.ds(pl.multiple_of((core * 4 + q) * PART_ROWS, PART_ROWS), PART_ROWS)],
            own.at[pl.ds(q * PART_ROWS, PART_ROWS)], own_sem.at[q])
        copy.start()
        own_copies.append(copy)
    pl.semaphore_wait(barrier, 5)

    def ring(q, n, size, here, at, sign, plain, send, recv, send_sem, recv_sem):
        half = n // 2

        def slot_of(kind, j):
            return j - 1 if kind == "major" else half + j - 1

        def copy_of(kind, j):
            slot = slot_of(kind, j)
            return pltpu.make_async_remote_copy(
                src_ref=send.at[q % 2, slot], dst_ref=recv.at[q % 2, slot],
                send_sem=send_sem.at[q % 2, slot], recv_sem=recv_sem.at[q % 2, slot],
                device_id=at(sign if kind == "major" else -sign), device_id_type=pl.DeviceIdType.MESH)

        def owner_of(kind, j):
            shift = sign * (half + 1 - j) if kind == "major" else -sign * (half - j)
            return (here + shift + n) % n

        def step(kind, j):
            o = owner_of(kind, j)
            slot = slot_of(kind, j)
            if j > 1:
                copy_of(kind, j - 1).wait_recv()

            def tile(i, carry):
                rows = pl.ds(pl.multiple_of(i * BOX, BOX), BOX)
                total = plain(o, i)
                if j > 1:
                    total = total + recv[q % 2, slot - 1, rows, :].astype(jnp.float32)
                send[q % 2, slot, rows, :] = total.astype(jnp.bfloat16)
                return carry

            lax.fori_loop(0, size // BOX, tile, 0)
            copy_of(kind, j).start()

        def final(store):
            copy_of("major", half).wait_recv()
            copy_of("minor", half - 1).wait_recv()

            def tile(i, carry):
                rows = pl.ds(pl.multiple_of(i * BOX, BOX), BOX)
                store(i, plain(here, i) + recv[q % 2, half - 1, rows, :].astype(jnp.float32)
                      + recv[q % 2, n - 2, rows, :].astype(jnp.float32))
                return carry

            lax.fori_loop(0, size // BOX, tile, 0)

        def drain():
            for kind, steps in (("major", half), ("minor", half - 1)):
                for j in range(1, steps + 1):
                    copy_of(kind, j).wait_send()

        return step, final, drain, owner_of

    A, B = XS * BOX, ZS * BOX
    twin_copies = {}

    def twin_copy(q, kind, j, o, size):
        index = len(twin_copies)
        rows = pl.multiple_of(q * PART_ROWS + o * size, size)
        copy = pltpu.make_async_remote_copy(
            src_ref=table_ref.at[pl.ds(pl.multiple_of((1 - core) * 4 * PART_ROWS + rows, size), size)],
            dst_ref=sib.at[pl.ds(rows, size)], send_sem=sib_send.at[index], recv_sem=sib_recv.at[index],
            device_id=twin, device_id_type=pl.DeviceIdType.MESH)
        copy.start()
        twin_copies[q, kind, j] = copy

    def plain_first(q, size):
        def plain(o, i):
            rows = pl.ds(pl.multiple_of(q * PART_ROWS + o * size + i * BOX, BOX), BOX)
            return own[rows, :].astype(jnp.float32) + sib[rows, :].astype(jnp.float32)
        return plain

    first, second = [], []
    for q in range(4):
        sign = 1 if q % 2 == 0 else -1
        if q < 2:
            first.append(ring(q, ZS, A, z, at_z, sign, plain_first(q, A), send_a, recv_a, a_send, a_recv))
            second.append(ring(q, XS, BOX, x, at_x, sign,
                               lambda o, i, q=q: mid_a[q % 2, pl.ds(pl.multiple_of(o * BOX, BOX), BOX), :],
                               send_c, recv_c, c_send, c_recv))
        else:
            first.append(ring(q, XS, B, x, at_x, sign, plain_first(q, B), send_b, recv_b, b_send, b_recv))
            second.append(ring(q, ZS, BOX, z, at_z, sign,
                               lambda o, i, q=q: mid_b[q % 2, pl.ds(pl.multiple_of(o * BOX, BOX), BOX), :],
                               send_d, recv_d, d_send, d_recv))

    order = []
    for kind in ("major", "minor"):
        order += [(0, kind, 1), (1, kind, 1)]
    order += [(2, "major", 1), (3, "major", 1), (2, "minor", 1), (3, "minor", 1)]
    order += [(0, "major", 2), (1, "major", 2), (0, "minor", 2), (1, "minor", 2)]
    order += [(2, "major", 2), (3, "major", 2)]
    for j in (3,):
        order += [(0, "major", j), (1, "major", j), (0, "minor", j), (1, "minor", j)]
    order += [(0, "major", 4), (1, "major", 4)]
    order += [(2, "own", 0), (3, "own", 0), (0, "own", 0), (1, "own", 0)]

    for q, kind, j in order:
        o = (z if q < 2 else x) if kind == "own" else first[q][3](kind, j)
        twin_copy(q, kind, j, o, A if q < 2 else B)

    waited = set()
    for q, kind, j in order:
        if q not in waited:
            own_copies[q].wait()
            waited.add(q)
        twin_copies[q, kind, j].wait_recv()
        if kind != "own":
            first[q][0](kind, j)
        else:
            def store(i, value, q=q):
                mid = mid_a if q < 2 else mid_b
                mid[q % 2, pl.ds(pl.multiple_of(i * BOX, BOX), BOX), :] = value
            first[q][1](store)
            second[q][0]("major", 1)
            second[q][0]("minor", 1)
    for j in (2, 3, 4):
        for q in (2, 3):
            second[q][0]("major", j)
            if j < 4:
                second[q][0]("minor", j)
        if j == 2:
            for q in (0, 1):
                second[q][0]("major", j)

    def store_last(i, value):
        last[...] = value

    for q in (0, 1, 2, 3):
        second[q][1](store_last)
        out_ref[0, q] = last[pl.ds(0, 64, stride=2), :]
        out_ref[1, q] = last[pl.ds(1, 64, stride=2), :]
    for q in range(4):
        first[q][2]()
        second[q][2]()
    for copy in twin_copies.values():
        copy.wait_send()


def reduce_table(table):
    dma = pltpu.SemaphoreType.DMA
    A, B = XS * BOX, ZS * BOX
    return pl.pallas_call(
        reduce_kernel,
        out_shape=jax.ShapeDtypeStruct((2, HALFMAPS, 64, BOX), jnp.float32),
        in_specs=[pl.BlockSpec(memory_space=pl.ANY)],
        out_specs=pl.BlockSpec(memory_space=pltpu.VMEM),
        scratch_shapes=[
            pltpu.VMEM((SPOTS // 2, BOX), jnp.bfloat16),
            pltpu.VMEM((SPOTS // 2, BOX), jnp.bfloat16),
            pltpu.VMEM((2, ZS - 1, A, BOX), jnp.bfloat16),
            pltpu.VMEM((2, ZS - 1, A, BOX), jnp.bfloat16),
            pltpu.VMEM((2, XS - 1, B, BOX), jnp.bfloat16),
            pltpu.VMEM((2, XS - 1, B, BOX), jnp.bfloat16),
            pltpu.VMEM((2, A, BOX), jnp.float32),
            pltpu.VMEM((2, B, BOX), jnp.float32),
            pltpu.VMEM((2, XS - 1, BOX, BOX), jnp.bfloat16),
            pltpu.VMEM((2, XS - 1, BOX, BOX), jnp.bfloat16),
            pltpu.VMEM((2, ZS - 1, BOX, BOX), jnp.bfloat16),
            pltpu.VMEM((2, ZS - 1, BOX, BOX), jnp.bfloat16),
            pltpu.VMEM((BOX, BOX), jnp.float32),
            dma((4,)), dma((24,)), dma((24,)),
            dma((2, ZS - 1)), dma((2, ZS - 1)), dma((2, XS - 1)), dma((2, XS - 1)),
            dma((2, XS - 1)), dma((2, XS - 1)), dma((2, ZS - 1)), dma((2, ZS - 1)),
        ],
        compiler_params=pltpu.CompilerParams(
            collective_id=0, has_side_effects=True, vmem_limit_bytes=57 * 2**20),
        name="reduce_table",
    )(table)


def tables():
    cos_table, sin_table = fourier_tables(BOX)
    stacked = jnp.concatenate([cos_table, sin_table], 0)
    mixed = jnp.concatenate([
        jnp.concatenate([cos_table.T, sin_table.T], 1),
        jnp.concatenate([-sin_table.T, cos_table.T], 1)], 0)
    return stacked, mixed


def places_of(rows, labels, slab_index, slab_count):
    owner, offset = rows // 64, rows % 64
    tilt = owner // slab_count
    core, z, x = tilt % 2, tilt // 2 % ZS, tilt // (2 * ZS)
    label = labels
    chip = jnp.where(label < 2, z * XS + x, x * ZS + z)
    place = 2 * (((core * HALFMAPS + label) * (TILTS // 2) + chip) * 64 + offset)
    return jnp.where(owner % slab_count == slab_index, place, -1)


def body(tilt_images, corners, visible, defocus, labels, row_owner, row_offset):
    patches, places, *factors = swap(
        corners[:, 0], visible, tilt_images[0], row_owner[..., 0], row_offset, defocus, labels[None])
    stacked, mixed = tables()
    return reduce_table(insert(patches, places, stacked, mixed, factors))


def solution(mesh):
    return jax.shard_map(
        body,
        mesh=mesh,
        in_specs=(
            P("tilt", None, None),
            P(None, "tilt", None),
            P("tilt", None),
            P("tilt", None),
            P("tilt"),
            P("tilt", None, None, None),
            P("tilt", None, None),
        ),
        out_specs=P(None, None, ("tilt", "slab"), None),
        check_vma=False,
    )
```

```python
import math

import jax
import jax.numpy as jnp
import numpy as np
from jax import lax
from jax.experimental import pallas as pl
from jax.experimental.pallas import tpu as pltpu
from jax.sharding import PartitionSpec as P

BOX = 128
HALFMAPS = 4
AMPLITUDE = 0.1
TILTS = 64
PARTICLES = 128
CELLS = TILTS * HALFMAPS * 64
GROUP = 4
PAIRS = PARTICLES // 2
WINDOW = 2 * GROUP
SLOTS = 104
CUTS = 8
CHUNK = 4096


def fourier_tables(row, column):
    angles = (((row - BOX // 2) * column) & (BOX - 1)).astype(jnp.float32) * (2.0 * math.pi / BOX)
    return jnp.cos(angles), -jnp.sin(angles)


def transfer_factors(defocus, column):
    frequency = (column - BOX // 2).astype(jnp.float32) / BOX
    angle = jnp.pi * defocus * (frequency * frequency)
    cos_part, sin_part = jnp.cos(angle), jnp.sin(angle)
    main = math.sqrt(1.0 - AMPLITUDE * AMPLITUDE)
    first = -(main * sin_part + AMPLITUDE * cos_part) / BOX
    second = -(main * cos_part - AMPLITUDE * sin_part) / BOX
    return first, second, cos_part, sin_part


def swap_kernel(corner_hbm, seen_hbm, image_hbm, owner_hbm, offset_hbm, defocus_hbm, label_hbm, patches_hbm, places_ref,
                first_ref, second_ref, cos_ref, sin_ref, corner_ref, seen_ref, image_ref, owner_ref, offset_ref,
                defocus_ref, label_ref, left, right, rows_ref, outbox, between, inbox, patches_ref, send_sem, recv_sem, load_sem, store_sem):
    loads = [
        pltpu.make_async_copy(source, target, load_sem.at[i]) for i, (source, target) in enumerate((
            (owner_hbm, owner_ref), (offset_hbm, offset_ref), (defocus_hbm, defocus_ref), (label_hbm, label_ref),
            (image_hbm, image_ref), (corner_hbm, corner_ref), (seen_hbm, seen_ref)))]
    for load in loads:
        load.start()
    tilt, slab = lax.axis_index("tilt"), lax.axis_index("slab")
    barrier = pltpu.get_barrier_semaphore()

    z, side = tilt // 2 % ZS, tilt // (2 * ZS) * 2 + tilt % 2

    def along_z(other):
        return (tilt - 2 * z + 2 * other, slab)

    def along_side(other):
        return (other // 2 * (2 * ZS) + 2 * z + other % 2, slab)

    for d in range(1, 8):
        for partner in (along_z((z + d) % 8), along_side((side + d) % 8)):
            pl.semaphore_signal(barrier, inc=1, device_id=partner, device_id_type=pl.DeviceIdType.MESH)
    for load in loads[:4]:
        load.wait()
    column = lax.broadcasted_iota(jnp.int32, (TILTS, BOX), 1)
    for j in range(2):
        rows_ref[j] = (owner_ref[j] * 64 + offset_ref[j]).astype(jnp.float32)
        outbox[:, :, 2, j * TILTS:(j + 1) * TILTS] = jnp.broadcast_to(
            defocus_ref[j:j + 1, :].reshape(1, 1, TILTS), (8, 8, TILTS))
        for to in range(8):
            outbox[:, to, j, :] = rows_ref[j, pl.ds(to // 2 * 16 + to % 2, 8, stride=2), :]
    column = lax.broadcasted_iota(jnp.int32, (8, 8, BOX), 2)
    outbox[:, :, 3, :] = jnp.where(column < TILTS, label_ref[0, 0], label_ref[0, 1]).astype(jnp.float32)
    pl.semaphore_wait(barrier, 14)

    def first_message(to, origin):
        return pltpu.make_async_remote_copy(
            src_ref=outbox.at[to], dst_ref=between.at[origin], send_sem=send_sem.at[0, to],
            recv_sem=recv_sem.at[0, origin], device_id=along_z(to), device_id_type=pl.DeviceIdType.MESH)

    def second_message(to, origin):
        return pltpu.make_async_remote_copy(
            src_ref=between.at[:, to], dst_ref=inbox.at[origin], send_sem=send_sem.at[1, to],
            recv_sem=recv_sem.at[1, origin], device_id=along_side(to), device_id_type=pl.DeviceIdType.MESH)

    for d in range(1, 8):
        first_message((z + d) % 8, z).start()
    between[z] = outbox[z]
    for load in loads[4:]:
        load.wait()
    left[...] = image_ref[:, :BOX].astype(jnp.float32)
    right[...] = image_ref[:, BOX:].astype(jnp.float32)
    lane = lax.broadcasted_iota(jnp.int32, (BOX, BOX), 1)

    def window(p):
        row, col = corner_ref[0, p], corner_ref[1, p]
        a = left[pl.ds(row, BOX), :]
        b = right[pl.ds(row, BOX), :]
        cut = pltpu.roll(jnp.where(lane >= col, a, b), (BOX - col) % BOX, axis=1)
        average = jnp.sum(jnp.sum(cut, axis=0, keepdims=True), axis=1, keepdims=True) * (1.0 / (BOX * BOX))
        centered = cut - average
        variance = jnp.sum(
            jnp.sum(centered * centered, axis=0, keepdims=True), axis=1, keepdims=True) * (1.0 / (BOX * BOX))
        scale = lax.rsqrt(variance + 1e-05) * seen_ref[0, p].astype(jnp.float32)
        return (centered * scale).astype(jnp.bfloat16)

    def leave(i):
        pairs = pl.ds(CUTS // 2 * i, CUTS // 2)
        return pltpu.make_async_copy(patches_ref.at[pairs], patches_hbm.at[pairs], store_sem.at[i])

    def cut_pairs(i, carry):
        windows = []
        for j in range(CUTS):
            pair = CUTS // 2 * i + j // 2
            source = pair // 16 * 16 + pair % 8 * 2 + pair // 8 % 2
            windows.append(window(2 * source + j % 2))
        for j, patch in enumerate(windows):
            patches_ref[CUTS // 2 * i + j // 2, :, j % 2 * BOX:(j % 2 + 1) * BOX] = patch
        leave(i).start()
        return carry

    lax.fori_loop(0, PARTICLES // CUTS // 2, cut_pairs, 0)
    for d in range(1, 8):
        first_message(z, (z + d) % 8).wait_recv()
    for d in range(1, 8):
        second_message((side + d) % 8, side).start()
    inbox[side] = between[:, side]
    lax.fori_loop(PARTICLES // CUTS // 2, PARTICLES // CUTS, cut_pairs, 0)
    for d in range(1, 8):
        second_message(side, (side + d) % 8).wait_recv()

    def received(r):
        return inbox[:, :, r, :].reshape(TILTS, BOX)

    rows = jnp.concatenate([received(0), received(1)], axis=0).astype(jnp.int32)
    misc = jnp.concatenate([received(2)] * 2, axis=0)
    line = lax.broadcasted_iota(jnp.int32, (BOX, BOX), 0)
    mine = jnp.where(lane == jnp.where(line < TILTS, tilt, TILTS + tilt), misc, 0.0)
    defocus = jnp.sum(mine, axis=1, keepdims=True)
    labels = jnp.concatenate([received(3)] * 2, axis=0)
    label = jnp.sum(jnp.where(lane == jnp.where(line < TILTS, 0, TILTS), labels, 0.0), axis=1, keepdims=True)
    places_ref[...] = places_of(rows, label.astype(jnp.int32), slab, lax.axis_size("slab")).T
    first, second, cos_part, sin_part = transfer_factors(defocus, lane)
    first_ref[...] = first.T
    second_ref[...] = second.T
    cos_ref[...] = cos_part
    sin_ref[...] = sin_part

    for d in range(1, 8):
        first_message((z + d) % 8, z).wait_send()
        second_message((side + d) % 8, side).wait_send()

    def left_all(i, carry):
        leave(i).wait()
        return carry

    lax.fori_loop(0, PARTICLES // CUTS, left_all, 0)


def swap(*operands):
    whole = pl.BlockSpec(memory_space=pltpu.VMEM)
    square = jax.ShapeDtypeStruct((BOX, BOX), jnp.float32)
    return pl.pallas_call(
        swap_kernel,
        out_shape=[jax.ShapeDtypeStruct((PAIRS, BOX, 2 * BOX), jnp.bfloat16),
                   jax.ShapeDtypeStruct((BOX, BOX), jnp.int32)] + [square] * 4,
        in_specs=[pl.BlockSpec(memory_space=pltpu.HBM)] * 7,
        out_specs=[pl.BlockSpec(memory_space=pltpu.HBM)] + [whole] * 5,
        scratch_shapes=[
            pltpu.SMEM((2, BOX), jnp.int32),
            pltpu.SMEM((1, BOX), jnp.int32),
            pltpu.VMEM((256, 256), jnp.bfloat16),
            pltpu.VMEM((2, TILTS, BOX), jnp.int32),
            pltpu.VMEM((2, TILTS, BOX), jnp.int32),
            pltpu.VMEM((2, TILTS), jnp.float32),
            pltpu.SMEM((1, 2), jnp.int32),
            pltpu.VMEM((256, BOX), jnp.float32),
            pltpu.VMEM((256, BOX), jnp.float32),
            pltpu.VMEM((2, TILTS, BOX), jnp.float32),
            pltpu.VMEM((8, 8, 4, BOX), jnp.float32),
            pltpu.VMEM((8, 8, 4, BOX), jnp.float32),
            pltpu.VMEM((8, 8, 4, BOX), jnp.float32),
            pltpu.VMEM((PAIRS, BOX, 2 * BOX), jnp.bfloat16),
            pltpu.SemaphoreType.DMA((2, 8)),
            pltpu.SemaphoreType.DMA((2, 8)),
            pltpu.SemaphoreType.DMA((7,)),
            pltpu.SemaphoreType.DMA((PARTICLES // CUTS,)),
        ],
        compiler_params=pltpu.CompilerParams(
            collective_id=1, has_side_effects=True, vmem_limit_bytes=62 * 2**20),
        name="swap_rows",
    )(*operands)


def insert_kernel(patches_hbm, places_ref, first_ref, second_ref, cos_ref, sin_ref, out_ref,
                  lists, spans, late_rows, spot_s, row_s, late_s, span_s, late_rows_s, sides, slices, staged, kept_slices, table, patches_ref, stacked_ref, mixed_ref, sems):
    fetch = pltpu.make_async_copy(patches_hbm, patches_ref, sems.at[5])
    fetch.start()
    entry = lax.broadcasted_iota(jnp.int32, (8, BOX), 0)
    lane = lax.broadcasted_iota(jnp.int32, (8, BOX), 1)
    rank = jnp.zeros((8, BOX), jnp.int32)
    spots = [2 * CELLS + 2 * ((8 * s + entry) % (2 * GROUP)) for s in range(SLOTS // 8)]
    spare = jnp.concatenate(spots, axis=0)
    sources = [jnp.zeros((8, BOX), jnp.int32) for _ in range(SLOTS // 8)]
    bounds = []
    for j in range(2):
        first_row, last_row = jnp.full((8, BOX), BOX, jnp.int32), jnp.zeros((8, BOX), jnp.int32)
        for block in range(BOX // 8):
            place = places_ref[8 * block:8 * block + 8, :]
            if j == 1:
                place = pltpu.roll(place, PAIRS, axis=1)
            kept = (place >= 0) & (lane < PAIRS)
            for s in range(SLOTS // 8):
                hit = kept & (rank == s)
                spots[s] = jnp.where(hit, place, spots[s])
                sources[s] = jnp.where(hit, 2 * (BOX * j + 8 * block + entry), sources[s])
            over = kept & (rank >= SLOTS // 8)
            late_rows[j, 8 * block:8 * block + 8, :] = jnp.where(over, place, 2 * CELLS)
            first_row = jnp.minimum(first_row, jnp.where(over, 8 * block + entry, BOX))
            last_row = jnp.maximum(last_row, jnp.where(over, 8 * block + entry + 1, 0))
            rank = rank + jnp.where(kept, 1, 0)
        bounds += [jnp.min(first_row, axis=0, keepdims=True), jnp.max(last_row, axis=0, keepdims=True)]
    spot = jnp.concatenate(spots, axis=0)
    slot = lax.broadcasted_iota(jnp.int32, (SLOTS, BOX), 0)
    late = jnp.zeros((SLOTS, BOX), jnp.bool_)
    for d in range(1, WINDOW):
        late = late | ((pltpu.roll(spot, SLOTS - d, axis=0) == spot) & (slot < SLOTS - d))
    lists[0] = jnp.where(late, spare, spot)
    lists[1] = jnp.concatenate(sources, axis=0)
    lists[2] = jnp.where(late, spot, spare)
    bounds += [jnp.min(jnp.where(late, slot, SLOTS), axis=0, keepdims=True),
               jnp.max(jnp.where(late, slot + 1, 0), axis=0, keepdims=True)]
    for i, bound in enumerate(bounds):
        spans[i:i + 1, :] = bound
    spans[6:7, :] = bounds[1] + bounds[3] + bounds[5]
    copies = [
        pltpu.make_async_copy(lists.at[0], spot_s, sems.at[0]),
        pltpu.make_async_copy(lists.at[1], row_s, sems.at[1]),
        pltpu.make_async_copy(lists.at[2], late_s, sems.at[2]),
        pltpu.make_async_copy(spans, span_s, sems.at[3]),
        pltpu.make_async_copy(late_rows, late_rows_s, sems.at[4]),
    ]
    for copy in copies:
        copy.start()

    cos_table, sin_table = fourier_tables(
        lax.broadcasted_iota(jnp.int32, (BOX, BOX), 0), lax.broadcasted_iota(jnp.int32, (BOX, BOX), 1))
    stacked_ref[:BOX, :] = cos_table.astype(jnp.bfloat16)
    stacked_ref[BOX:, :] = sin_table.astype(jnp.bfloat16)
    mixed_ref[:BOX, :BOX] = cos_table.T.astype(jnp.bfloat16)
    mixed_ref[:BOX, BOX:] = sin_table.T.astype(jnp.bfloat16)
    mixed_ref[BOX:, :BOX] = (-sin_table).T.astype(jnp.bfloat16)
    mixed_ref[BOX:, BOX:] = cos_table.T.astype(jnp.bfloat16)

    def clear(i, carry):
        table[pl.ds(pl.multiple_of(i * 512, 512), 512), :] = jnp.zeros((512, BOX), jnp.float32)
        return carry

    lax.fori_loop(0, 2 * CELLS // 512, clear, 0)
    for copy in copies[:2]:
        copy.wait()

    def line(pair, j):
        return j * PAIRS + pair

    def first_pair(patch, target):
        section = jnp.dot(stacked_ref[...], patch, preferred_element_type=jnp.float32).astype(jnp.bfloat16)
        for j in range(2):
            target[j * BOX:(j + 1) * BOX, :BOX] = section[:BOX, j * BOX:(j + 1) * BOX]
            target[j * BOX:(j + 1) * BOX, BOX:] = section[BOX:, j * BOX:(j + 1) * BOX]

    def second_pair(pair, rows, source, target):
        spectrum = jnp.dot(source[...], mixed_ref[...], preferred_element_type=jnp.float32)
        for j in range(2):
            pick = jnp.full((BOX, BOX), line(pair, j), jnp.int32)
            first = jnp.take_along_axis(first_ref[...], pick, axis=1)
            second = jnp.take_along_axis(second_ref[...], pick, axis=1)
            transfer = first * rows[j][0] + second * rows[j][1]
            real = transfer * spectrum[j * BOX:(j + 1) * BOX, :BOX]
            imag = transfer * spectrum[j * BOX:(j + 1) * BOX, BOX:]
            target[pl.ds(2 * BOX * j, BOX, stride=2), :] = real
            target[pl.ds(2 * BOX * j + 1, BOX, stride=2), :] = imag
            kept_slices[pair, pl.ds(2 * BOX * j, BOX, stride=2), :] = real
            kept_slices[pair, pl.ds(2 * BOX * j + 1, BOX, stride=2), :] = imag

    def insert(p, source):
        waiting = None
        for g in range(SLOTS // GROUP + 1):
            if g < SLOTS // GROUP:
                spots = [spot_s[g * GROUP + i, p] for i in range(GROUP)]
                sums = [table[pl.ds(spots[i], 2), :] + source[pl.ds(row_s[g * GROUP + i, p], 2), :]
                        for i in range(GROUP)]
            if waiting is not None:
                for spot, total in zip(*waiting):
                    table[pl.ds(spot, 2), :] = total
            waiting = (spots, sums)

    def insert_late(p, carry):
        @pl.when(span_s[6, p] > 0)
        def _():
            def from_slot(i, carry):
                table[pl.ds(late_s[i, p], 2), :] += kept_slices[p, pl.ds(row_s[i, p], 2), :]
                return carry

            lax.fori_loop(span_s[4, p], span_s[5, p], from_slot, 0)
            for j in range(2):
                def from_row(i, carry):
                    table[pl.ds(late_rows_s[j, i, p], 2), :] += kept_slices[p, pl.ds(2 * BOX * j + 2 * i, 2), :]
                    return carry

                lax.fori_loop(span_s[2 * j, p], span_s[2 * j + 1, p], from_row, 0)

        return carry

    def step(i, carry):
        for h in range(2):
            tick = 2 * i + h
            patch = patches_ref[jnp.minimum(tick, PAIRS - 1)]
            pair = jnp.clip(tick - 1, 0, PAIRS - 1)
            rows = [(cos_ref[pl.ds(line(pair, j), 1), :], sin_ref[pl.ds(line(pair, j), 1), :]) for j in range(2)]
            idle = (tick < 2) | (tick >= PAIRS + 2)
            insert(jnp.where(idle, PAIRS, tick - 2), slices[h])
            first_pair(patch, sides[h])
            second_pair(pair, rows, sides[1 - h], slices[1 - h])
        return carry

    fetch.wait()
    lax.fori_loop(0, (PAIRS + 2) // 2, step, 0)
    for copy in copies[2:]:
        copy.wait()
    lax.fori_loop(0, PAIRS, insert_late, 0)

    def leave(c):
        return pltpu.make_async_copy(
            staged.at[c % 2], out_ref.at[pl.ds(c * CHUNK, CHUNK)], sems.at[c % 2])

    for c in range(2 * CELLS // CHUNK):
        if c >= 2:
            leave(c - 2).wait()

        def convert(i, carry):
            rows = pl.ds(pl.multiple_of(i * 512, 512), 512)
            staged[c % 2, rows, :] = table[pl.ds(pl.multiple_of(c * CHUNK + i * 512, 512), 512), :].astype(jnp.bfloat16)
            return carry

        lax.fori_loop(0, CHUNK // 512, convert, 0)
        leave(c).start()
    for c in range(2 * CELLS // CHUNK - 2, 2 * CELLS // CHUNK):
        leave(c).wait()


def insert(patches, places, factors):
    whole = pl.BlockSpec(memory_space=pltpu.VMEM)
    return pl.pallas_call(
        insert_kernel,
        out_shape=jax.ShapeDtypeStruct((2 * CELLS, BOX), jnp.bfloat16),
        in_specs=[pl.BlockSpec(memory_space=pltpu.HBM)] + [whole] * 5,
        out_specs=pl.BlockSpec(memory_space=pltpu.HBM),
        scratch_shapes=[
            pltpu.VMEM((3, SLOTS, BOX), jnp.int32),
            pltpu.VMEM((8, BOX), jnp.int32),
            pltpu.VMEM((2, BOX, BOX), jnp.int32),
            pltpu.SMEM((SLOTS, BOX), jnp.int32),
            pltpu.SMEM((SLOTS, BOX), jnp.int32),
            pltpu.SMEM((SLOTS, BOX), jnp.int32),
            pltpu.SMEM((8, BOX), jnp.int32),
            pltpu.SMEM((2, BOX, BOX), jnp.int32),
            [pltpu.VMEM((2 * BOX, 2 * BOX), jnp.bfloat16)] * 2,
            [pltpu.VMEM((4 * BOX, BOX), jnp.float32)] * 2,
            pltpu.VMEM((2, CHUNK, BOX), jnp.bfloat16),
            pltpu.VMEM((PAIRS, 4 * BOX, BOX), jnp.float32),
            pltpu.VMEM((2 * CELLS + 4 * GROUP, BOX), jnp.float32),
            pltpu.VMEM((PAIRS, BOX, 2 * BOX), jnp.bfloat16),
            pltpu.VMEM((2 * BOX, BOX), jnp.bfloat16),
            pltpu.VMEM((2 * BOX, 2 * BOX), jnp.bfloat16),
            pltpu.SemaphoreType.DMA((6,)),
        ],
        compiler_params=pltpu.CompilerParams(vmem_limit_bytes=62 * 2**20),
        name="insert_slices",
    )(patches, places, *factors)


ZS, XS = 8, 4
PART_ROWS = TILTS // 2 * BOX
SPOTS = 2 * CELLS


def reduce_kernel(table_ref, out_ref, own, sib, send_a, recv_a, send_b, recv_b, mid_a, mid_b, send_c, recv_c, send_d,
                  recv_d, last, own_sem, sib_send, sib_recv, a_send, a_recv, b_send, b_recv, c_send, c_recv, d_send,
                  d_recv):
    tilt, slab = lax.axis_index("tilt"), lax.axis_index("slab")
    core, z, x = tilt % 2, tilt // 2 % ZS, tilt // (2 * ZS)

    def at_z(step):
        return (x * (2 * ZS) + (z + step + ZS) % ZS * 2 + core, slab)

    def at_x(step):
        return ((x + step + XS) % XS * (2 * ZS) + z * 2 + core, slab)

    twin = (tilt + 1 - 2 * core, slab)
    barrier = pltpu.get_barrier_semaphore()
    for device in (twin, at_z(1), at_z(-1), at_x(1), at_x(-1)):
        pl.semaphore_signal(barrier, inc=1, device_id=device, device_id_type=pl.DeviceIdType.MESH)

    own_copies = []
    for q in (0, 1, 2, 3):
        copy = pltpu.make_async_copy(
            table_ref.at[pl.ds(pl.multiple_of((core * 4 + q) * PART_ROWS, PART_ROWS), PART_ROWS)],
            own.at[pl.ds(q * PART_ROWS, PART_ROWS)], own_sem.at[q])
        copy.start()
        own_copies.append(copy)
    pl.semaphore_wait(barrier, 5)

    def ring(q, n, size, here, at, sign, plain, send, recv, send_sem, recv_sem):
        half = n // 2

        def slot_of(kind, j):
            return j - 1 if kind == "major" else half + j - 1

        def copy_of(kind, j):
            slot = slot_of(kind, j)
            return pltpu.make_async_remote_copy(
                src_ref=send.at[q % 2, slot], dst_ref=recv.at[q % 2, slot],
                send_sem=send_sem.at[q % 2, slot], recv_sem=recv_sem.at[q % 2, slot],
                device_id=at(sign if kind == "major" else -sign), device_id_type=pl.DeviceIdType.MESH)

        def owner_of(kind, j):
            shift = sign * (half + 1 - j) if kind == "major" else -sign * (half - j)
            return (here + shift + n) % n

        def step(kind, j):
            o = owner_of(kind, j)
            slot = slot_of(kind, j)
            if j > 1:
                copy_of(kind, j - 1).wait_recv()

            def tile(i, carry):
                rows = pl.ds(pl.multiple_of(i * BOX, BOX), BOX)
                total = plain(o, i)
                if j > 1:
                    total = total + recv[q % 2, slot - 1, rows, :].astype(jnp.float32)
                send[q % 2, slot, rows, :] = total.astype(jnp.bfloat16)
                return carry

            lax.fori_loop(0, size // BOX, tile, 0)
            copy_of(kind, j).start()

        def final(store):
            copy_of("major", half).wait_recv()
            copy_of("minor", half - 1).wait_recv()

            def tile(i, carry):
                rows = pl.ds(pl.multiple_of(i * BOX, BOX), BOX)
                store(i, plain(here, i) + recv[q % 2, half - 1, rows, :].astype(jnp.float32)
                      + recv[q % 2, n - 2, rows, :].astype(jnp.float32))
                return carry

            lax.fori_loop(0, size // BOX, tile, 0)

        def drain():
            for kind, steps in (("major", half), ("minor", half - 1)):
                for j in range(1, steps + 1):
                    copy_of(kind, j).wait_send()

        return step, final, drain, owner_of

    A, B = XS * BOX, ZS * BOX
    twin_copies = {}

    def twin_copy(q, kind, j, o, size):
        index = len(twin_copies)
        rows = pl.multiple_of(q * PART_ROWS + o * size, size)
        copy = pltpu.make_async_remote_copy(
            src_ref=table_ref.at[pl.ds(pl.multiple_of((1 - core) * 4 * PART_ROWS + rows, size), size)],
            dst_ref=sib.at[pl.ds(rows, size)], send_sem=sib_send.at[index], recv_sem=sib_recv.at[index],
            device_id=twin, device_id_type=pl.DeviceIdType.MESH)
        copy.start()
        twin_copies[q, kind, j] = copy

    def plain_first(q, size):
        def plain(o, i):
            rows = pl.ds(pl.multiple_of(q * PART_ROWS + o * size + i * BOX, BOX), BOX)
            return own[rows, :].astype(jnp.float32) + sib[rows, :].astype(jnp.float32)
        return plain

    first, second = [], []
    for q in range(4):
        sign = 1 if q % 2 == 0 else -1
        if q < 2:
            first.append(ring(q, ZS, A, z, at_z, sign, plain_first(q, A), send_a, recv_a, a_send, a_recv))
            second.append(ring(q, XS, BOX, x, at_x, sign,
                               lambda o, i, q=q: mid_a[q % 2, pl.ds(pl.multiple_of(o * BOX, BOX), BOX), :],
                               send_c, recv_c, c_send, c_recv))
        else:
            first.append(ring(q, XS, B, x, at_x, sign, plain_first(q, B), send_b, recv_b, b_send, b_recv))
            second.append(ring(q, ZS, BOX, z, at_z, sign,
                               lambda o, i, q=q: mid_b[q % 2, pl.ds(pl.multiple_of(o * BOX, BOX), BOX), :],
                               send_d, recv_d, d_send, d_recv))

    order = []
    for kind in ("major", "minor"):
        order += [(0, kind, 1), (1, kind, 1)]
    order += [(2, "major", 1), (3, "major", 1), (2, "minor", 1), (3, "minor", 1)]
    order += [(0, "major", 2), (1, "major", 2), (0, "minor", 2), (1, "minor", 2)]
    order += [(2, "major", 2), (3, "major", 2)]
    for j in (3,):
        order += [(0, "major", j), (1, "major", j), (0, "minor", j), (1, "minor", j)]
    order += [(0, "major", 4), (1, "major", 4)]
    order += [(2, "own", 0), (3, "own", 0), (0, "own", 0), (1, "own", 0)]

    for q, kind, j in order:
        o = (z if q < 2 else x) if kind == "own" else first[q][3](kind, j)
        twin_copy(q, kind, j, o, A if q < 2 else B)

    waited = set()
    for q, kind, j in order:
        if q not in waited:
            own_copies[q].wait()
            waited.add(q)
        twin_copies[q, kind, j].wait_recv()
        if kind != "own":
            first[q][0](kind, j)
        else:
            def store(i, value, q=q):
                mid = mid_a if q < 2 else mid_b
                mid[q % 2, pl.ds(pl.multiple_of(i * BOX, BOX), BOX), :] = value
            first[q][1](store)
            second[q][0]("major", 1)
            second[q][0]("minor", 1)
    for j in (2, 3, 4):
        for q in (2, 3):
            second[q][0]("major", j)
            if j < 4:
                second[q][0]("minor", j)
        if j == 2:
            for q in (0, 1):
                second[q][0]("major", j)

    def store_last(i, value):
        last[...] = value

    for q in (0, 1, 2, 3):
        second[q][1](store_last)
        out_ref[0, q] = last[pl.ds(0, 64, stride=2), :]
        out_ref[1, q] = last[pl.ds(1, 64, stride=2), :]
    for q in range(4):
        first[q][2]()
        second[q][2]()
    for copy in twin_copies.values():
        copy.wait_send()


def reduce_table(table):
    dma = pltpu.SemaphoreType.DMA
    A, B = XS * BOX, ZS * BOX
    return pl.pallas_call(
        reduce_kernel,
        out_shape=jax.ShapeDtypeStruct((2, HALFMAPS, 64, BOX), jnp.float32),
        in_specs=[pl.BlockSpec(memory_space=pl.ANY)],
        out_specs=pl.BlockSpec(memory_space=pltpu.VMEM),
        scratch_shapes=[
            pltpu.VMEM((SPOTS // 2, BOX), jnp.bfloat16),
            pltpu.VMEM((SPOTS // 2, BOX), jnp.bfloat16),
            pltpu.VMEM((2, ZS - 1, A, BOX), jnp.bfloat16),
            pltpu.VMEM((2, ZS - 1, A, BOX), jnp.bfloat16),
            pltpu.VMEM((2, XS - 1, B, BOX), jnp.bfloat16),
            pltpu.VMEM((2, XS - 1, B, BOX), jnp.bfloat16),
            pltpu.VMEM((2, A, BOX), jnp.float32),
            pltpu.VMEM((2, B, BOX), jnp.float32),
            pltpu.VMEM((2, XS - 1, BOX, BOX), jnp.bfloat16),
            pltpu.VMEM((2, XS - 1, BOX, BOX), jnp.bfloat16),
            pltpu.VMEM((2, ZS - 1, BOX, BOX), jnp.bfloat16),
            pltpu.VMEM((2, ZS - 1, BOX, BOX), jnp.bfloat16),
            pltpu.VMEM((BOX, BOX), jnp.float32),
            dma((4,)), dma((24,)), dma((24,)),
            dma((2, ZS - 1)), dma((2, ZS - 1)), dma((2, XS - 1)), dma((2, XS - 1)),
            dma((2, XS - 1)), dma((2, XS - 1)), dma((2, ZS - 1)), dma((2, ZS - 1)),
        ],
        compiler_params=pltpu.CompilerParams(
            collective_id=0, has_side_effects=True, vmem_limit_bytes=57 * 2**20),
        name="reduce_table",
    )(table)


def places_of(rows, labels, slab_index, slab_count):
    owner, offset = rows // 64, rows % 64
    tilt = owner // slab_count
    core, z, x = tilt % 2, tilt // 2 % ZS, tilt // (2 * ZS)
    label = labels
    chip = jnp.where(label < 2, z * XS + x, x * ZS + z)
    place = 2 * (((core * HALFMAPS + label) * (TILTS // 2) + chip) * 64 + offset)
    return jnp.where(owner % slab_count == slab_index, place, -1)


def body(tilt_images, corners, visible, defocus, labels, row_owner, row_offset):
    patches, places, *factors = swap(
        corners[:, 0], visible, tilt_images[0], row_owner[..., 0], row_offset, defocus, labels[None])
    return reduce_table(insert(patches, places, factors))


def solution(mesh):
    return jax.shard_map(
        body,
        mesh=mesh,
        in_specs=(
            P("tilt", None, None),
            P(None, "tilt", None),
            P("tilt", None),
            P("tilt", None),
            P("tilt"),
            P("tilt", None, None, None),
            P("tilt", None, None),
        ),
        out_specs=P(None, None, ("tilt", "slab"), None),
        check_vma=False,
    )
```
